256 devices in a mesh: dp: 32 (over x, y, core), pack: 8 (over z).
Axes of the slice: x: 4, y: 4, z: 8, core: 2. Of those that a mesh axis runs over, the one named last changes fastest.
Arguments:
- queries: bfloat16 [40960, 2560], P(('dp', 'pack')), may hold values from -6 to 6
- keys: bfloat16 [40960, 512], P(('dp', 'pack')), may hold values from -6 to 6
- values: bfloat16 [40960, 512], P(('dp', 'pack')), may hold values from -6 to 6
- out_grad: bfloat16 [40960, 2560], P(('dp', 'pack')), may hold values from -6 to 6
- pair_weight: float32 [32, 2], P('dp'), may hold values from 0.3 to 3
- lengths: int32 [32, 2, 3], P('dp'), may hold values from 1 to 640, as said below
- route_dest: int32 [40960], P(('dp', 'pack')), may hold values from 0 to 31, as said below
- route_slot: int32 [40960], P(('dp', 'pack')), may hold values from 0 to 159
Outputs:
- attended: bfloat16 [40960, 2560], P(('dp', 'pack'))
- query_grad: bfloat16 [40960, 2560], P(('dp', 'pack'))
- key_grad: bfloat16 [40960, 512], P(('dp', 'pack'))
- value_grad: bfloat16 [40960, 512], P(('dp', 'pack'))
The draws below stay inside these ranges and needn't reach their ends.
Inputs may be any that keep to these rules, and one draw needn't show every extreme that they name: `route_dest`: for each pack index the rows of all data ranks fill each data rank's 160 slots exactly once; at most 10 rows of one device go to one data rank, and every device sends exactly 10 to one of them. The lengths of one data rank sum to 1280.
All inputs are finite; a program needn't handle non-finite values.
Results may differ from the reference program's by a relative error of at most 0.018.
Values may be sent and summed in bfloat16 or wider, within the bound.
No kernel may reach another device: no remote copies, remote signals or barrier semaphores. Data moves between devices by JAX's collectives and lax.ppermute only.
A program may use at most 128 MiB of HBM per device.

```python
import math
import jax
import jax.numpy as jnp
from jax import lax

HEAD_DIM = 128
HEADS = 20
KV_HEADS = 4
PAIRS = 2
TOK_DEV = 160
GROUP = 5
CAP = 10
TOKENS = 40960
N_DP = 32
N_PACK = 8


def routing(base_key):

    def one_column(column_key):
        shift_key, perturb_key, send_key, recv_key = jax.random.split(column_key, 4)
        shifts = jax.random.permutation(shift_key, N_DP)
        spare = TOK_DEV - CAP
        steady = spare // (N_DP - 1)
        excess = spare % (N_DP - 1)
        spread = min(steady, CAP - steady - 1)
        ranks_index = jnp.arange(N_DP, dtype=jnp.int32)
        counts = jnp.where(ranks_index == 0, CAP, steady + (ranks_index - 1 < excess).astype(jnp.int32))
        couples = (N_DP - 1) // 2
        if couples > 0:
            moves = jax.random.randint(perturb_key, (couples,), -spread, spread + 1)
            counts = counts.at[1:2 * couples + 1:2].add(moves)
            counts = counts.at[2:2 * couples + 2:2].add(-moves)
        ends = jnp.cumsum(counts)
        slot_index = jnp.arange(TOK_DEV, dtype=jnp.int32)
        which = jnp.sum((slot_index[:, None] >= ends[None, :]).astype(jnp.int32), axis=1)
        sources = jnp.arange(N_DP, dtype=jnp.int32)
        destination = (sources[:, None] + shifts[which][None, :]) % N_DP
        send_order = jax.vmap(lambda sub_key: jax.random.permutation(sub_key, TOK_DEV))(jax.random.split(send_key, N_DP))
        recv_order = jax.vmap(lambda sub_key: jax.random.permutation(sub_key, TOK_DEV))(jax.random.split(recv_key, N_DP))
        slots = recv_order[destination, slot_index[None, :]]
        dest_rows = jnp.zeros((N_DP, TOK_DEV), jnp.int32).at[sources[:, None], send_order].set(destination)
        slot_rows = jnp.zeros((N_DP, TOK_DEV), jnp.int32).at[sources[:, None], send_order].set(slots)
        return (dest_rows, slot_rows)
    column_keys = jax.vmap(lambda index: jax.random.fold_in(base_key, index))(jnp.arange(N_PACK))
    dest_all, slot_all = jax.vmap(one_column)(column_keys)
    return (dest_all.transpose(1, 0, 2).reshape(-1), slot_all.transpose(1, 0, 2).reshape(-1))


def draw_route_dest(key, part):
    dest_all, slot_all = routing(key)
    return dest_all


def draw_route_slot(key, part):
    dest_all, slot_all = routing(key)
    return slot_all


def draw_lengths(key, part):
    key = jax.random.fold_in(key, 5)
    seq_len = TOK_DEV * N_PACK
    middle = seq_len // 2
    others = 3 * PAIRS - 2
    choose_key, ranks_key = jax.random.split(key)
    special_rank = jax.random.randint(choose_key, (), 0, N_DP)

    def one_rank(rank_key, rank_index):
        wide_key, upper_key = jax.random.split(rank_key)
        wide = jax.random.permutation(wide_key, seq_len - 2)[:others].astype(jnp.int32) + 1
        wide = jnp.where(wide >= middle, wide + 1, wide)
        upper = jax.random.permutation(upper_key, seq_len - middle - 1)[:others].astype(jnp.int32) + middle + 1
        chosen = jnp.where(rank_index == special_rank, upper, wide)
        cuts = jnp.sort(jnp.concatenate([chosen, jnp.full((1,), middle, jnp.int32)]))
        bounds = jnp.concatenate([jnp.zeros((1,), jnp.int32), cuts, jnp.full((1,), seq_len, jnp.int32)])
        return (bounds[1:] - bounds[:-1]).reshape(PAIRS, 3)
    return jax.vmap(one_rank)(jax.random.split(ranks_key, N_DP), jnp.arange(N_DP, dtype=jnp.int32))


def draw_queries(key, part):
    key = jax.random.fold_in(key, 11)
    base_key, scale_key = jax.random.split(key)
    base = jax.random.normal(base_key, (TOKENS, HEADS, HEAD_DIM))
    row_scale = jnp.exp(jax.random.uniform(scale_key, (TOKENS, 1, 1), minval=jnp.log(0.5), maxval=jnp.log(1.5)))
    result = base * row_scale
    return jnp.clip(result, -6.0, 6.0).reshape(TOKENS, HEADS * HEAD_DIM).astype(jnp.bfloat16)


def draw_keys(key, part):
    key = jax.random.fold_in(key, 13)
    result = jax.random.normal(key, (TOKENS, KV_HEADS, HEAD_DIM))
    return jnp.clip(result, -6.0, 6.0).reshape(TOKENS, KV_HEADS * HEAD_DIM).astype(jnp.bfloat16)


def block_levels(own_key, extent, cuts, smallest, high):
    factor_of, own = 1.0, jax.random.fold_in(own_key, 6)
    for axis_at, blocks in cuts:
        draws = jnp.exp(jax.random.uniform(jax.random.fold_in(own, axis_at), (blocks,), jnp.float32, smallest / len(cuts), high / len(cuts)))
        factor_of = factor_of * jnp.repeat(draws, extent[axis_at] // blocks).reshape([-1 if axis == axis_at else 1 for axis in range(len(extent))])
    return factor_of


def gaussian(stream_key, dims, scale, limit, cuts=(), kind=jnp.bfloat16):
    loudness = block_levels(stream_key, dims, cuts, -0.22, 0.18) if cuts else 1.0
    entries = jax.random.normal(stream_key, dims, jnp.float32) * scale * loudness
    return jnp.minimum(jnp.maximum(entries, -limit), limit).astype(kind)


def setup_inputs(seed: int = 0) -> dict:
    key_list = jax.random.split(jax.random.key(seed), 9)
    return {
        "queries": draw_queries(jax.random.fold_in(key_list[8], 71), 0),
        "keys": draw_keys(jax.random.fold_in(key_list[8], 71), 0),
        "values": gaussian(key_list[2], (TOKENS, KV_HEADS * HEAD_DIM), 1.0, 6.0, ((0, 256),)),
        "out_grad": gaussian(key_list[3], (TOKENS, HEADS * HEAD_DIM), 1.0, 6.0, ((0, 256),)),
        "pair_weight": jnp.clip(jnp.exp(math.log(3.0) - 2.3025851 * jax.random.uniform(key_list[4], (N_DP, PAIRS), jnp.float32) ** block_levels(key_list[4], (N_DP, PAIRS), ((0, 32),), -0.2, 0.2)), 0.3, 3.0),
        "lengths": draw_lengths(jax.random.fold_in(key_list[8], 71), 0),
        "route_dest": draw_route_dest(jax.random.fold_in(key_list[8], 71), 0),
        "route_slot": draw_route_slot(jax.random.fold_in(key_list[8], 71), 0),
    }


masked_score = -1.0e30


def layout_of(lengths_row, seq_len):
    ends = jnp.cumsum(lengths_row.reshape(-1))
    positions = jnp.arange(seq_len, dtype=jnp.int32)
    segment = jnp.sum((positions[:, None] >= ends[None, :]).astype(jnp.int32), axis=1)
    return segment // 3, segment % 3


def visible(query_pair, query_role, query_place, other_pair, other_role, other_place):
    same_pair = query_pair[:, None] == other_pair[None, :]
    causal = other_place[None, :] <= query_place[:, None]
    crossed = (query_role[:, None] == 2) & (other_role[None, :] == 1)
    return same_pair & causal & jnp.logical_not(crossed)


def reference(queries, keys, values, out_grad, pair_weight, lengths, route_dest, route_slot):
    seq_len = TOK_DEV * N_PACK
    scaling = HEAD_DIM ** -0.5
    arrival = jnp.arange(TOKENS, dtype=jnp.int32)
    target = (route_dest * N_PACK + (arrival // TOK_DEV) % N_PACK) * TOK_DEV + route_slot

    def placed(source):
        return jnp.zeros_like(source).at[target].set(source).reshape(N_DP, seq_len, -1)

    stacked = (placed(queries), placed(keys), placed(values), placed(out_grad), pair_weight, lengths)

    def one_rank(bundle):
        q_rank, k_rank, v_rank, g_rank, weights, rank_lengths = bundle
        pair_ids, roles = layout_of(rank_lengths, seq_len)
        positions = jnp.arange(seq_len, dtype=jnp.int32)
        allowed = visible(pair_ids, roles, positions, pair_ids, roles, positions)
        factor = weights[pair_ids] * jnp.where(roles == 2, -1.0, 1.0)
        cotangent = (factor[:, None] * g_rank.astype(jnp.float32)).astype(jnp.bfloat16)
        q_heads = q_rank.reshape(seq_len, KV_HEADS, GROUP, HEAD_DIM).transpose(1, 0, 2, 3)
        c_heads = cotangent.reshape(seq_len, KV_HEADS, GROUP, HEAD_DIM).transpose(1, 0, 2, 3)
        k_heads = k_rank.reshape(seq_len, KV_HEADS, HEAD_DIM).transpose(1, 0, 2)
        v_heads = v_rank.reshape(seq_len, KV_HEADS, HEAD_DIM).transpose(1, 0, 2)

        def one_group(members):
            q_group, k_group, v_group, c_group = members
            q_float = q_group.astype(jnp.float32)
            k_float = k_group.astype(jnp.float32)
            v_float = v_group.astype(jnp.float32)
            c_float = c_group.astype(jnp.float32)
            score = jnp.einsum("thd,kd->htk", q_float, k_float) * scaling
            score = jnp.where(allowed[None], score, masked_score)
            highest = jnp.max(score, axis=2, keepdims=True)
            raised = jnp.exp(score - highest)
            probs = raised / jnp.sum(raised, axis=2, keepdims=True)
            probs_low = probs.astype(jnp.bfloat16)
            attended = jnp.einsum("htk,kd->thd", probs_low.astype(jnp.float32), v_float).astype(jnp.bfloat16)
            delta = jnp.sum(c_float * attended.astype(jnp.float32), axis=2)
            dprob = jnp.einsum("thd,kd->htk", c_float, v_float)
            dscore = (probs * (dprob - delta.T[:, :, None])).astype(jnp.bfloat16)
            dscore_float = dscore.astype(jnp.float32)
            q_grad = (scaling * jnp.einsum("htk,kd->thd", dscore_float, k_float)).astype(jnp.bfloat16)
            k_grad = (scaling * jnp.einsum("htk,thd->kd", dscore_float, q_float)).astype(jnp.bfloat16)
            v_grad = jnp.einsum("htk,thd->kd", probs_low.astype(jnp.float32), c_float).astype(jnp.bfloat16)
            return attended, q_grad, k_grad, v_grad

        attended, q_grad, k_grad, v_grad = lax.map(one_group, (q_heads, k_heads, v_heads, c_heads))
        attended = attended.transpose(1, 0, 2, 3).reshape(seq_len, -1)
        q_grad = q_grad.transpose(1, 0, 2, 3).reshape(seq_len, -1)
        k_grad = k_grad.transpose(1, 0, 2).reshape(seq_len, -1)
        v_grad = v_grad.transpose(1, 0, 2).reshape(seq_len, -1)
        return attended, q_grad, k_grad, v_grad

    attended, q_grad, k_grad, v_grad = lax.map(one_rank, stacked)

    def returned(result):
        return result.reshape(TOKENS, -1)[target]

    return returned(attended), returned(q_grad), returned(k_grad), returned(v_grad)
```

```python
import functools
import math

import jax
import jax.numpy as jnp
from jax import lax
from jax.experimental import pallas as pl
from jax.experimental.pallas import tpu as pltpu
from jax.sharding import PartitionSpec as P

HEAD_DIM = 128
HEADS = 20
KV_HEADS = 4
GROUP = 5
CAP = 10
MAIN = 8
SPARE = CAP - MAIN

QUERY_WIDTH = HEADS * HEAD_DIM
KV_WIDTH = KV_HEADS * HEAD_DIM
GROUP_WIDTH = GROUP * HEAD_DIM
PAIR_WIDTH = 2 * HEAD_DIM
SCALING = HEAD_DIM ** (-0.5)
EXPONENT = SCALING * math.log2(math.e)
MASKED = -1e30
VMEM_LIMIT = 60 * 1024 * 1024


def dot(left, right, contract=((1,), (0,))):
    return lax.dot_general(left, right, (contract, ((), ())), preferred_element_type=jnp.float32)


def low(x):
    return x.astype(jnp.bfloat16)


def iota(shape, dim):
    return lax.broadcasted_iota(jnp.int32, shape, dim)


def one_hot(condition):
    return jnp.where(condition, 1.0, 0.0).astype(jnp.bfloat16)


def compiler_params(**extra):
    return pltpu.CompilerParams(vmem_limit_bytes=VMEM_LIMIT, **extra)


def send_kernel(dest_ref, slot_ref, keys_ref, values_ref, send_ref, p1_ref, p2_ref, p1t_ref, p2t_ref):
    rows = keys_ref.shape[0]
    slots = send_ref.shape[0]
    dest_row = dest_ref[...]
    place_row = slot_ref[...] + 1
    down = iota((rows, rows), 0)
    across = iota((rows, rows), 1)
    dest_col = jnp.sum(
        jnp.where(down == across, dest_row.astype(jnp.float32), 0.0), axis=1, keepdims=True
    ).astype(jnp.int32)
    same = dest_col == dest_row
    rank_row = jnp.sum(
        jnp.where(same & (down < across), 1.0, 0.0), axis=0, keepdims=True
    ).astype(jnp.int32)
    rank_col = jnp.sum(
        jnp.where(same & (across < down), 1.0, 0.0), axis=1, keepdims=True
    ).astype(jnp.int32)

    def keys_of(dest, rank):
        first = dest * MAIN + rank
        return (
            jnp.where(rank < MAIN, first, -MAIN),
            jnp.where(rank < MAIN, -MAIN, first - MAIN),
        )

    main_row, spare_row = keys_of(dest_row, rank_row)
    main_col, spare_col = keys_of(dest_col, rank_col)
    slot_down = iota((slots, rows), 0)
    slot_across = iota((rows, slots), 1)
    p1 = slot_down == main_row
    p1_low = one_hot(p1)
    p1_ref[...] = p1_low
    p1t_ref[...] = one_hot(slot_across == main_col)
    place = place_row.astype(jnp.float32)
    place_main = jnp.sum(jnp.where(p1, place, 0.0), axis=1, keepdims=True)
    place_spare = jnp.zeros((slots, 1), jnp.float32)
    spare = jnp.zeros((slots, PAIR_WIDTH), jnp.float32)
    for g in range(KV_HEADS):
        p2 = slot_down == spare_row + SPARE * g
        p2_low = one_hot(p2)
        p2_ref[g] = p2_low
        p2t_ref[g] = one_hot(slot_across == spare_col + SPARE * g)
        place_spare += jnp.sum(jnp.where(p2, place, 0.0), axis=1, keepdims=True)
        source = keys_ref if g < 2 else values_ref
        columns = source[:, (g % 2) * PAIR_WIDTH : (g % 2 + 1) * PAIR_WIDTH]
        send_ref[:, g * PAIR_WIDTH : (g + 1) * PAIR_WIDTH] = low(dot(p1_low, columns))
        spare += dot(p2_low, columns)
    send_ref[:, 4 * PAIR_WIDTH : 5 * PAIR_WIDTH] = low(spare)
    lane = iota((slots, HEAD_DIM), 1)
    send_ref[:, 5 * PAIR_WIDTH :] = low(
        jnp.where(lane == 0, place_main, jnp.where(lane == 1, place_spare, 0.0))
    )


def receive_kernel(recv_ref, kv_ref, r1_ref, r2_ref, r1t_ref, r2t_ref):
    rows = kv_ref.shape[0]
    slots = recv_ref.shape[0]
    tile = recv_ref[:, 5 * PAIR_WIDTH :].astype(jnp.float32)
    lane = iota((slots, HEAD_DIM), 1)
    main_col = jnp.sum(jnp.where(lane == 0, tile, 0.0), axis=1, keepdims=True)
    spare_col = jnp.sum(jnp.where(lane == 1, tile, 0.0), axis=1, keepdims=True)
    diagonal = iota((slots, slots), 0) == iota((slots, slots), 1)
    main_row = jnp.sum(jnp.where(diagonal, main_col, 0.0), axis=0, keepdims=True).astype(jnp.int32)
    spare_row = jnp.sum(jnp.where(diagonal, spare_col, 0.0), axis=0, keepdims=True).astype(jnp.int32)
    main_col = main_col.astype(jnp.int32)
    spare_col = spare_col.astype(jnp.int32)
    place_across = iota((slots, rows), 1) + 1
    place_down = iota((rows, slots), 0) + 1
    part_down = (iota((slots, rows), 0) & (MAIN - 1)) >> 1
    part_across = (iota((rows, slots), 1) & (MAIN - 1)) >> 1
    r1_ref[...] = one_hot(place_across == main_col)
    r1t = one_hot(place_down == main_row)
    r1t_ref[...] = r1t
    spare = recv_ref[:, 4 * PAIR_WIDTH : 5 * PAIR_WIDTH]
    for g in range(KV_HEADS):
        r2_ref[g] = one_hot((place_across == spare_col) & (part_down == g))
        r2t = one_hot((place_down == spare_row) & (part_across == g))
        r2t_ref[g] = r2t
        columns = slice(g * PAIR_WIDTH, (g + 1) * PAIR_WIDTH)
        kv_ref[:, columns] = low(dot(r1t, recv_ref[:, columns]) + dot(r2t, spare))


def pack_kernel(source_ref, m1_ref, m2_ref, send_ref):
    width = source_ref.shape[1] // KV_HEADS
    m1 = m1_ref[...]
    spare = jnp.zeros((send_ref.shape[0], width), jnp.float32)
    for g in range(KV_HEADS):
        columns = slice(g * width, (g + 1) * width)
        part = low(source_ref[:, columns])
        send_ref[:, columns] = low(dot(m1, part))
        spare += dot(m2_ref[g], part)
    send_ref[:, KV_HEADS * width :] = low(spare)


def unpack_kernel(recv_ref, m1_ref, m2_ref, out_ref):
    width = out_ref.shape[1] // KV_HEADS
    m1 = m1_ref[...]
    spare = recv_ref[:, KV_HEADS * width :]
    for g in range(KV_HEADS):
        columns = slice(g * width, (g + 1) * width)
        out_ref[:, columns] = low(dot(m1, recv_ref[:, columns]) + dot(m2_ref[g], spare))


def unpack_kv_kernel(recv_ref, m1_ref, m2_ref, key_ref, value_ref):
    m1 = m1_ref[...]
    spare = recv_ref[:, KV_HEADS * PAIR_WIDTH :]
    for g in range(KV_HEADS):
        both = low(
            dot(m1, recv_ref[:, g * PAIR_WIDTH : (g + 1) * PAIR_WIDTH]) + dot(m2_ref[g], spare)
        )
        key_ref[:, g * HEAD_DIM : (g + 1) * HEAD_DIM] = both[:, :HEAD_DIM]
        value_ref[:, g * HEAD_DIM : (g + 1) * HEAD_DIM] = both[:, HEAD_DIM:]


def ends_of(info_ref):
    ends = [info_ref[0]]
    for k in range(1, 6):
        ends.append(ends[-1] + info_ref[k])
    return ends


def forward_kernel(
    info_ref, main_ref, spare_ref, key_ref, value_ref, r1t_ref, r2t_ref, r1_ref, r2_ref,
    query_ref, attended_ref, prob_ref, send_ref, bias, spare_sum,
):
    g = pl.program_id(0)
    rows = query_ref.shape[0]
    keys = key_ref.shape[0]

    @pl.when(g == 0)
    def _():
        e0, e1, e2, e3, e4, _ = ends_of(info_ref)
        place = info_ref[6] * rows + iota((rows, 1), 0)
        first = jnp.where(place >= e2, e2, 0)
        rejected = (place >= e1) & (place < e2)
        hidden_from = jnp.where(place >= e4, e3, jnp.where(rejected, e0, 0))
        hidden_to = jnp.where(place >= e4, e4, jnp.where(rejected, e1, 0))
        other = iota((rows, keys), 1)
        seen = (other >= first) & (other <= place) & ((other < hidden_from) | (other >= hidden_to))
        bias[...] = jnp.where(seen, 0.0, MASKED)
        spare_sum[...] = jnp.zeros_like(spare_sum)

    query = low(dot(r1t_ref[...], main_ref[...]) + dot(r2t_ref[0], spare_ref[...]))
    query_ref[...] = query
    key = key_ref[...]
    value = value_ref[...]
    parts = []
    for h in range(GROUP):
        score = dot(query[:, h * HEAD_DIM : (h + 1) * HEAD_DIM], key, ((1,), (1,))) + bias[...]
        highest = jnp.max(score, axis=1, keepdims=True)
        raised = jnp.exp2((score - highest) * EXPONENT)
        total = jnp.sum(raised, axis=1, keepdims=True)
        prob = low(raised * (1.0 / total))
        prob_ref[h * rows : (h + 1) * rows, :] = prob
        parts.append(low(dot(prob, value)))
    attended = jnp.concatenate(parts, axis=1)
    attended_ref[...] = attended
    send_ref[:, pl.ds(pl.multiple_of(g * GROUP_WIDTH, GROUP_WIDTH), GROUP_WIDTH)] = low(
        dot(r1_ref[...], attended)
    )
    spare_sum[...] += dot(r2_ref[0], attended)

    @pl.when(g == KV_HEADS - 1)
    def _():
        send_ref[:, KV_HEADS * GROUP_WIDTH :] = low(spare_sum[...])


def backward_kernel(
    info_ref, weight_ref, main_ref, spare_ref, key_ref, value_ref, r1t_ref, r2t_ref, r1_ref, r2_ref,
    query_ref, attended_ref, prob_ref, kv_ref, send_ref, spare_sum,
):
    g = pl.program_id(0)
    rows = query_ref.shape[0]

    @pl.when(g == 0)
    def _():
        spare_sum[...] = jnp.zeros_like(spare_sum)

    _, e1, e2, _, e4, _ = ends_of(info_ref)
    place = info_ref[6] * rows + iota((rows, 1), 0)
    weight = jnp.where(place >= e2, weight_ref[1], weight_ref[0])
    rejected = ((place >= e1) & (place < e2)) | (place >= e4)
    factor = jnp.where(rejected, -weight, weight)
    grad = dot(r1t_ref[...], main_ref[...]) + dot(r2t_ref[0], spare_ref[...])
    cotangent = low(factor * grad)
    query = query_ref[...]
    attended = attended_ref[...]
    key = key_ref[...]
    value = value_ref[...]
    parts = []
    key_sum = jnp.zeros((HEAD_DIM, key.shape[0]), jnp.float32)
    value_sum = jnp.zeros((HEAD_DIM, key.shape[0]), jnp.float32)
    for h in range(GROUP):
        columns = slice(h * HEAD_DIM, (h + 1) * HEAD_DIM)
        cot = cotangent[:, columns]
        delta = jnp.sum(
            cot.astype(jnp.float32) * attended[:, columns].astype(jnp.float32), axis=1, keepdims=True
        )
        prob = prob_ref[h * rows : (h + 1) * rows, :]
        dscore = low(prob.astype(jnp.float32) * (dot(cot, value, ((1,), (1,))) - delta))
        parts.append(low(SCALING * dot(dscore, key)))
        key_sum += dot(query[:, columns].T, dscore)
        value_sum += dot(cot.T, prob)
    kv_ref[:, :HEAD_DIM] = low((SCALING * key_sum).T)
    kv_ref[:, HEAD_DIM:] = low(value_sum.T)
    query_grad = jnp.concatenate(parts, axis=1)
    send_ref[:, pl.ds(pl.multiple_of(g * GROUP_WIDTH, GROUP_WIDTH), GROUP_WIDTH)] = low(
        dot(r1_ref[...], query_grad)
    )
    spare_sum[...] += dot(r2_ref[0], query_grad)

    @pl.when(g == KV_HEADS - 1)
    def _():
        send_ref[:, KV_HEADS * GROUP_WIDTH :] = low(spare_sum[...])


def shape(dims, kind=jnp.bfloat16):
    return jax.ShapeDtypeStruct(dims, kind)


def cost(flops, moved, exps=0):
    return pl.CostEstimate(flops=int(flops), bytes_accessed=int(moved), transcendentals=int(exps))


def body(queries, keys, values, out_grad, pair_weight, lengths, route_dest, route_slot):
    rows = queries.shape[0]
    ranks = lax.axis_size("dp")
    packs = lax.axis_size("pack")
    seq = rows * packs
    slots = ranks * MAIN
    wide = (KV_HEADS + 1) * GROUP_WIDTH
    narrow = (KV_HEADS + 1) * PAIR_WIDTH
    fence = lax.optimization_barrier

    def exchange(block):
        moved = lax.all_to_all(
            block.reshape(ranks, MAIN, block.shape[1]), "dp", split_axis=0, concat_axis=0, tiled=True
        )
        return moved.reshape(block.shape)

    maps = (
        shape((slots, rows)),
        shape((KV_HEADS, slots, rows)),
        shape((rows, slots)),
        shape((KV_HEADS, rows, slots)),
    )

    def pack(source, m1, m2):
        width = source.shape[1]
        return pl.pallas_call(
            pack_kernel,
            out_shape=shape((slots, width // KV_HEADS * (KV_HEADS + 1))),
            compiler_params=compiler_params(),
            cost_estimate=cost(400 * slots * rows * width, 5 * slots * width),
        )(source, m1, m2)

    kv_send, p1, p2, p1t, p2t = pl.pallas_call(
        send_kernel,
        out_shape=(shape((slots, narrow + HEAD_DIM)), *maps),
        compiler_params=compiler_params(),
        cost_estimate=cost(4 * slots * rows * 2 * KV_WIDTH, 6 * slots * 2 * KV_WIDTH),
    )(route_dest.reshape(1, rows), route_slot.reshape(1, rows), keys, values)

    kv_recv = exchange(kv_send)
    query_send = pack(queries, p1, p2)
    grad_send = pack(out_grad, p1, p2)
    kv_recv, query_send, grad_send = fence((kv_recv, query_send, grad_send))

    kv_own, r1, r2, r1t, r2t = pl.pallas_call(
        receive_kernel,
        out_shape=(shape((rows, 2 * KV_WIDTH)), *maps),
        compiler_params=compiler_params(),
        cost_estimate=cost(4 * slots * rows * 2 * KV_WIDTH, 6 * slots * 2 * KV_WIDTH),
    )(kv_recv)
    kv_all = lax.all_gather(kv_own, "pack", axis=0, tiled=True)

    query_recv = exchange(query_send)
    query_recv, grad_send = fence((query_recv, grad_send))
    grad_recv = exchange(grad_send)

    info = jnp.concatenate(
        [lengths.reshape(6), lax.axis_index("pack").astype(jnp.int32).reshape(1)]
    )
    smem = pl.BlockSpec(memory_space=pltpu.SMEM)
    main_spec = pl.BlockSpec((slots, GROUP_WIDTH), lambda g: (0, g))
    spare_spec = pl.BlockSpec((slots, GROUP_WIDTH), lambda g: (0, KV_HEADS))
    key_spec = pl.BlockSpec((seq, HEAD_DIM), lambda g: (0, g))
    value_spec = pl.BlockSpec((seq, HEAD_DIM), lambda g: (0, KV_HEADS + g))
    map_specs = [
        pl.BlockSpec((rows, slots), lambda g: (0, 0)),
        pl.BlockSpec((1, rows, slots), lambda g: (g, 0, 0)),
        pl.BlockSpec((slots, rows), lambda g: (0, 0)),
        pl.BlockSpec((1, slots, rows), lambda g: (g, 0, 0)),
    ]
    row_spec = pl.BlockSpec((rows, GROUP_WIDTH), lambda g: (0, g))
    prob_spec = pl.BlockSpec((GROUP * rows, seq), lambda g: (g, 0))
    send_spec = pl.BlockSpec((slots, wide), lambda g: (0, 0))
    work = HEADS * rows * seq * HEAD_DIM
    query_rows, attended, probs, attended_send = pl.pallas_call(
        forward_kernel,
        grid=(KV_HEADS,),
        in_specs=[smem, main_spec, spare_spec, key_spec, value_spec, *map_specs],
        out_specs=(row_spec, row_spec, prob_spec, send_spec),
        out_shape=(
            shape((rows, QUERY_WIDTH)),
            shape((rows, QUERY_WIDTH)),
            shape((HEADS * rows, seq)),
            shape((slots, wide)),
        ),
        scratch_shapes=[
            pltpu.VMEM((rows, seq), jnp.float32),
            pltpu.VMEM((slots, GROUP_WIDTH), jnp.float32),
        ],
        compiler_params=compiler_params(dimension_semantics=("arbitrary",)),
        cost_estimate=cost(4 * work, 2 * HEADS * rows * seq, HEADS * rows * seq),
    )(info, query_recv, query_recv, kv_all, kv_all, r1t, r2t, r1, r2)

    grad_recv, attended_send = fence((grad_recv, attended_send))
    attended_back = exchange(attended_send)

    kv_part, qgrad_send = pl.pallas_call(
        backward_kernel,
        grid=(KV_HEADS,),
        in_specs=[
            smem, smem, main_spec, spare_spec, key_spec, value_spec, *map_specs,
            row_spec, row_spec, prob_spec,
        ],
        out_specs=(pl.BlockSpec((seq, PAIR_WIDTH), lambda g: (0, g)), send_spec),
        out_shape=(shape((seq, 2 * KV_WIDTH)), shape((slots, wide))),
        scratch_shapes=[pltpu.VMEM((slots, GROUP_WIDTH), jnp.float32)],
        compiler_params=compiler_params(dimension_semantics=("arbitrary",)),
        cost_estimate=cost(8 * work, 2 * HEADS * rows * seq),
    )(
        info, pair_weight.reshape(2), grad_recv, grad_recv, kv_all, kv_all, r1t, r2t, r1, r2,
        query_rows, attended, probs,
    )

    kv_grad = lax.psum_scatter(kv_part, "pack", scatter_dimension=0, tiled=True)
    attended_back, qgrad_send = fence((attended_back, qgrad_send))
    qgrad_back = exchange(qgrad_send)

    def unpack(block):
        return pl.pallas_call(
            unpack_kernel,
            out_shape=shape((rows, QUERY_WIDTH)),
            compiler_params=compiler_params(),
            cost_estimate=cost(400 * slots * rows * QUERY_WIDTH, 4 * slots * QUERY_WIDTH),
        )(block, p1t, p2t)

    kv_grad_send = pack(kv_grad, r1, r2)
    qgrad_back, kv_grad_send = fence((qgrad_back, kv_grad_send))
    kv_back = exchange(kv_grad_send)
    key_grad, value_grad = pl.pallas_call(
        unpack_kv_kernel,
        out_shape=(shape((rows, KV_WIDTH)), shape((rows, KV_WIDTH))),
        compiler_params=compiler_params(),
        cost_estimate=cost(4 * slots * rows * 2 * KV_WIDTH, 4 * slots * 2 * KV_WIDTH),
    )(kv_back, p1t, p2t)
    return unpack(attended_back), unpack(qgrad_back), key_grad, value_grad


def solution(mesh):
    rows = P(("dp", "pack"), None)
    flat = P(("dp", "pack"))
    return jax.shard_map(
        body,
        mesh=mesh,
        in_specs=(rows, rows, rows, rows, P("dp", None), P("dp", None, None), flat, flat),
        out_specs=(rows, rows, rows, rows),
        check_vma=False,
    )
```

```python
import functools
import math

import jax
import jax.numpy as jnp
from jax import lax
from jax.experimental import pallas as pl
from jax.experimental.pallas import tpu as pltpu
from jax.sharding import PartitionSpec as P

HEAD_DIM = 128
HEADS = 20
KV_HEADS = 4
GROUP = 5
CAP = 10
MAIN = 8
SPARE = CAP - MAIN

QUERY_WIDTH = HEADS * HEAD_DIM
KV_WIDTH = KV_HEADS * HEAD_DIM
GROUP_WIDTH = GROUP * HEAD_DIM
PAIR_WIDTH = 2 * HEAD_DIM
SCALING = HEAD_DIM ** (-0.5)
EXPONENT = SCALING * math.log2(math.e)
MASKED = -1e30
VMEM_LIMIT = 60 * 1024 * 1024
SMALL_VMEM = 16 * 1024 * 1024
BOTH_WIDTH = 2 * GROUP_WIDTH
LONG = 10**11


def dot(left, right, contract=((1,), (0,))):
    return lax.dot_general(left, right, (contract, ((), ())), preferred_element_type=jnp.float32)


def low(x):
    return x.astype(jnp.bfloat16)


def iota(shape, dim):
    return lax.broadcasted_iota(jnp.int32, shape, dim)


def one_hot(condition):
    return jnp.where(condition, 1.0, 0.0).astype(jnp.bfloat16)


def compiler_params(limit=VMEM_LIMIT, **extra):
    return pltpu.CompilerParams(vmem_limit_bytes=limit, **extra)


def ranks_of(dest_row):
    rows = dest_row.shape[1]
    down = iota((rows, rows), 0)
    across = iota((rows, rows), 1)
    dest_col = jnp.sum(
        jnp.where(down == across, dest_row.astype(jnp.float32), 0.0), axis=1, keepdims=True
    ).astype(jnp.int32)
    return dest_col, dest_col == dest_row, down, across


def places_of(dest, rank):
    rank = rank.astype(jnp.int32)
    first = dest * MAIN + rank
    return jnp.where(rank < MAIN, first, -MAIN), jnp.where(rank < MAIN, -MAIN, first - MAIN)


def send_kernel(dest_ref, slot_ref, keys_ref, values_ref, send_ref, p1_ref, p2_ref):
    rows = keys_ref.shape[0]
    slots = send_ref.shape[0]
    dest_row = dest_ref[...]
    _, same, down, across = ranks_of(dest_row)
    rank_row = jnp.sum(jnp.where(same & (down < across), 1.0, 0.0), axis=0, keepdims=True)
    main_row, spare_row = places_of(dest_row, rank_row)
    slot_down = iota((slots, rows), 0)
    p1 = slot_down == main_row
    p1_low = one_hot(p1)
    p1_ref[...] = p1_low
    place = (slot_ref[...] + 1).astype(jnp.float32)
    place_main = jnp.sum(jnp.where(p1, place, 0.0), axis=1, keepdims=True)
    taken = jnp.zeros((slots, rows), jnp.float32)
    spare = jnp.zeros((slots, PAIR_WIDTH), jnp.float32)
    for g in range(KV_HEADS):
        p2 = slot_down == spare_row + SPARE * g
        p2_low = one_hot(p2)
        p2_ref[g] = p2_low
        taken += jnp.where(p2, place, 0.0)
        source = keys_ref if g < 2 else values_ref
        columns = source[:, (g % 2) * PAIR_WIDTH : (g % 2 + 1) * PAIR_WIDTH]
        send_ref[:, g * PAIR_WIDTH : (g + 1) * PAIR_WIDTH] = low(dot(p1_low, columns))
        spare += dot(p2_low, columns)
    place_spare = jnp.sum(taken, axis=1, keepdims=True)
    send_ref[:, 4 * PAIR_WIDTH : 5 * PAIR_WIDTH] = low(spare)
    lane = iota((slots, HEAD_DIM), 1)
    send_ref[:, 5 * PAIR_WIDTH :] = low(
        jnp.where(lane == 0, place_main, jnp.where(lane == 1, place_spare, 0.0))
    )


def home_maps_kernel(dest_ref, p1t_ref, p2t_ref):
    rows, slots = p1t_ref.shape
    dest_col, same, down, across = ranks_of(dest_ref[...])
    rank_col = jnp.sum(jnp.where(same & (across < down), 1.0, 0.0), axis=1, keepdims=True)
    main_col, spare_col = places_of(dest_col, rank_col)
    slot_across = iota((rows, slots), 1)
    p1t_ref[...] = one_hot(slot_across == main_col)
    for g in range(KV_HEADS):
        p2t_ref[g] = one_hot(slot_across == spare_col + SPARE * g)


def landing_of(recv_ref):
    slots = recv_ref.shape[0]
    tile = recv_ref[:, 5 * PAIR_WIDTH :].astype(jnp.float32)
    lane = iota((slots, HEAD_DIM), 1)
    main_col = jnp.sum(jnp.where(lane == 0, tile, 0.0), axis=1, keepdims=True)
    spare_col = jnp.sum(jnp.where(lane == 1, tile, 0.0), axis=1, keepdims=True)
    return main_col, spare_col


def landing_rows(main_col, spare_col):
    slots = main_col.shape[0]
    diagonal = iota((slots, slots), 0) == iota((slots, slots), 1)
    return (
        jnp.sum(jnp.where(diagonal, main_col, 0.0), axis=0, keepdims=True).astype(jnp.int32),
        jnp.sum(jnp.where(diagonal, spare_col, 0.0), axis=0, keepdims=True).astype(jnp.int32),
    )


def landing_maps(rows, slots, main_row, spare_row):
    place_down = iota((rows, slots), 0) + 1
    part_across = (iota((rows, slots), 1) & (MAIN - 1)) >> 1
    r1t = one_hot(place_down == main_row)
    return r1t, [one_hot((place_down == spare_row) & (part_across == g)) for g in range(KV_HEADS)]


def receive_kernel(recv_ref, kv_ref):
    rows = kv_ref.shape[0]
    slots = recv_ref.shape[0]
    r1t, r2t = landing_maps(rows, slots, *landing_rows(*landing_of(recv_ref)))
    spare = recv_ref[:, 4 * PAIR_WIDTH : 5 * PAIR_WIDTH]
    for g in range(KV_HEADS):
        columns = slice(g * PAIR_WIDTH, (g + 1) * PAIR_WIDTH)
        kv_ref[:, columns] = low(dot(r1t, recv_ref[:, columns]) + dot(r2t[g], spare))


def landing_maps_kernel(recv_ref, r1_ref, r2_ref, r1t_ref, r2t_ref):
    slots, rows = r1_ref.shape
    main_col, spare_col = landing_of(recv_ref)
    r1t, r2t = landing_maps(rows, slots, *landing_rows(main_col, spare_col))
    r1t_ref[...] = r1t
    main_col = main_col.astype(jnp.int32)
    spare_col = spare_col.astype(jnp.int32)
    place_across = iota((slots, rows), 1) + 1
    part_down = (iota((slots, rows), 0) & (MAIN - 1)) >> 1
    r1_ref[...] = one_hot(place_across == main_col)
    for g in range(KV_HEADS):
        r2_ref[g] = one_hot((place_across == spare_col) & (part_down == g))
        r2t_ref[g] = r2t[g]


def pack_queries_kernel(query_ref, grad_ref, m1_ref, m2_ref, send_ref):
    m1 = m1_ref[...]
    spare = jnp.zeros((send_ref.shape[0], BOTH_WIDTH), jnp.float32)
    for g in range(KV_HEADS):
        columns = slice(g * GROUP_WIDTH, (g + 1) * GROUP_WIDTH)
        part = jnp.concatenate([query_ref[:, columns], grad_ref[:, columns]], axis=1)
        send_ref[:, g * BOTH_WIDTH : (g + 1) * BOTH_WIDTH] = low(dot(m1, part))
        spare += dot(m2_ref[g], part)
    send_ref[:, KV_HEADS * BOTH_WIDTH :] = low(spare)


def pack_kernel(source_ref, m1_ref, m2_ref, send_ref):
    width = source_ref.shape[1] // KV_HEADS
    m1 = m1_ref[...]
    spare = jnp.zeros((send_ref.shape[0], width), jnp.float32)
    for g in range(KV_HEADS):
        columns = slice(g * width, (g + 1) * width)
        part = low(source_ref[:, columns])
        send_ref[:, columns] = low(dot(m1, part))
        spare += dot(m2_ref[g], part)
    send_ref[:, KV_HEADS * width :] = low(spare)


def unpack_queries_kernel(recv_ref, m1_ref, m2_ref, attended_ref, grad_ref):
    m1 = m1_ref[...]
    spare = recv_ref[:, KV_HEADS * BOTH_WIDTH :]
    for g in range(KV_HEADS):
        part = recv_ref[:, g * BOTH_WIDTH : (g + 1) * BOTH_WIDTH]
        both = low(dot(m1, part) + dot(m2_ref[g], spare))
        columns = slice(g * GROUP_WIDTH, (g + 1) * GROUP_WIDTH)
        attended_ref[:, columns] = both[:, :GROUP_WIDTH]
        grad_ref[:, columns] = both[:, GROUP_WIDTH:]


def unpack_kv_kernel(recv_ref, m1_ref, m2_ref, key_ref, value_ref):
    m1 = m1_ref[...]
    spare = recv_ref[:, KV_HEADS * PAIR_WIDTH :]
    for g in range(KV_HEADS):
        both = low(
            dot(m1, recv_ref[:, g * PAIR_WIDTH : (g + 1) * PAIR_WIDTH]) + dot(m2_ref[g], spare)
        )
        key_ref[:, g * HEAD_DIM : (g + 1) * HEAD_DIM] = both[:, :HEAD_DIM]
        value_ref[:, g * HEAD_DIM : (g + 1) * HEAD_DIM] = both[:, HEAD_DIM:]


def ends_of(info_ref):
    ends = [info_ref[0]]
    for k in range(1, 6):
        ends.append(ends[-1] + info_ref[k])
    return ends


def stack_heads(x):
    return jnp.concatenate(
        [x[:, h * HEAD_DIM : (h + 1) * HEAD_DIM] for h in range(GROUP)], axis=0
    )


def unstack_heads(x):
    rows = x.shape[0] // GROUP
    return jnp.concatenate([x[h * rows : (h + 1) * rows] for h in range(GROUP)], axis=1)


def attention_kernel(
    info_ref, weight_ref, main_ref, spare_ref, key_ref, value_ref, r1t_ref, r2t_ref, r1_ref, r2_ref,
    kv_ref, send_ref, bias, spare_sum, value_ones, raised, dscore, score, dprob,
):
    step = pl.program_id(0)
    rows, keys = bias.shape
    count = len(score)
    e0, e1, e2, e3, e4, _ = ends_of(info_ref)
    place = info_ref[6] * rows + iota((rows, 1), 0)
    rejected = (place >= e1) & (place < e2)

    @pl.when(step == 0)
    def _():
        first = jnp.where(place >= e2, e2, 0)
        hidden_from = jnp.where(place >= e4, e3, jnp.where(rejected, e0, 0))
        hidden_to = jnp.where(place >= e4, e4, jnp.where(rejected, e1, 0))
        other = iota((rows, keys), 1)
        seen = (other >= first) & (other <= place) & ((other < hidden_from) | (other >= hidden_to))
        bias[...] = jnp.where(seen, 0.0, MASKED)
        spare_sum[...] = jnp.zeros_like(spare_sum)
        for n in range(count):
            value_ones[n][:, HEAD_DIM:] = jnp.ones((keys, HEAD_DIM), jnp.bfloat16)

    weight = jnp.where(place >= e2, weight_ref[1], weight_ref[0])
    factor = jnp.where(rejected | (place >= e4), -weight, weight)
    query, cotangent, key, inverse, attended, delta = ([None] * count for _ in range(6))
    for n in range(count):
        columns = slice(n * HEAD_DIM, (n + 1) * HEAD_DIM)
        both = dot(r1t_ref[...], main_ref[:, n * BOTH_WIDTH : (n + 1) * BOTH_WIDTH]) + dot(
            r2t_ref[n], spare_ref[...]
        )
        query[n] = stack_heads(low(both[:, :GROUP_WIDTH]))
        cotangent[n] = stack_heads(low(factor * both[:, GROUP_WIDTH:]))
        key[n] = key_ref[:, columns]
        value_ones[n][:, :HEAD_DIM] = value_ref[:, columns]
    for n in range(count):
        score[n][...] = dot(query[n], key[n], ((1,), (1,)))
    for n in range(count):
        for h in range(GROUP):
            part = slice(h * rows, (h + 1) * rows)
            seen = score[n][part, :] + bias[...]
            highest = jnp.max(seen, axis=1, keepdims=True)
            raised[n][part, :] = low(jnp.exp2((seen - highest) * EXPONENT))
    for n in range(count):
        dprob[n][...] = dot(cotangent[n], value_ones[n][:, :HEAD_DIM], ((1,), (1,)))
    for n in range(count):
        summed = dot(raised[n][...], value_ones[n][...])
        inverse[n] = 1.0 / summed[:, HEAD_DIM:]
        attended[n] = low(summed[:, :HEAD_DIM] * inverse[n])
        delta[n] = jnp.sum(
            cotangent[n].astype(jnp.float32) * attended[n].astype(jnp.float32),
            axis=1,
            keepdims=True,
        )
    for n in range(count):
        dscore[n][...] = raised[n][...] * low(dprob[n][...] - delta[n])
    for n in range(count):
        scaled = inverse[n] * SCALING
        query_grad = low(dot(dscore[n][...], key[n]) * scaled)
        query_low = low(query[n].astype(jnp.float32) * scaled)
        cotangent_low = low(cotangent[n].astype(jnp.float32) * inverse[n])
        first = n * PAIR_WIDTH
        kv_ref[:, first : first + HEAD_DIM] = low(dot(query_low.T, dscore[n][...])).T
        kv_ref[:, first + HEAD_DIM : first + PAIR_WIDTH] = low(dot(cotangent_low.T, raised[n][...])).T
        both = jnp.concatenate([unstack_heads(attended[n]), unstack_heads(query_grad)], axis=1)
        start = pl.multiple_of((step * count + n) * BOTH_WIDTH, BOTH_WIDTH)
        send_ref[:, pl.ds(start, BOTH_WIDTH)] = low(dot(r1_ref[...], both))
        spare_sum[...] += dot(r2_ref[n], both)

    @pl.when(step == KV_HEADS // count - 1)
    def _():
        send_ref[:, KV_HEADS * BOTH_WIDTH :] = low(spare_sum[...])


def shape(dims, kind=jnp.bfloat16):
    return jax.ShapeDtypeStruct(dims, kind)


def cost(flops, moved, exps=0):
    return pl.CostEstimate(flops=int(flops), bytes_accessed=int(moved), transcendentals=int(exps))


def body(queries, keys, values, out_grad, pair_weight, lengths, route_dest, route_slot):
    rows = queries.shape[0]
    ranks = lax.axis_size("dp")
    packs = lax.axis_size("pack")
    seq = rows * packs
    slots = ranks * MAIN
    wide = (KV_HEADS + 1) * BOTH_WIDTH
    narrow = (KV_HEADS + 1) * PAIR_WIDTH
    fence = lax.optimization_barrier

    def exchange(block):
        moved = lax.all_to_all(
            block.reshape(ranks, MAIN, block.shape[1]), "dp", split_axis=0, concat_axis=0, tiled=True
        )
        return moved.reshape(block.shape)

    down = (shape((slots, rows)), shape((KV_HEADS, slots, rows)))
    across = (shape((rows, slots)), shape((KV_HEADS, rows, slots)))
    dest = route_dest.reshape(1, rows)

    kv_send, p1, p2 = pl.pallas_call(
        send_kernel,
        out_shape=(shape((slots, narrow + HEAD_DIM)), *down),
        compiler_params=compiler_params(),
        cost_estimate=cost(4 * slots * rows * 2 * KV_WIDTH, 6 * slots * 2 * KV_WIDTH),
    )(dest, route_slot.reshape(1, rows), keys, values)

    kv_recv = exchange(kv_send)
    p1t, p2t = pl.pallas_call(
        home_maps_kernel,
        out_shape=across,
        compiler_params=compiler_params(),
        cost_estimate=cost(LONG, 6 * slots * rows),
    )(dest)
    query_send = pl.pallas_call(
        pack_queries_kernel,
        out_shape=shape((slots, wide)),
        compiler_params=compiler_params(),
        cost_estimate=cost(LONG, 10 * slots * QUERY_WIDTH),
    )(queries, out_grad, p1, p2)
    kv_recv, query_send, p1t, p2t = fence((kv_recv, query_send, p1t, p2t))

    kv_own = pl.pallas_call(
        receive_kernel,
        out_shape=shape((rows, 2 * KV_WIDTH)),
        compiler_params=compiler_params(SMALL_VMEM),
        cost_estimate=cost(4 * slots * rows * 2 * KV_WIDTH, 6 * slots * 2 * KV_WIDTH),
    )(kv_recv)
    kv_all = lax.all_gather(kv_own, "pack", axis=0, tiled=True)
    kv_recv, query_send, kv_own = fence((kv_recv, query_send, kv_own))
    r1, r2, r1t, r2t = pl.pallas_call(
        landing_maps_kernel,
        out_shape=(*down, *across),
        compiler_params=compiler_params(),
        cost_estimate=cost(LONG, 6 * slots * rows),
    )(kv_recv)
    query_recv = exchange(query_send)

    info = jnp.concatenate(
        [lengths.reshape(6), lax.axis_index("pack").astype(jnp.int32).reshape(1)]
    )
    smem = pl.BlockSpec(memory_space=pltpu.SMEM)
    at_once = 2
    steps = KV_HEADS // at_once
    work = HEADS * rows * seq * HEAD_DIM

    def several(dims, kind=jnp.bfloat16):
        return [pltpu.VMEM(dims, kind)] * at_once

    kv_part, back_send = pl.pallas_call(
        attention_kernel,
        grid=(steps,),
        in_specs=[
            smem,
            smem,
            pl.BlockSpec((slots, at_once * BOTH_WIDTH), lambda g: (0, g)),
            pl.BlockSpec((slots, BOTH_WIDTH), lambda g: (0, KV_HEADS)),
            pl.BlockSpec((seq, at_once * HEAD_DIM), lambda g: (0, g)),
            pl.BlockSpec((seq, at_once * HEAD_DIM), lambda g: (0, steps + g)),
            pl.BlockSpec((rows, slots), lambda g: (0, 0)),
            pl.BlockSpec((at_once, rows, slots), lambda g: (g, 0, 0)),
            pl.BlockSpec((slots, rows), lambda g: (0, 0)),
            pl.BlockSpec((at_once, slots, rows), lambda g: (g, 0, 0)),
        ],
        out_specs=(
            pl.BlockSpec((seq, at_once * PAIR_WIDTH), lambda g: (0, g)),
            pl.BlockSpec((slots, wide), lambda g: (0, 0)),
        ),
        out_shape=(shape((seq, 2 * KV_WIDTH)), shape((slots, wide))),
        scratch_shapes=[
            pltpu.VMEM((rows, seq), jnp.float32),
            pltpu.VMEM((slots, BOTH_WIDTH), jnp.float32),
            several((seq, PAIR_WIDTH)),
            several((GROUP * rows, seq)),
            several((GROUP * rows, seq)),
            several((GROUP * rows, seq), jnp.float32),
            several((GROUP * rows, seq), jnp.float32),
        ],
        compiler_params=compiler_params(dimension_semantics=("arbitrary",)),
        cost_estimate=cost(12 * work, 2 * HEADS * rows * seq, HEADS * rows * seq),
    )(
        info, pair_weight.reshape(2), query_recv, query_recv, kv_all, kv_all, r1t, r2t, r1, r2,
    )

    back_recv = exchange(back_send)
    kv_grad = lax.psum_scatter(kv_part, "pack", scatter_dimension=0, tiled=True)
    kv_grad_send = pl.pallas_call(
        pack_kernel,
        out_shape=shape((slots, narrow)),
        compiler_params=compiler_params(),
        cost_estimate=cost(4 * slots * rows * 2 * KV_WIDTH, 10 * slots * KV_WIDTH),
    )(kv_grad, r1, r2)
    back_recv, kv_grad_send = fence((back_recv, kv_grad_send))
    kv_back = exchange(kv_grad_send)
    attended, query_grad = pl.pallas_call(
        unpack_queries_kernel,
        out_shape=(shape((rows, QUERY_WIDTH)), shape((rows, QUERY_WIDTH))),
        compiler_params=compiler_params(),
        cost_estimate=cost(LONG, 10 * slots * QUERY_WIDTH),
    )(back_recv, p1t, p2t)
    key_grad, value_grad = pl.pallas_call(
        unpack_kv_kernel,
        out_shape=(shape((rows, KV_WIDTH)), shape((rows, KV_WIDTH))),
        compiler_params=compiler_params(SMALL_VMEM),
        cost_estimate=cost(4 * slots * rows * 2 * KV_WIDTH, 4 * slots * 2 * KV_WIDTH),
    )(kv_back, p1t, p2t)
    return attended, query_grad, key_grad, value_grad


def solution(mesh):
    rows = P(("dp", "pack"), None)
    flat = P(("dp", "pack"))
    return jax.shard_map(
        body,
        mesh=mesh,
        in_specs=(rows, rows, rows, rows, P("dp", None), P("dp", None, None), flat, flat),
        out_specs=(rows, rows, rows, rows),
        check_vma=False,
    )
```

```python
import functools
import math

import jax
import jax.numpy as jnp
from jax import lax
from jax.experimental import pallas as pl
from jax.experimental.pallas import tpu as pltpu
from jax.sharding import PartitionSpec as P

HEAD_DIM = 128
HEADS = 20
KV_HEADS = 4
GROUP = 5
CAP = 10
MAIN = 8
SPARE = CAP - MAIN

QUERY_WIDTH = HEADS * HEAD_DIM
KV_WIDTH = KV_HEADS * HEAD_DIM
GROUP_WIDTH = GROUP * HEAD_DIM
PAIR_WIDTH = 2 * HEAD_DIM
SCALING = HEAD_DIM ** (-0.5)
EXPONENT = SCALING * math.log2(math.e)
MASKED = -1e30
VMEM_LIMIT = 60 * 1024 * 1024
SMALL_VMEM = 16 * 1024 * 1024
BOTH_WIDTH = 2 * GROUP_WIDTH
PIECES = ((0, 1, 2), (3,))
LONG = 10**11


def dot(left, right, contract=((1,), (0,))):
    return lax.dot_general(left, right, (contract, ((), ())), preferred_element_type=jnp.float32)


def low(x):
    return x.astype(jnp.bfloat16)


def iota(shape, dim):
    return lax.broadcasted_iota(jnp.int32, shape, dim)


def one_hot(condition):
    return jnp.where(condition, 1.0, 0.0).astype(jnp.bfloat16)


def compiler_params(limit=VMEM_LIMIT, **extra):
    return pltpu.CompilerParams(vmem_limit_bytes=limit, **extra)


def ranks_of(dest_row):
    rows = dest_row.shape[1]
    down = iota((rows, rows), 0)
    across = iota((rows, rows), 1)
    dest_col = jnp.sum(
        jnp.where(down == across, dest_row.astype(jnp.float32), 0.0), axis=1, keepdims=True
    ).astype(jnp.int32)
    return dest_col, dest_col == dest_row, down, across


def places_of(dest, rank):
    rank = rank.astype(jnp.int32)
    first = dest * MAIN + rank
    return jnp.where(rank < MAIN, first, -MAIN), jnp.where(rank < MAIN, -MAIN, first - MAIN)


def home_places(dest_ref):
    dest_row = dest_ref[...]
    _, same, down, across = ranks_of(dest_row)
    rank_row = jnp.sum(jnp.where(same & (down < across), 1.0, 0.0), axis=0, keepdims=True)
    return places_of(dest_row, rank_row)


def send_kernel(dest_ref, slot_ref, keys_ref, values_ref, send_ref):
    rows = keys_ref.shape[0]
    slots = send_ref.shape[0]
    main_row, spare_row = home_places(dest_ref)
    slot_down = iota((slots, rows), 0)
    p1 = slot_down == main_row
    p1_low = one_hot(p1)
    place = (slot_ref[...] + 1).astype(jnp.float32)
    place_main = jnp.sum(jnp.where(p1, place, 0.0), axis=1, keepdims=True)
    taken = jnp.zeros((slots, rows), jnp.float32)
    spare = jnp.zeros((slots, PAIR_WIDTH), jnp.float32)
    for g in range(KV_HEADS):
        p2 = slot_down == spare_row + SPARE * g
        p2_low = one_hot(p2)
        taken += jnp.where(p2, place, 0.0)
        source = keys_ref if g < 2 else values_ref
        columns = source[:, (g % 2) * PAIR_WIDTH : (g % 2 + 1) * PAIR_WIDTH]
        send_ref[:, g * PAIR_WIDTH : (g + 1) * PAIR_WIDTH] = low(dot(p1_low, columns))
        spare += dot(p2_low, columns)
    place_spare = jnp.sum(taken, axis=1, keepdims=True)
    send_ref[:, 4 * PAIR_WIDTH : 5 * PAIR_WIDTH] = low(spare)
    lane = iota((slots, HEAD_DIM), 1)
    send_ref[:, 5 * PAIR_WIDTH :] = low(
        jnp.where(lane == 0, place_main, jnp.where(lane == 1, place_spare, 0.0))
    )


def home_maps_kernel(dest_ref, p1t_ref, p2t_ref):
    rows, slots = p1t_ref.shape
    dest_col, same, down, across = ranks_of(dest_ref[...])
    rank_col = jnp.sum(jnp.where(same & (across < down), 1.0, 0.0), axis=1, keepdims=True)
    main_col, spare_col = places_of(dest_col, rank_col)
    slot_across = iota((rows, slots), 1)
    p1t_ref[...] = one_hot(slot_across == main_col)
    for g in range(KV_HEADS):
        p2t_ref[g] = one_hot(slot_across == spare_col + SPARE * g)


def landing_of(recv_ref):
    slots = recv_ref.shape[0]
    tile = recv_ref[:, 5 * PAIR_WIDTH :].astype(jnp.float32)
    lane = iota((slots, HEAD_DIM), 1)
    main_col = jnp.sum(jnp.where(lane == 0, tile, 0.0), axis=1, keepdims=True)
    spare_col = jnp.sum(jnp.where(lane == 1, tile, 0.0), axis=1, keepdims=True)
    return main_col, spare_col


def landing_rows(main_col, spare_col):
    slots = main_col.shape[0]
    diagonal = iota((slots, slots), 0) == iota((slots, slots), 1)
    return (
        jnp.sum(jnp.where(diagonal, main_col, 0.0), axis=0, keepdims=True).astype(jnp.int32),
        jnp.sum(jnp.where(diagonal, spare_col, 0.0), axis=0, keepdims=True).astype(jnp.int32),
    )


def landing_maps(rows, slots, main_row, spare_row):
    place_down = iota((rows, slots), 0) + 1
    part_across = (iota((rows, slots), 1) & (MAIN - 1)) >> 1
    r1t = one_hot(place_down == main_row)
    return r1t, [one_hot((place_down == spare_row) & (part_across == g)) for g in range(KV_HEADS)]


def receive_kernel(recv_ref, kv_ref):
    rows = kv_ref.shape[0]
    slots = recv_ref.shape[0]
    r1t, r2t = landing_maps(rows, slots, *landing_rows(*landing_of(recv_ref)))
    spare = recv_ref[:, 4 * PAIR_WIDTH : 5 * PAIR_WIDTH]
    for g in range(KV_HEADS):
        columns = slice(g * PAIR_WIDTH, (g + 1) * PAIR_WIDTH)
        kv_ref[:, columns] = low(dot(r1t, recv_ref[:, columns]) + dot(r2t[g], spare))


def landing_maps_kernel(recv_ref, r1_ref, r2_ref, r1t_ref, r2t_ref):
    slots, rows = r1_ref.shape
    main_col, spare_col = landing_of(recv_ref)
    r1t, r2t = landing_maps(rows, slots, *landing_rows(main_col, spare_col))
    r1t_ref[...] = r1t
    main_col = main_col.astype(jnp.int32)
    spare_col = spare_col.astype(jnp.int32)
    place_across = iota((slots, rows), 1) + 1
    part_down = (iota((slots, rows), 0) & (MAIN - 1)) >> 1
    r1_ref[...] = one_hot(place_across == main_col)
    for g in range(KV_HEADS):
        r2_ref[g] = one_hot((place_across == spare_col) & (part_down == g))
        r2t_ref[g] = r2t[g]


def spread(tiles):
    part = -(-tiles // KV_HEADS)
    return part, [(c * part, min((c + 1) * part, tiles)) for c in range(KV_HEADS)]


def pack_queries_kernel(dest_ref, query_ref, grad_ref, *send_refs):
    rows = query_ref.shape[0]
    slots = send_refs[0].shape[0]
    main_row, spare_row = home_places(dest_ref)
    slot_down = iota((slots, rows), 0)
    m1 = one_hot(slot_down == main_row)
    m2 = [one_hot(slot_down == spare_row + SPARE * c) for c in range(KV_HEADS)]
    for send_ref, heads in zip(send_refs, PIECES):
        parts = []
        for n, g in enumerate(heads):
            columns = slice(g * GROUP_WIDTH, (g + 1) * GROUP_WIDTH)
            parts.append(jnp.concatenate([query_ref[:, columns], grad_ref[:, columns]], axis=1))
            send_ref[:, n * BOTH_WIDTH : (n + 1) * BOTH_WIDTH] = low(dot(m1, parts[-1]))
        whole = jnp.concatenate(parts, axis=1)
        main = whole.shape[1]
        part, ranges = spread(main // HEAD_DIM)
        shortest = ranges[-1][1] - ranges[-1][0]
        total = sum(
            dot(m2[c], whole[:, lo * HEAD_DIM : (lo + shortest) * HEAD_DIM])
            for c, (lo, _) in enumerate(ranges)
        )
        send_ref[:, main : main + shortest * HEAD_DIM] = low(total)
        if shortest < part:
            total = sum(
                dot(m2[c], whole[:, (lo + shortest) * HEAD_DIM : hi * HEAD_DIM])
                for c, (lo, hi) in enumerate(ranges[:-1])
            )
            send_ref[:, main + shortest * HEAD_DIM :] = low(total)


def pack_kernel(source_ref, m1_ref, m2_ref, send_ref):
    width = source_ref.shape[1] // KV_HEADS
    m1 = m1_ref[...]
    spare = jnp.zeros((send_ref.shape[0], width), jnp.float32)
    for g in range(KV_HEADS):
        columns = slice(g * width, (g + 1) * width)
        part = low(source_ref[:, columns])
        send_ref[:, columns] = low(dot(m1, part))
        spare += dot(m2_ref[g], part)
    send_ref[:, KV_HEADS * width :] = low(spare)


def unpack_queries_kernel(recv_ref, m1_ref, m2_ref, attended_ref, grad_ref):
    m1 = m1_ref[...]
    spare = recv_ref[:, KV_HEADS * BOTH_WIDTH :]
    for g in range(KV_HEADS):
        part = recv_ref[:, g * BOTH_WIDTH : (g + 1) * BOTH_WIDTH]
        both = low(dot(m1, part) + dot(m2_ref[g], spare))
        columns = slice(g * GROUP_WIDTH, (g + 1) * GROUP_WIDTH)
        attended_ref[:, columns] = both[:, :GROUP_WIDTH]
        grad_ref[:, columns] = both[:, GROUP_WIDTH:]


def unpack_kv_kernel(recv_ref, m1_ref, m2_ref, key_ref, value_ref):
    m1 = m1_ref[...]
    spare = recv_ref[:, KV_HEADS * PAIR_WIDTH :]
    for g in range(KV_HEADS):
        both = low(
            dot(m1, recv_ref[:, g * PAIR_WIDTH : (g + 1) * PAIR_WIDTH]) + dot(m2_ref[g], spare)
        )
        key_ref[:, g * HEAD_DIM : (g + 1) * HEAD_DIM] = both[:, :HEAD_DIM]
        value_ref[:, g * HEAD_DIM : (g + 1) * HEAD_DIM] = both[:, HEAD_DIM:]


def ends_of(info_ref):
    ends = [info_ref[0]]
    for k in range(1, 6):
        ends.append(ends[-1] + info_ref[k])
    return ends


def stack_heads(x):
    return jnp.concatenate(
        [x[:, h * HEAD_DIM : (h + 1) * HEAD_DIM] for h in range(GROUP)], axis=0
    )


def unstack_heads(x):
    rows = x.shape[0] // GROUP
    return jnp.concatenate([x[h * rows : (h + 1) * rows] for h in range(GROUP)], axis=1)


def attend(
    info_ref, weight_ref, recv_ref, keys, values, r1t_ref, r2t_ref, r1_ref,
    bias, value_ones, raised, dscore, score, put_kv, put_back,
):
    rows, length = bias.shape
    count = len(score)
    e0, e1, e2, e3, e4, _ = ends_of(info_ref)
    place = info_ref[6] * rows + iota((rows, 1), 0)
    rejected = (place >= e1) & (place < e2)
    first = jnp.where(place >= e2, e2, 0)
    hidden_from = jnp.where(place >= e4, e3, jnp.where(rejected, e0, 0))
    hidden_to = jnp.where(place >= e4, e4, jnp.where(rejected, e1, 0))
    other = iota((rows, length), 1)
    seen = (other >= first) & (other <= place) & ((other < hidden_from) | (other >= hidden_to))
    bias[...] = jnp.where(seen, 0.0, MASKED)
    weight = jnp.where(place >= e2, weight_ref[1], weight_ref[0])
    factor = jnp.where(rejected | (place >= e4), -weight, weight)

    main = count * BOTH_WIDTH
    _, ranges = spread(main // HEAD_DIM)
    r1t = r1t_ref[...]
    query, cotangent, inverse, attended, delta = ([None] * count for _ in range(5))
    for n in range(count):
        value_ones[n][:, HEAD_DIM:] = jnp.ones((length, HEAD_DIM), jnp.bfloat16)
        value_ones[n][:, :HEAD_DIM] = values[n]()
        tiles = BOTH_WIDTH // HEAD_DIM
        spare = []
        for c, (lo, hi) in enumerate(ranges):
            start, stop = max(lo, n * tiles), min(hi, (n + 1) * tiles)
            if start < stop:
                columns = slice(main + (start - lo) * HEAD_DIM, main + (stop - lo) * HEAD_DIM)
                spare.append(dot(r2t_ref[c], recv_ref[:, columns]))
        both = dot(r1t, recv_ref[:, n * BOTH_WIDTH : (n + 1) * BOTH_WIDTH]) + jnp.concatenate(
            spare, axis=1
        )
        query[n] = stack_heads(low(both[:, :GROUP_WIDTH]))
        cotangent[n] = stack_heads(low(factor * both[:, GROUP_WIDTH:]))
    for n in range(count):
        score[n][...] = dot(query[n], keys[n](), ((1,), (1,)))
    for n in range(count):
        for h in range(GROUP):
            part = slice(h * rows, (h + 1) * rows)
            masked = score[n][part, :] + bias[...]
            highest = jnp.max(masked, axis=1, keepdims=True)
            raised[n][part, :] = low(jnp.exp2((masked - highest) * EXPONENT))
    for n in range(count):
        score[n][...] = dot(cotangent[n], value_ones[n][:, :HEAD_DIM], ((1,), (1,)))
    for n in range(count):
        summed = dot(raised[n][...], value_ones[n][...])
        inverse[n] = 1.0 / summed[:, HEAD_DIM:]
        attended[n] = low(summed[:, :HEAD_DIM] * inverse[n])
        delta[n] = jnp.sum(
            cotangent[n].astype(jnp.float32) * attended[n].astype(jnp.float32),
            axis=1,
            keepdims=True,
        )
    for n in range(count):
        dscore[n][...] = raised[n][...] * low(score[n][...] - delta[n])
    for n in range(count):
        scaled = inverse[n] * SCALING
        query_low = low(query[n].astype(jnp.float32) * scaled)
        cotangent_low = low(cotangent[n].astype(jnp.float32) * inverse[n])
        put_kv(
            n,
            low(dot(query_low.T, dscore[n][...])).T,
            low(dot(cotangent_low.T, raised[n][...])).T,
        )
        query_grad = low(dot(dscore[n][...], keys[n]()) * scaled)
        both = jnp.concatenate([unstack_heads(attended[n]), unstack_heads(query_grad)], axis=1)
        put_back(n, low(dot(r1_ref[...], both)), both)


def first_kernel(
    info_ref, weight_ref, recv_ref, kv_all_ref, r1t_ref, r2t_ref, r1_ref, r2_ref,
    kv_ref, send_ref, spare_ref,
    bias, value_ones, raised, dscore, score, kv_own, send_own, copied,
):
    count = len(score)
    spare = []
    copies = []

    def copy(source, target):
        copies.append(pltpu.make_async_copy(source, target, copied.at[len(copies)]))
        copies[-1].start()

    def key(n):
        return lambda: kv_all_ref[:, n * HEAD_DIM : (n + 1) * HEAD_DIM]

    def value(n):
        return lambda: kv_all_ref[:, KV_WIDTH + n * HEAD_DIM : KV_WIDTH + (n + 1) * HEAD_DIM]

    def put_kv(n, key_part, value_part):
        kv_own[n][:, :HEAD_DIM] = key_part
        kv_own[n][:, HEAD_DIM:] = value_part
        copy(kv_own[n], kv_ref.at[:, n * PAIR_WIDTH : (n + 1) * PAIR_WIDTH])

    def put_back(n, main, both):
        send_own[n][...] = main
        copy(send_own[n], send_ref.at[:, n * BOTH_WIDTH : (n + 1) * BOTH_WIDTH])
        spare.append(dot(r2_ref[n], both))

    attend(
        info_ref, weight_ref, recv_ref, [key(n) for n in range(count)],
        [value(n) for n in range(count)], r1t_ref, r2t_ref, r1_ref,
        bias, value_ones, raised, dscore, score, put_kv, put_back,
    )
    spare_ref[...] = low(sum(spare))
    for started in copies:
        started.wait()


def last_kernel(
    info_ref, weight_ref, recv_ref, key_ref, value_ref, r1t_ref, r2t_ref, r1_ref, r2_ref,
    spare_ref, _kv, _send, kv_ref, send_ref,
    bias, value_ones, raised, dscore, score, kv_own, send_own, copied,
):
    group = KV_HEADS - 1
    copies = []

    def copy(source, target):
        copies.append(pltpu.make_async_copy(source, target, copied.at[len(copies)]))
        copies[-1].start()

    def put_kv(n, key_part, value_part):
        kv_own[:, :HEAD_DIM] = key_part
        kv_own[:, HEAD_DIM:] = value_part
        copy(kv_own, kv_ref.at[:, group * PAIR_WIDTH : (group + 1) * PAIR_WIDTH])

    def put_back(n, main, both):
        send_own[:, :BOTH_WIDTH] = main
        send_own[:, BOTH_WIDTH:] = low(dot(r2_ref[0], both)) + spare_ref[...]
        copy(send_own, send_ref.at[:, group * BOTH_WIDTH :])

    attend(
        info_ref, weight_ref, recv_ref, [lambda: key_ref[...]], [lambda: value_ref[...]],
        r1t_ref, r2t_ref, r1_ref,
        bias, value_ones, raised, dscore, score, put_kv, put_back,
    )
    for started in copies:
        started.wait()


def shape(dims, kind=jnp.bfloat16):
    return jax.ShapeDtypeStruct(dims, kind)


def cost(flops, moved, exps=0):
    return pl.CostEstimate(flops=int(flops), bytes_accessed=int(moved), transcendentals=int(exps))


def body(queries, keys, values, out_grad, pair_weight, lengths, route_dest, route_slot):
    rows = queries.shape[0]
    ranks = lax.axis_size("dp")
    packs = lax.axis_size("pack")
    seq = rows * packs
    slots = ranks * MAIN
    wide = (KV_HEADS + 1) * BOTH_WIDTH
    narrow = (KV_HEADS + 1) * PAIR_WIDTH
    fence = lax.optimization_barrier

    def exchange(block):
        moved = lax.all_to_all(
            block.reshape(ranks, MAIN, block.shape[1]), "dp", split_axis=0, concat_axis=0, tiled=True
        )
        return moved.reshape(block.shape)

    down = (shape((slots, rows)), shape((KV_HEADS, slots, rows)))
    across = (shape((rows, slots)), shape((KV_HEADS, rows, slots)))
    dest = route_dest.reshape(1, rows)

    kv_send = pl.pallas_call(
        send_kernel,
        out_shape=shape((slots, narrow + HEAD_DIM)),
        compiler_params=compiler_params(),
        cost_estimate=cost(4 * slots * rows * 2 * KV_WIDTH, 6 * slots * 2 * KV_WIDTH),
    )(dest, route_slot.reshape(1, rows), keys, values)

    kv_recv = exchange(kv_send)
    p1t, p2t = pl.pallas_call(
        home_maps_kernel,
        out_shape=across,
        compiler_params=compiler_params(),
        cost_estimate=cost(LONG, 6 * slots * rows),
    )(dest)

    def block_width(heads):
        tiles = len(heads) * BOTH_WIDTH // HEAD_DIM
        return (tiles + spread(tiles)[0]) * HEAD_DIM

    first_send, last_send = pl.pallas_call(
        pack_queries_kernel,
        out_shape=tuple(shape((slots, block_width(heads))) for heads in PIECES),
        compiler_params=compiler_params(),
        cost_estimate=cost(LONG, 10 * slots * QUERY_WIDTH),
    )(dest, queries, out_grad)
    kv_recv, first_send, last_send, p1t, p2t = fence((kv_recv, first_send, last_send, p1t, p2t))

    kv_own = pl.pallas_call(
        receive_kernel,
        out_shape=shape((rows, 2 * KV_WIDTH)),
        compiler_params=compiler_params(SMALL_VMEM),
        cost_estimate=cost(4 * slots * rows * 2 * KV_WIDTH, 6 * slots * 2 * KV_WIDTH),
    )(kv_recv)
    kv_all = lax.all_gather(kv_own, "pack", axis=0, tiled=True)
    kv_recv, first_send, last_send, kv_own = fence((kv_recv, first_send, last_send, kv_own))
    r1, r2, r1t, r2t = pl.pallas_call(
        landing_maps_kernel,
        out_shape=(*down, *across),
        compiler_params=compiler_params(),
        cost_estimate=cost(LONG, 6 * slots * rows),
    )(kv_recv)
    first_recv = exchange(first_send)
    first_recv, last_send, r1, r2, r1t, r2t = fence((first_recv, last_send, r1, r2, r1t, r2t))
    last_recv = exchange(last_send)

    info = jnp.concatenate(
        [lengths.reshape(6), lax.axis_index("pack").astype(jnp.int32).reshape(1)]
    )
    weight = pair_weight.reshape(2)
    smem = pl.BlockSpec(memory_space=pltpu.SMEM)
    vmem = pl.BlockSpec(memory_space=pltpu.VMEM)
    anywhere = pl.BlockSpec(memory_space=pl.ANY)
    work = GROUP * rows * seq * HEAD_DIM
    group_rows = GROUP * rows

    def scratch(count):
        return [
            pltpu.VMEM((rows, seq), jnp.float32),
            [pltpu.VMEM((seq, PAIR_WIDTH), jnp.bfloat16)] * count,
            [pltpu.VMEM((group_rows, seq), jnp.bfloat16)] * count,
            [pltpu.VMEM((group_rows, seq), jnp.bfloat16)] * count,
            [pltpu.VMEM((group_rows, seq), jnp.float32)] * count,
        ]

    count = len(PIECES[0])
    kv_first, back_first, back_spare = pl.pallas_call(
        first_kernel,
        in_specs=[smem, smem, vmem, vmem, vmem, vmem, vmem, vmem],
        out_specs=(anywhere, anywhere, vmem),
        out_shape=(
            shape((seq, 2 * KV_WIDTH)),
            shape((slots, wide)),
            shape((slots, BOTH_WIDTH)),
        ),
        scratch_shapes=[
            *scratch(count),
            [pltpu.VMEM((seq, PAIR_WIDTH), jnp.bfloat16)] * count,
            [pltpu.VMEM((slots, BOTH_WIDTH), jnp.bfloat16)] * count,
            pltpu.SemaphoreType.DMA((2 * count,)),
        ],
        compiler_params=compiler_params(),
        cost_estimate=cost(LONG, 2 * HEADS * rows * seq, HEADS * rows * seq),
    )(info, weight, first_recv, kv_all, r1t, r2t, r1, r2)

    def whole(dims):
        return pl.BlockSpec(dims, lambda i: (0,) * len(dims))

    group = KV_HEADS - 1
    kv_part, back_send = pl.pallas_call(
        last_kernel,
        grid=(1,),
        in_specs=[
            smem,
            smem,
            whole(last_recv.shape),
            pl.BlockSpec((seq, HEAD_DIM), lambda i: (0, group)),
            pl.BlockSpec((seq, HEAD_DIM), lambda i: (0, KV_HEADS + group)),
            whole(r1t.shape),
            whole(r2t.shape),
            whole(r1.shape),
            pl.BlockSpec((1, slots, rows), lambda i: (group, 0, 0)),
            whole(back_spare.shape),
            anywhere,
            anywhere,
        ],
        out_specs=(anywhere, anywhere),
        out_shape=(shape((seq, 2 * KV_WIDTH)), shape((slots, wide))),
        input_output_aliases={10: 0, 11: 1},
        scratch_shapes=[
            *scratch(1),
            pltpu.VMEM((seq, PAIR_WIDTH), jnp.bfloat16),
            pltpu.VMEM((slots, 2 * BOTH_WIDTH), jnp.bfloat16),
            pltpu.SemaphoreType.DMA((2,)),
        ],
        compiler_params=compiler_params(dimension_semantics=("arbitrary",)),
        cost_estimate=cost(12 * work, 2 * GROUP * rows * seq, GROUP * rows * seq),
    )(
        info, weight, last_recv, kv_all, kv_all, r1t, r2t, r1, r2, back_spare, kv_first, back_first,
    )

    back_recv = exchange(back_send)
    kv_grad = lax.psum_scatter(kv_part, "pack", scatter_dimension=0, tiled=True)
    kv_grad_send = pl.pallas_call(
        pack_kernel,
        out_shape=shape((slots, narrow)),
        compiler_params=compiler_params(),
        cost_estimate=cost(4 * slots * rows * 2 * KV_WIDTH, 10 * slots * KV_WIDTH),
    )(kv_grad, r1, r2)
    back_recv, kv_grad_send = fence((back_recv, kv_grad_send))
    kv_back = exchange(kv_grad_send)
    attended, query_grad = pl.pallas_call(
        unpack_queries_kernel,
        out_shape=(shape((rows, QUERY_WIDTH)), shape((rows, QUERY_WIDTH))),
        compiler_params=compiler_params(SMALL_VMEM),
        cost_estimate=cost(LONG, 10 * slots * QUERY_WIDTH),
    )(back_recv, p1t, p2t)
    key_grad, value_grad = pl.pallas_call(
        unpack_kv_kernel,
        out_shape=(shape((rows, KV_WIDTH)), shape((rows, KV_WIDTH))),
        compiler_params=compiler_params(SMALL_VMEM),
        cost_estimate=cost(4 * slots * rows * 2 * KV_WIDTH, 4 * slots * 2 * KV_WIDTH),
    )(kv_back, p1t, p2t)
    return attended, query_grad, key_grad, value_grad


def solution(mesh):
    rows = P(("dp", "pack"), None)
    flat = P(("dp", "pack"))
    return jax.shard_map(
        body,
        mesh=mesh,
        in_specs=(rows, rows, rows, rows, P("dp", None), P("dp", None, None), flat, flat),
        out_specs=(rows, rows, rows, rows),
        check_vma=False,
    )
```

```python
import functools
import math

import jax
import jax.numpy as jnp
from jax import lax
from jax.experimental import pallas as pl
from jax.experimental.pallas import tpu as pltpu
from jax.sharding import PartitionSpec as P

HEAD_DIM = 128
HEADS = 20
KV_HEADS = 4
GROUP = 5
CAP = 10
MAIN = 8
SPARE = CAP - MAIN

QUERY_WIDTH = HEADS * HEAD_DIM
KV_WIDTH = KV_HEADS * HEAD_DIM
GROUP_WIDTH = GROUP * HEAD_DIM
PAIR_WIDTH = 2 * HEAD_DIM
SCALING = HEAD_DIM ** (-0.5)
EXPONENT = SCALING * math.log2(math.e)
MASKED = -1e30
VMEM_LIMIT = 60 * 1024 * 1024
SMALL_VMEM = 16 * 1024 * 1024
BOTH_WIDTH = 2 * GROUP_WIDTH
LONG = 10**11


def dot(left, right, contract=((1,), (0,))):
    return lax.dot_general(left, right, (contract, ((), ())), preferred_element_type=jnp.float32)


def low(x):
    return x.astype(jnp.bfloat16)


def iota(shape, dim):
    return lax.broadcasted_iota(jnp.int32, shape, dim)


def one_hot(condition):
    return jnp.where(condition, 1.0, 0.0).astype(jnp.bfloat16)


def compiler_params(limit=VMEM_LIMIT, **extra):
    return pltpu.CompilerParams(vmem_limit_bytes=limit, **extra)


def ranks_of(dest_row):
    rows = dest_row.shape[1]
    down = iota((rows, rows), 0)
    across = iota((rows, rows), 1)
    dest_col = jnp.sum(
        jnp.where(down == across, dest_row.astype(jnp.float32), 0.0), axis=1, keepdims=True
    ).astype(jnp.int32)
    return dest_col, dest_col == dest_row, down, across


def places_of(dest, rank):
    rank = rank.astype(jnp.int32)
    first = dest * MAIN + rank
    return jnp.where(rank < MAIN, first, -MAIN), jnp.where(rank < MAIN, -MAIN, first - MAIN)


def send_kernel(dest_ref, slot_ref, keys_ref, values_ref, send_ref, p1_ref, p2_ref):
    rows = keys_ref.shape[0]
    slots = send_ref.shape[0]
    dest_row = dest_ref[...]
    _, same, down, across = ranks_of(dest_row)
    rank_row = jnp.sum(jnp.where(same & (down < across), 1.0, 0.0), axis=0, keepdims=True)
    main_row, spare_row = places_of(dest_row, rank_row)
    slot_down = iota((slots, rows), 0)
    p1 = slot_down == main_row
    p1_low = one_hot(p1)
    p1_ref[...] = p1_low
    place = (slot_ref[...] + 1).astype(jnp.float32)
    place_main = jnp.sum(jnp.where(p1, place, 0.0), axis=1, keepdims=True)
    taken = jnp.zeros((slots, rows), jnp.float32)
    spare = jnp.zeros((slots, PAIR_WIDTH), jnp.float32)
    for g in range(KV_HEADS):
        p2 = slot_down == spare_row + SPARE * g
        p2_low = one_hot(p2)
        p2_ref[g] = p2_low
        taken += jnp.where(p2, place, 0.0)
        source = keys_ref if g < 2 else values_ref
        columns = source[:, (g % 2) * PAIR_WIDTH : (g % 2 + 1) * PAIR_WIDTH]
        send_ref[:, g * PAIR_WIDTH : (g + 1) * PAIR_WIDTH] = low(dot(p1_low, columns))
        spare += dot(p2_low, columns)
    place_spare = jnp.sum(taken, axis=1, keepdims=True)
    send_ref[:, 4 * PAIR_WIDTH : 5 * PAIR_WIDTH] = low(spare)
    lane = iota((slots, HEAD_DIM), 1)
    send_ref[:, 5 * PAIR_WIDTH :] = low(
        jnp.where(lane == 0, place_main, jnp.where(lane == 1, place_spare, 0.0))
    )


def home_kernel(dest_ref, home_ref):
    dest_col, same, down, across = ranks_of(dest_ref[...])
    rank_col = jnp.sum(jnp.where(same & (across < down), 1.0, 0.0), axis=1, keepdims=True)
    main_col, spare_col = places_of(dest_col, rank_col)
    lane = iota(home_ref.shape, 1)
    home_ref[...] = jnp.where(lane == 0, main_col, spare_col)


def home_maps(home_ref, slots):
    rows = home_ref.shape[0]
    slot_across = iota((rows, slots), 1)
    spare_col = home_ref[:, 1:2]
    return one_hot(slot_across == home_ref[:, :1]), [
        one_hot(slot_across == spare_col + SPARE * g) for g in range(KV_HEADS)
    ]


def landing_of(recv_ref):
    slots = recv_ref.shape[0]
    tile = recv_ref[:, 5 * PAIR_WIDTH :].astype(jnp.float32)
    lane = iota((slots, HEAD_DIM), 1)
    main_col = jnp.sum(jnp.where(lane == 0, tile, 0.0), axis=1, keepdims=True)
    spare_col = jnp.sum(jnp.where(lane == 1, tile, 0.0), axis=1, keepdims=True)
    return main_col, spare_col


def landing_rows(main_col, spare_col):
    slots = main_col.shape[0]
    diagonal = iota((slots, slots), 0) == iota((slots, slots), 1)
    return (
        jnp.sum(jnp.where(diagonal, main_col, 0.0), axis=0, keepdims=True).astype(jnp.int32),
        jnp.sum(jnp.where(diagonal, spare_col, 0.0), axis=0, keepdims=True).astype(jnp.int32),
    )


def landing_maps(rows, slots, main_row, spare_row):
    place_down = iota((rows, slots), 0) + 1
    part_across = (iota((rows, slots), 1) & (MAIN - 1)) >> 1
    r1t = one_hot(place_down == main_row)
    return r1t, [one_hot((place_down == spare_row) & (part_across == g)) for g in range(KV_HEADS)]


def receive_kernel(recv_ref, kv_ref):
    rows = kv_ref.shape[0]
    slots = recv_ref.shape[0]
    r1t, r2t = landing_maps(rows, slots, *landing_rows(*landing_of(recv_ref)))
    spare = recv_ref[:, 4 * PAIR_WIDTH : 5 * PAIR_WIDTH]
    for g in range(KV_HEADS):
        columns = slice(g * PAIR_WIDTH, (g + 1) * PAIR_WIDTH)
        kv_ref[:, columns] = low(dot(r1t, recv_ref[:, columns]) + dot(r2t[g], spare))


def landing_maps_kernel(recv_ref, r1_ref, r2_ref, r1t_ref, r2t_ref):
    slots, rows = r1_ref.shape
    main_col, spare_col = landing_of(recv_ref)
    r1t, r2t = landing_maps(rows, slots, *landing_rows(main_col, spare_col))
    r1t_ref[...] = r1t
    main_col = main_col.astype(jnp.int32)
    spare_col = spare_col.astype(jnp.int32)
    place_across = iota((slots, rows), 1) + 1
    part_down = (iota((slots, rows), 0) & (MAIN - 1)) >> 1
    r1_ref[...] = one_hot(place_across == main_col)
    for g in range(KV_HEADS):
        r2_ref[g] = one_hot((place_across == spare_col) & (part_down == g))
        r2t_ref[g] = r2t[g]


def pack_queries_kernel(query_ref, grad_ref, m1_ref, m2_ref, send_ref):
    m1 = m1_ref[...]
    spare = jnp.zeros((send_ref.shape[0], BOTH_WIDTH), jnp.float32)
    for g in range(KV_HEADS):
        columns = slice(g * GROUP_WIDTH, (g + 1) * GROUP_WIDTH)
        part = jnp.concatenate([query_ref[:, columns], grad_ref[:, columns]], axis=1)
        send_ref[:, g * BOTH_WIDTH : (g + 1) * BOTH_WIDTH] = low(dot(m1, part))
        spare += dot(m2_ref[g], part)
    send_ref[:, KV_HEADS * BOTH_WIDTH :] = low(spare)


def pack_kernel(source_ref, m1_ref, m2_ref, send_ref):
    width = source_ref.shape[1] // KV_HEADS
    m1 = m1_ref[...]
    spare = jnp.zeros((send_ref.shape[0], width), jnp.float32)
    for g in range(KV_HEADS):
        columns = slice(g * width, (g + 1) * width)
        part = low(source_ref[:, columns])
        send_ref[:, columns] = low(dot(m1, part))
        spare += dot(m2_ref[g], part)
    send_ref[:, KV_HEADS * width :] = low(spare)


def unpack_queries_kernel(recv_ref, home_ref, attended_ref, grad_ref):
    m1, m2 = home_maps(home_ref, recv_ref.shape[0])
    spare = recv_ref[:, KV_HEADS * BOTH_WIDTH :]
    for g in range(KV_HEADS):
        part = recv_ref[:, g * BOTH_WIDTH : (g + 1) * BOTH_WIDTH]
        both = low(dot(m1, part) + dot(m2[g], spare))
        columns = slice(g * GROUP_WIDTH, (g + 1) * GROUP_WIDTH)
        attended_ref[:, columns] = both[:, :GROUP_WIDTH]
        grad_ref[:, columns] = both[:, GROUP_WIDTH:]


def unpack_kv_kernel(recv_ref, home_ref, key_ref, value_ref):
    m1, m2 = home_maps(home_ref, recv_ref.shape[0])
    spare = recv_ref[:, KV_HEADS * PAIR_WIDTH :]
    for g in range(KV_HEADS):
        both = low(
            dot(m1, recv_ref[:, g * PAIR_WIDTH : (g + 1) * PAIR_WIDTH]) + dot(m2[g], spare)
        )
        key_ref[:, g * HEAD_DIM : (g + 1) * HEAD_DIM] = both[:, :HEAD_DIM]
        value_ref[:, g * HEAD_DIM : (g + 1) * HEAD_DIM] = both[:, HEAD_DIM:]


def ends_of(info_ref):
    ends = [info_ref[0]]
    for k in range(1, 6):
        ends.append(ends[-1] + info_ref[k])
    return ends


def stack_heads(x):
    return jnp.concatenate(
        [x[:, h * HEAD_DIM : (h + 1) * HEAD_DIM] for h in range(GROUP)], axis=0
    )


def unstack_heads(x):
    rows = x.shape[0] // GROUP
    return jnp.concatenate([x[h * rows : (h + 1) * rows] for h in range(GROUP)], axis=1)


def attention_kernel(
    info_ref, weight_ref, main_ref, spare_ref, key_ref, value_ref, r1t_ref, r2t_ref, r1_ref, r2_ref,
    kv_ref, send_ref, bias, spare_sum, value_ones, raised, dscore, score, dprob, ready, left,
):
    step = pl.program_id(0)
    rows, keys = bias.shape
    count = len(score)
    steps = KV_HEADS // count

    def leave(k):
        first = k * count * BOTH_WIDTH
        columns = pl.ds(first, BOTH_WIDTH if k == steps else count * BOTH_WIDTH)
        return pltpu.make_async_copy(ready.at[:, columns], send_ref.at[:, columns], left.at[k])

    e0, e1, e2, e3, e4, _ = ends_of(info_ref)
    place = info_ref[6] * rows + iota((rows, 1), 0)
    rejected = (place >= e1) & (place < e2)

    @pl.when(step == 0)
    def _():
        first = jnp.where(place >= e2, e2, 0)
        hidden_from = jnp.where(place >= e4, e3, jnp.where(rejected, e0, 0))
        hidden_to = jnp.where(place >= e4, e4, jnp.where(rejected, e1, 0))
        other = iota((rows, keys), 1)
        seen = (other >= first) & (other <= place) & ((other < hidden_from) | (other >= hidden_to))
        bias[...] = jnp.where(seen, 0.0, MASKED)
        spare_sum[...] = jnp.zeros_like(spare_sum)
        for n in range(count):
            value_ones[n][:, HEAD_DIM:] = jnp.ones((keys, HEAD_DIM), jnp.bfloat16)

    weight = jnp.where(place >= e2, weight_ref[1], weight_ref[0])
    factor = jnp.where(rejected | (place >= e4), -weight, weight)
    query, cotangent, key, inverse, attended, delta = ([None] * count for _ in range(6))
    for n in range(count):
        columns = slice(n * HEAD_DIM, (n + 1) * HEAD_DIM)
        both = dot(r1t_ref[...], main_ref[:, n * BOTH_WIDTH : (n + 1) * BOTH_WIDTH]) + dot(
            r2t_ref[n], spare_ref[...]
        )
        query[n] = stack_heads(low(both[:, :GROUP_WIDTH]))
        cotangent[n] = stack_heads(low(factor * both[:, GROUP_WIDTH:]))
        key[n] = key_ref[:, columns]
        value_ones[n][:, :HEAD_DIM] = value_ref[:, columns]
    for n in range(count):
        score[n][...] = dot(query[n], key[n], ((1,), (1,)))
    for n in range(count):
        for h in range(GROUP):
            part = slice(h * rows, (h + 1) * rows)
            seen = score[n][part, :] + bias[...]
            highest = jnp.max(seen, axis=1, keepdims=True)
            raised[n][part, :] = low(jnp.exp2((seen - highest) * EXPONENT))
    for n in range(count):
        dprob[n][...] = dot(cotangent[n], value_ones[n][:, :HEAD_DIM], ((1,), (1,)))
    for n in range(count):
        summed = dot(raised[n][...], value_ones[n][...])
        inverse[n] = 1.0 / summed[:, HEAD_DIM:]
        attended[n] = low(summed[:, :HEAD_DIM] * inverse[n])
        delta[n] = jnp.sum(
            cotangent[n].astype(jnp.float32) * attended[n].astype(jnp.float32),
            axis=1,
            keepdims=True,
        )
    for n in range(count):
        dscore[n][...] = raised[n][...] * low(dprob[n][...] - delta[n])
    for n in range(count):
        scaled = inverse[n] * SCALING
        query_grad = low(dot(dscore[n][...], key[n]) * scaled)
        query_low = low(query[n].astype(jnp.float32) * scaled)
        cotangent_low = low(cotangent[n].astype(jnp.float32) * inverse[n])
        first = n * PAIR_WIDTH
        kv_ref[:, first : first + HEAD_DIM] = low(dot(query_low.T, dscore[n][...])).T
        kv_ref[:, first + HEAD_DIM : first + PAIR_WIDTH] = low(dot(cotangent_low.T, raised[n][...])).T
        both = jnp.concatenate([unstack_heads(attended[n]), unstack_heads(query_grad)], axis=1)
        start = pl.multiple_of((step * count + n) * BOTH_WIDTH, BOTH_WIDTH)
        ready[:, pl.ds(start, BOTH_WIDTH)] = low(dot(r1_ref[...], both))
        spare_sum[...] += dot(r2_ref[n], both)

    for k in range(steps):

        @pl.when(step == k)
        def _():
            leave(k).start()

    @pl.when(step == steps - 1)
    def _():
        ready[:, KV_HEADS * BOTH_WIDTH :] = low(spare_sum[...])
        leave(steps).start()
        for k in range(steps + 1):
            leave(k).wait()


def shape(dims, kind=jnp.bfloat16):
    return jax.ShapeDtypeStruct(dims, kind)


def cost(flops, moved, exps=0):
    return pl.CostEstimate(flops=int(flops), bytes_accessed=int(moved), transcendentals=int(exps))


def body(queries, keys, values, out_grad, pair_weight, lengths, route_dest, route_slot):
    rows = queries.shape[0]
    ranks = lax.axis_size("dp")
    packs = lax.axis_size("pack")
    seq = rows * packs
    slots = ranks * MAIN
    wide = (KV_HEADS + 1) * BOTH_WIDTH
    narrow = (KV_HEADS + 1) * PAIR_WIDTH
    fence = lax.optimization_barrier

    def exchange(block):
        moved = lax.all_to_all(
            block.reshape(ranks, MAIN, block.shape[1]), "dp", split_axis=0, concat_axis=0, tiled=True
        )
        return moved.reshape(block.shape)

    down = (shape((slots, rows)), shape((KV_HEADS, slots, rows)))
    across = (shape((rows, slots)), shape((KV_HEADS, rows, slots)))
    dest = route_dest.reshape(1, rows)

    kv_send, p1, p2 = pl.pallas_call(
        send_kernel,
        out_shape=(shape((slots, narrow + HEAD_DIM)), *down),
        compiler_params=compiler_params(),
        cost_estimate=cost(4 * slots * rows * 2 * KV_WIDTH, 6 * slots * 2 * KV_WIDTH),
    )(dest, route_slot.reshape(1, rows), keys, values)

    kv_recv = exchange(kv_send)
    home = pl.pallas_call(
        home_kernel,
        out_shape=shape((rows, HEAD_DIM), jnp.int32),
        compiler_params=compiler_params(),
        cost_estimate=cost(LONG, 6 * slots * rows),
    )(dest)
    query_send = pl.pallas_call(
        pack_queries_kernel,
        out_shape=shape((slots, wide)),
        compiler_params=compiler_params(),
        cost_estimate=cost(LONG, 10 * slots * QUERY_WIDTH),
    )(queries, out_grad, p1, p2)
    kv_recv, query_send, home = fence((kv_recv, query_send, home))

    kv_own = pl.pallas_call(
        receive_kernel,
        out_shape=shape((rows, 2 * KV_WIDTH)),
        compiler_params=compiler_params(SMALL_VMEM),
        cost_estimate=cost(4 * slots * rows * 2 * KV_WIDTH, 6 * slots * 2 * KV_WIDTH),
    )(kv_recv)
    kv_all = lax.all_gather(kv_own, "pack", axis=0, tiled=True)
    kv_recv, query_send, kv_own = fence((kv_recv, query_send, kv_own))
    r1, r2, r1t, r2t = pl.pallas_call(
        landing_maps_kernel,
        out_shape=(*down, *across),
        compiler_params=compiler_params(),
        cost_estimate=cost(LONG, 6 * slots * rows),
    )(kv_recv)
    query_recv = exchange(query_send)

    info = jnp.concatenate(
        [lengths.reshape(6), lax.axis_index("pack").astype(jnp.int32).reshape(1)]
    )
    smem = pl.BlockSpec(memory_space=pltpu.SMEM)
    at_once = 2
    steps = KV_HEADS // at_once
    work = HEADS * rows * seq * HEAD_DIM

    def several(dims, kind=jnp.bfloat16):
        return [pltpu.VMEM(dims, kind)] * at_once

    kv_part, back_send = pl.pallas_call(
        attention_kernel,
        grid=(steps,),
        in_specs=[
            smem,
            smem,
            pl.BlockSpec((slots, at_once * BOTH_WIDTH), lambda g: (0, g)),
            pl.BlockSpec((slots, BOTH_WIDTH), lambda g: (0, KV_HEADS)),
            pl.BlockSpec((seq, at_once * HEAD_DIM), lambda g: (0, g)),
            pl.BlockSpec((seq, at_once * HEAD_DIM), lambda g: (0, steps + g)),
            pl.BlockSpec((rows, slots), lambda g: (0, 0)),
            pl.BlockSpec((at_once, rows, slots), lambda g: (g, 0, 0)),
            pl.BlockSpec((slots, rows), lambda g: (0, 0)),
            pl.BlockSpec((at_once, slots, rows), lambda g: (g, 0, 0)),
        ],
        out_specs=(
            pl.BlockSpec((seq, at_once * PAIR_WIDTH), lambda g: (0, g)),
            pl.BlockSpec(memory_space=pl.ANY),
        ),
        out_shape=(shape((seq, 2 * KV_WIDTH)), shape((slots, wide))),
        scratch_shapes=[
            pltpu.VMEM((rows, seq), jnp.float32),
            pltpu.VMEM((slots, BOTH_WIDTH), jnp.float32),
            several((seq, PAIR_WIDTH)),
            several((GROUP * rows, seq)),
            several((GROUP * rows, seq)),
            several((GROUP * rows, seq), jnp.float32),
            several((GROUP * rows, seq), jnp.float32),
            pltpu.VMEM((slots, wide), jnp.bfloat16),
            pltpu.SemaphoreType.DMA((steps + 1,)),
        ],
        compiler_params=compiler_params(dimension_semantics=("arbitrary",)),
        cost_estimate=cost(12 * work, 2 * HEADS * rows * seq, HEADS * rows * seq),
    )(
        info, pair_weight.reshape(2), query_recv, query_recv, kv_all, kv_all, r1t, r2t, r1, r2,
    )

    back_recv = exchange(back_send)
    kv_grad = lax.psum_scatter(kv_part, "pack", scatter_dimension=0, tiled=True)
    kv_grad_send = pl.pallas_call(
        pack_kernel,
        out_shape=shape((slots, narrow)),
        compiler_params=compiler_params(),
        cost_estimate=cost(4 * slots * rows * 2 * KV_WIDTH, 10 * slots * KV_WIDTH),
    )(kv_grad, r1, r2)
    back_recv, kv_grad_send = fence((back_recv, kv_grad_send))
    kv_back = exchange(kv_grad_send)
    attended, query_grad = pl.pallas_call(
        unpack_queries_kernel,
        out_shape=(shape((rows, QUERY_WIDTH)), shape((rows, QUERY_WIDTH))),
        compiler_params=compiler_params(SMALL_VMEM),
        cost_estimate=cost(LONG, 10 * slots * QUERY_WIDTH),
    )(back_recv, home)
    key_grad, value_grad = pl.pallas_call(
        unpack_kv_kernel,
        out_shape=(shape((rows, KV_WIDTH)), shape((rows, KV_WIDTH))),
        compiler_params=compiler_params(SMALL_VMEM),
        cost_estimate=cost(4 * slots * rows * 2 * KV_WIDTH, 4 * slots * 2 * KV_WIDTH),
    )(kv_back, home)
    return attended, query_grad, key_grad, value_grad


def solution(mesh):
    rows = P(("dp", "pack"), None)
    flat = P(("dp", "pack"))
    return jax.shard_map(
        body,
        mesh=mesh,
        in_specs=(rows, rows, rows, rows, P("dp", None), P("dp", None, None), flat, flat),
        out_specs=(rows, rows, rows, rows),
        check_vma=False,
    )
```

```python
import functools
import math

import jax
import jax.numpy as jnp
from jax import lax
from jax.experimental import pallas as pl
from jax.experimental.pallas import tpu as pltpu
from jax.sharding import PartitionSpec as P

HEAD_DIM = 128
HEADS = 20
KV_HEADS = 4
GROUP = 5
CAP = 10
MAIN = 8
SPARE = CAP - MAIN

QUERY_WIDTH = HEADS * HEAD_DIM
KV_WIDTH = KV_HEADS * HEAD_DIM
GROUP_WIDTH = GROUP * HEAD_DIM
PAIR_WIDTH = 2 * HEAD_DIM
SCALING = HEAD_DIM ** (-0.5)
EXPONENT = SCALING * math.log2(math.e)
MASKED = -1e30
VMEM_LIMIT = 60 * 1024 * 1024
SMALL_VMEM = 16 * 1024 * 1024
BOTH_WIDTH = 2 * GROUP_WIDTH
LONG = 10**11


def dot(left, right, contract=((1,), (0,))):
    return lax.dot_general(left, right, (contract, ((), ())), preferred_element_type=jnp.float32)


def low(x):
    return x.astype(jnp.bfloat16)


def iota(shape, dim):
    return lax.broadcasted_iota(jnp.int32, shape, dim)


def one_hot(condition):
    return jnp.where(condition, 1.0, 0.0).astype(jnp.bfloat16)


def compiler_params(limit=VMEM_LIMIT, **extra):
    return pltpu.CompilerParams(vmem_limit_bytes=limit, **extra)


def ranks_of(dest_row):
    rows = dest_row.shape[1]
    down = iota((rows, rows), 0)
    across = iota((rows, rows), 1)
    dest_col = jnp.sum(
        jnp.where(down == across, dest_row.astype(jnp.float32), 0.0), axis=1, keepdims=True
    ).astype(jnp.int32)
    return dest_col, dest_col == dest_row, down, across


def places_of(dest, rank):
    rank = rank.astype(jnp.int32)
    first = dest * MAIN + rank
    return jnp.where(rank < MAIN, first, -MAIN), jnp.where(rank < MAIN, -MAIN, first - MAIN)


def send_kernel(dest_ref, slot_ref, keys_ref, values_ref, send_ref, p1_ref, p2_ref):
    rows = keys_ref.shape[0]
    slots = send_ref.shape[0]
    dest_row = dest_ref[...]
    _, same, down, across = ranks_of(dest_row)
    rank_row = jnp.sum(jnp.where(same & (down < across), 1.0, 0.0), axis=0, keepdims=True)
    main_row, spare_row = places_of(dest_row, rank_row)
    slot_down = iota((slots, rows), 0)
    p1 = slot_down == main_row
    p1_low = one_hot(p1)
    p1_ref[...] = p1_low
    place = (slot_ref[...] + 1).astype(jnp.float32)
    place_main = jnp.sum(jnp.where(p1, place, 0.0), axis=1, keepdims=True)
    taken = jnp.zeros((slots, rows), jnp.float32)
    spare = jnp.zeros((slots, PAIR_WIDTH), jnp.float32)
    for g in range(KV_HEADS):
        p2 = slot_down == spare_row + SPARE * g
        p2_low = one_hot(p2)
        p2_ref[g] = p2_low
        taken += jnp.where(p2, place, 0.0)
        source = keys_ref if g < 2 else values_ref
        columns = source[:, (g % 2) * PAIR_WIDTH : (g % 2 + 1) * PAIR_WIDTH]
        send_ref[:, g * PAIR_WIDTH : (g + 1) * PAIR_WIDTH] = low(dot(p1_low, columns))
        spare += dot(p2_low, columns)
    place_spare = jnp.sum(taken, axis=1, keepdims=True)
    send_ref[:, 4 * PAIR_WIDTH : 5 * PAIR_WIDTH] = low(spare)
    lane = iota((slots, HEAD_DIM), 1)
    send_ref[:, 5 * PAIR_WIDTH :] = low(
        jnp.where(lane == 0, place_main, jnp.where(lane == 1, place_spare, 0.0))
    )


def home_kernel(dest_ref, home_ref):
    dest_col, same, down, across = ranks_of(dest_ref[...])
    rank_col = jnp.sum(jnp.where(same & (across < down), 1.0, 0.0), axis=1, keepdims=True)
    main_col, spare_col = places_of(dest_col, rank_col)
    lane = iota(home_ref.shape, 1)
    home_ref[...] = jnp.where(lane == 0, main_col, spare_col)


def home_maps(home_ref, slots):
    rows = home_ref.shape[0]
    slot_across = iota((rows, slots), 1)
    spare_col = home_ref[:, 1:2]
    return one_hot(slot_across == home_ref[:, :1]), [
        one_hot(slot_across == spare_col + SPARE * g) for g in range(KV_HEADS)
    ]


def landing_of(tile):
    slots = tile.shape[0]
    tile = tile.astype(jnp.float32)
    lane = iota((slots, HEAD_DIM), 1)
    main_col = jnp.sum(jnp.where(lane == 0, tile, 0.0), axis=1, keepdims=True)
    spare_col = jnp.sum(jnp.where(lane == 1, tile, 0.0), axis=1, keepdims=True)
    return main_col, spare_col


def landing_rows(main_col, spare_col):
    slots = main_col.shape[0]
    diagonal = iota((slots, slots), 0) == iota((slots, slots), 1)
    return (
        jnp.sum(jnp.where(diagonal, main_col, 0.0), axis=0, keepdims=True).astype(jnp.int32),
        jnp.sum(jnp.where(diagonal, spare_col, 0.0), axis=0, keepdims=True).astype(jnp.int32),
    )


def across_maps(rows, main_row, spare_row):
    slots = main_row.shape[1]
    place_down = iota((rows, slots), 0) + 1
    part_across = (iota((rows, slots), 1) & (MAIN - 1)) >> 1
    return one_hot(place_down == main_row), [
        one_hot((place_down == spare_row) & (part_across == g)) for g in range(KV_HEADS)
    ]


def down_maps(rows, main_col, spare_col):
    slots = main_col.shape[0]
    main_col = main_col.astype(jnp.int32)
    spare_col = spare_col.astype(jnp.int32)
    place_across = iota((slots, rows), 1) + 1
    part_down = (iota((slots, rows), 0) & (MAIN - 1)) >> 1
    return one_hot(place_across == main_col), [
        one_hot((place_across == spare_col) & (part_down == g)) for g in range(KV_HEADS)
    ]


def receive_kernel(recv_ref, kv_ref):
    r1t, r2t = across_maps(kv_ref.shape[0], *landing_rows(*landing_of(recv_ref[:, 5 * PAIR_WIDTH :])))
    spare = recv_ref[:, 4 * PAIR_WIDTH : 5 * PAIR_WIDTH]
    for g in range(KV_HEADS):
        columns = slice(g * PAIR_WIDTH, (g + 1) * PAIR_WIDTH)
        kv_ref[:, columns] = low(dot(r1t, recv_ref[:, columns]) + dot(r2t[g], spare))


def pack_queries_kernel(query_ref, grad_ref, m1_ref, m2_ref, send_ref):
    m1 = m1_ref[...]
    spare = jnp.zeros((send_ref.shape[0], BOTH_WIDTH), jnp.float32)
    for g in range(KV_HEADS):
        columns = slice(g * GROUP_WIDTH, (g + 1) * GROUP_WIDTH)
        part = jnp.concatenate([query_ref[:, columns], grad_ref[:, columns]], axis=1)
        send_ref[:, g * BOTH_WIDTH : (g + 1) * BOTH_WIDTH] = low(dot(m1, part))
        spare += dot(m2_ref[g], part)
    send_ref[:, KV_HEADS * BOTH_WIDTH :] = low(spare)


def pack_kernel(source_ref, landing_ref, send_ref):
    width = source_ref.shape[1] // KV_HEADS
    m1, m2 = down_maps(source_ref.shape[0], *landing_of(landing_ref[...]))
    spare = jnp.zeros((send_ref.shape[0], width), jnp.float32)
    for g in range(KV_HEADS):
        columns = slice(g * width, (g + 1) * width)
        part = low(source_ref[:, columns])
        send_ref[:, columns] = low(dot(m1, part))
        spare += dot(m2[g], part)
    send_ref[:, KV_HEADS * width :] = low(spare)


def unpack_queries_kernel(recv_ref, home_ref, attended_ref, grad_ref):
    m1, m2 = home_maps(home_ref, recv_ref.shape[0])
    spare = recv_ref[:, KV_HEADS * BOTH_WIDTH :]
    for g in range(KV_HEADS):
        part = recv_ref[:, g * BOTH_WIDTH : (g + 1) * BOTH_WIDTH]
        both = low(dot(m1, part) + dot(m2[g], spare))
        columns = slice(g * GROUP_WIDTH, (g + 1) * GROUP_WIDTH)
        attended_ref[:, columns] = both[:, :GROUP_WIDTH]
        grad_ref[:, columns] = both[:, GROUP_WIDTH:]


def unpack_kv_kernel(recv_ref, home_ref, key_ref, value_ref):
    m1, m2 = home_maps(home_ref, recv_ref.shape[0])
    spare = recv_ref[:, KV_HEADS * PAIR_WIDTH :]
    for g in range(KV_HEADS):
        both = low(
            dot(m1, recv_ref[:, g * PAIR_WIDTH : (g + 1) * PAIR_WIDTH]) + dot(m2[g], spare)
        )
        key_ref[:, g * HEAD_DIM : (g + 1) * HEAD_DIM] = both[:, :HEAD_DIM]
        value_ref[:, g * HEAD_DIM : (g + 1) * HEAD_DIM] = both[:, HEAD_DIM:]


def ends_of(info_ref):
    ends = [info_ref[0]]
    for k in range(1, 6):
        ends.append(ends[-1] + info_ref[k])
    return ends


def stack_heads(x):
    return jnp.concatenate(
        [x[:, h * HEAD_DIM : (h + 1) * HEAD_DIM] for h in range(GROUP)], axis=0
    )


def unstack_heads(x):
    rows = x.shape[0] // GROUP
    return jnp.concatenate([x[h * rows : (h + 1) * rows] for h in range(GROUP)], axis=1)


def attention_kernel(
    info_ref, weight_ref, main_ref, spare_ref, key_ref, value_ref, landing_ref,
    kv_ref, send_ref, bias, spare_sum, value_ones, raised, dscore, score, dprob, ready, left,
    r1, r2, r1t, r2t,
):
    step = pl.program_id(0)
    rows, keys = bias.shape
    count = len(score)
    steps = KV_HEADS // count

    def leave(k):
        first = k * count * BOTH_WIDTH
        columns = pl.ds(first, BOTH_WIDTH if k == steps else count * BOTH_WIDTH)
        return pltpu.make_async_copy(ready.at[:, columns], send_ref.at[:, columns], left.at[k])

    e0, e1, e2, e3, e4, _ = ends_of(info_ref)
    place = info_ref[6] * rows + iota((rows, 1), 0)
    rejected = (place >= e1) & (place < e2)

    @pl.when(step == 0)
    def _():
        first = jnp.where(place >= e2, e2, 0)
        hidden_from = jnp.where(place >= e4, e3, jnp.where(rejected, e0, 0))
        hidden_to = jnp.where(place >= e4, e4, jnp.where(rejected, e1, 0))
        other = iota((rows, keys), 1)
        seen = (other >= first) & (other <= place) & ((other < hidden_from) | (other >= hidden_to))
        bias[...] = jnp.where(seen, 0.0, MASKED)
        spare_sum[...] = jnp.zeros_like(spare_sum)
        landing = landing_of(landing_ref[...])
        r1[...], down = down_maps(rows, *landing)
        r1t[...], across = across_maps(rows, *landing_rows(*landing))
        for g in range(KV_HEADS):
            r2[g] = down[g]
            r2t[g] = across[g]
        for n in range(count):
            value_ones[n][:, HEAD_DIM:] = jnp.ones((keys, HEAD_DIM), jnp.bfloat16)

    weight = jnp.where(place >= e2, weight_ref[1], weight_ref[0])
    factor = jnp.where(rejected | (place >= e4), -weight, weight)
    query, cotangent, key, inverse, attended, delta = ([None] * count for _ in range(6))
    for n in range(count):
        columns = slice(n * HEAD_DIM, (n + 1) * HEAD_DIM)
        both = dot(r1t[...], main_ref[:, n * BOTH_WIDTH : (n + 1) * BOTH_WIDTH]) + dot(
            r2t[step * count + n], spare_ref[...]
        )
        query[n] = stack_heads(low(both[:, :GROUP_WIDTH]))
        cotangent[n] = stack_heads(low(factor * both[:, GROUP_WIDTH:]))
        key[n] = key_ref[:, columns]
        value_ones[n][:, :HEAD_DIM] = value_ref[:, columns]
    for n in range(count):
        score[n][...] = dot(query[n], key[n], ((1,), (1,)))
    for n in range(count):
        for h in range(GROUP):
            part = slice(h * rows, (h + 1) * rows)
            seen = score[n][part, :] + bias[...]
            highest = jnp.max(seen, axis=1, keepdims=True)
            raised[n][part, :] = low(jnp.exp2((seen - highest) * EXPONENT))
    for n in range(count):
        dprob[n][...] = dot(cotangent[n], value_ones[n][:, :HEAD_DIM], ((1,), (1,)))
    for n in range(count):
        summed = dot(raised[n][...], value_ones[n][...])
        inverse[n] = 1.0 / summed[:, HEAD_DIM:]
        attended[n] = low(summed[:, :HEAD_DIM] * inverse[n])
        delta[n] = jnp.sum(
            cotangent[n].astype(jnp.float32) * attended[n].astype(jnp.float32),
            axis=1,
            keepdims=True,
        )
    for n in range(count):
        dscore[n][...] = raised[n][...] * low(dprob[n][...] - delta[n])
    for n in range(count):
        scaled = inverse[n] * SCALING
        query_grad = low(dot(dscore[n][...], key[n]) * scaled)
        query_low = low(query[n].astype(jnp.float32) * scaled)
        cotangent_low = low(cotangent[n].astype(jnp.float32) * inverse[n])
        first = n * PAIR_WIDTH
        kv_ref[:, first : first + HEAD_DIM] = low(dot(query_low.T, dscore[n][...])).T
        kv_ref[:, first + HEAD_DIM : first + PAIR_WIDTH] = low(dot(cotangent_low.T, raised[n][...])).T
        both = jnp.concatenate([unstack_heads(attended[n]), unstack_heads(query_grad)], axis=1)
        start = pl.multiple_of((step * count + n) * BOTH_WIDTH, BOTH_WIDTH)
        ready[:, pl.ds(start, BOTH_WIDTH)] = low(dot(r1[...], both))
        spare_sum[...] += dot(r2[step * count + n], both)

    for k in range(steps):

        @pl.when(step == k)
        def _():
            leave(k).start()

    @pl.when(step == steps - 1)
    def _():
        ready[:, KV_HEADS * BOTH_WIDTH :] = low(spare_sum[...])
        leave(steps).start()
        for k in range(steps + 1):
            leave(k).wait()


def shape(dims, kind=jnp.bfloat16):
    return jax.ShapeDtypeStruct(dims, kind)


def cost(flops, moved, exps=0):
    return pl.CostEstimate(flops=int(flops), bytes_accessed=int(moved), transcendentals=int(exps))


def body(queries, keys, values, out_grad, pair_weight, lengths, route_dest, route_slot):
    rows = queries.shape[0]
    ranks = lax.axis_size("dp")
    packs = lax.axis_size("pack")
    seq = rows * packs
    slots = ranks * MAIN
    wide = (KV_HEADS + 1) * BOTH_WIDTH
    narrow = (KV_HEADS + 1) * PAIR_WIDTH
    fence = lax.optimization_barrier

    def exchange(block):
        moved = lax.all_to_all(
            block.reshape(ranks, MAIN, block.shape[1]), "dp", split_axis=0, concat_axis=0, tiled=True
        )
        return moved.reshape(block.shape)

    down = (shape((slots, rows)), shape((KV_HEADS, slots, rows)))
    dest = route_dest.reshape(1, rows)

    kv_send, p1, p2 = pl.pallas_call(
        send_kernel,
        out_shape=(shape((slots, narrow + HEAD_DIM)), *down),
        compiler_params=compiler_params(),
        cost_estimate=cost(4 * slots * rows * 2 * KV_WIDTH, 6 * slots * 2 * KV_WIDTH),
    )(dest, route_slot.reshape(1, rows), keys, values)

    kv_recv = exchange(kv_send)
    home = pl.pallas_call(
        home_kernel,
        out_shape=shape((rows, HEAD_DIM), jnp.int32),
        compiler_params=compiler_params(),
        cost_estimate=cost(LONG, 6 * slots * rows),
    )(dest)
    query_send = pl.pallas_call(
        pack_queries_kernel,
        out_shape=shape((slots, wide)),
        compiler_params=compiler_params(),
        cost_estimate=cost(LONG, 10 * slots * QUERY_WIDTH),
    )(queries, out_grad, p1, p2)
    info = jnp.concatenate(
        [lengths.reshape(6), lax.axis_index("pack").astype(jnp.int32).reshape(1)]
    )
    kv_recv, query_send, home, info = fence((kv_recv, query_send, home, info))

    kv_own = pl.pallas_call(
        receive_kernel,
        out_shape=shape((rows, 2 * KV_WIDTH)),
        compiler_params=compiler_params(SMALL_VMEM),
        cost_estimate=cost(4 * slots * rows * 2 * KV_WIDTH, 6 * slots * 2 * KV_WIDTH),
    )(kv_recv)
    kv_all = lax.all_gather(kv_own, "pack", axis=0, tiled=True)
    query_send, kv_own = fence((query_send, kv_own))
    query_recv = exchange(query_send)

    smem = pl.BlockSpec(memory_space=pltpu.SMEM)
    at_once = 2
    landing_spec = pl.BlockSpec((slots, HEAD_DIM), lambda g: (0, narrow // HEAD_DIM))
    steps = KV_HEADS // at_once
    work = HEADS * rows * seq * HEAD_DIM

    def several(dims, kind=jnp.bfloat16):
        return [pltpu.VMEM(dims, kind)] * at_once

    kv_part, back_send = pl.pallas_call(
        attention_kernel,
        grid=(steps,),
        in_specs=[
            smem,
            smem,
            pl.BlockSpec((slots, at_once * BOTH_WIDTH), lambda g: (0, g)),
            pl.BlockSpec((slots, BOTH_WIDTH), lambda g: (0, KV_HEADS)),
            pl.BlockSpec((seq, at_once * HEAD_DIM), lambda g: (0, g)),
            pl.BlockSpec((seq, at_once * HEAD_DIM), lambda g: (0, steps + g)),
            landing_spec,
        ],
        out_specs=(
            pl.BlockSpec((seq, at_once * PAIR_WIDTH), lambda g: (0, g)),
            pl.BlockSpec(memory_space=pl.ANY),
        ),
        out_shape=(shape((seq, 2 * KV_WIDTH)), shape((slots, wide))),
        scratch_shapes=[
            pltpu.VMEM((rows, seq), jnp.float32),
            pltpu.VMEM((slots, BOTH_WIDTH), jnp.float32),
            several((seq, PAIR_WIDTH)),
            several((GROUP * rows, seq)),
            several((GROUP * rows, seq)),
            several((GROUP * rows, seq), jnp.float32),
            several((GROUP * rows, seq), jnp.float32),
            pltpu.VMEM((slots, wide), jnp.bfloat16),
            pltpu.SemaphoreType.DMA((steps + 1,)),
            pltpu.VMEM((slots, rows), jnp.bfloat16),
            pltpu.VMEM((KV_HEADS, slots, rows), jnp.bfloat16),
            pltpu.VMEM((rows, slots), jnp.bfloat16),
            pltpu.VMEM((KV_HEADS, rows, slots), jnp.bfloat16),
        ],
        compiler_params=compiler_params(dimension_semantics=("arbitrary",)),
        cost_estimate=cost(12 * work, 2 * HEADS * rows * seq, HEADS * rows * seq),
    )(
        info, pair_weight.reshape(2), query_recv, query_recv, kv_all, kv_all, kv_recv,
    )

    back_recv = exchange(back_send)
    kv_grad = lax.psum_scatter(kv_part, "pack", scatter_dimension=0, tiled=True)
    kv_grad_send = pl.pallas_call(
        pack_kernel,
        grid=(1,),
        in_specs=[pl.BlockSpec((rows, 2 * KV_WIDTH), lambda i: (0, 0)), landing_spec],
        out_specs=pl.BlockSpec((slots, narrow), lambda i: (0, 0)),
        out_shape=shape((slots, narrow)),
        compiler_params=compiler_params(),
        cost_estimate=cost(4 * slots * rows * 2 * KV_WIDTH, 10 * slots * KV_WIDTH),
    )(kv_grad, kv_recv)
    back_recv, kv_grad_send = fence((back_recv, kv_grad_send))
    kv_back = exchange(kv_grad_send)
    attended, query_grad = pl.pallas_call(
        unpack_queries_kernel,
        out_shape=(shape((rows, QUERY_WIDTH)), shape((rows, QUERY_WIDTH))),
        compiler_params=compiler_params(SMALL_VMEM),
        cost_estimate=cost(LONG, 10 * slots * QUERY_WIDTH),
    )(back_recv, home)
    key_grad, value_grad = pl.pallas_call(
        unpack_kv_kernel,
        out_shape=(shape((rows, KV_WIDTH)), shape((rows, KV_WIDTH))),
        compiler_params=compiler_params(SMALL_VMEM),
        cost_estimate=cost(4 * slots * rows * 2 * KV_WIDTH, 4 * slots * 2 * KV_WIDTH),
    )(kv_back, home)
    return attended, query_grad, key_grad, value_grad


def solution(mesh):
    rows = P(("dp", "pack"), None)
    flat = P(("dp", "pack"))
    return jax.shard_map(
        body,
        mesh=mesh,
        in_specs=(rows, rows, rows, rows, P("dp", None), P("dp", None, None), flat, flat),
        out_specs=(rows, rows, rows, rows),
        check_vma=False,
    )
```

```python
import functools
import math

import jax
import jax.numpy as jnp
from jax import lax
from jax.experimental import pallas as pl
from jax.experimental.pallas import tpu as pltpu
from jax.sharding import PartitionSpec as P

HEAD_DIM = 128
HEADS = 20
KV_HEADS = 4
GROUP = 5
CAP = 10
MAIN = 8
SPARE = CAP - MAIN

QUERY_WIDTH = HEADS * HEAD_DIM
KV_WIDTH = KV_HEADS * HEAD_DIM
GROUP_WIDTH = GROUP * HEAD_DIM
PAIR_WIDTH = 2 * HEAD_DIM
SCALING = HEAD_DIM ** (-0.5)
EXPONENT = SCALING * math.log2(math.e)
MASKED = -1e30
VMEM_LIMIT = 60 * 1024 * 1024
SMALL_VMEM = 16 * 1024 * 1024
BOTH_WIDTH = 2 * GROUP_WIDTH
LONG = 10**11


def dot(left, right, contract=((1,), (0,))):
    return lax.dot_general(left, right, (contract, ((), ())), preferred_element_type=jnp.float32)


def low(x):
    return x.astype(jnp.bfloat16)


def iota(shape, dim):
    return lax.broadcasted_iota(jnp.int32, shape, dim)


def one_hot(condition):
    return jnp.where(condition, 1.0, 0.0).astype(jnp.bfloat16)


def compiler_params(limit=VMEM_LIMIT, **extra):
    return pltpu.CompilerParams(vmem_limit_bytes=limit, **extra)


def ranks_of(dest_row):
    rows = dest_row.shape[1]
    down = iota((rows, rows), 0)
    across = iota((rows, rows), 1)
    dest_col = jnp.sum(
        jnp.where(down == across, dest_row.astype(jnp.float32), 0.0), axis=1, keepdims=True
    ).astype(jnp.int32)
    return dest_col, dest_col == dest_row, down, across


def places_of(dest, rank):
    rank = rank.astype(jnp.int32)
    first = dest * MAIN + rank
    return jnp.where(rank < MAIN, first, -MAIN), jnp.where(rank < MAIN, -MAIN, first - MAIN)


def send_kernel(dest_ref, slot_ref, keys_ref, values_ref, send_ref, p1_ref, p2_ref):
    rows = keys_ref.shape[0]
    slots = send_ref.shape[0]
    dest_row = dest_ref[...]
    _, same, down, across = ranks_of(dest_row)
    rank_row = jnp.sum(jnp.where(same & (down < across), 1.0, 0.0), axis=0, keepdims=True)
    main_row, spare_row = places_of(dest_row, rank_row)
    slot_down = iota((slots, rows), 0)
    p1 = slot_down == main_row
    p1_low = one_hot(p1)
    p1_ref[...] = p1_low
    place = (slot_ref[...] + 1).astype(jnp.float32)
    place_main = jnp.sum(jnp.where(p1, place, 0.0), axis=1, keepdims=True)
    taken = jnp.zeros((slots, rows), jnp.float32)
    spare = jnp.zeros((slots, PAIR_WIDTH), jnp.float32)
    for g in range(KV_HEADS):
        p2 = slot_down == spare_row + SPARE * g
        p2_low = one_hot(p2)
        p2_ref[g] = p2_low
        taken += jnp.where(p2, place, 0.0)
        source = keys_ref if g < 2 else values_ref
        columns = source[:, (g % 2) * PAIR_WIDTH : (g % 2 + 1) * PAIR_WIDTH]
        send_ref[:, g * PAIR_WIDTH : (g + 1) * PAIR_WIDTH] = low(dot(p1_low, columns))
        spare += dot(p2_low, columns)
    place_spare = jnp.sum(taken, axis=1, keepdims=True)
    send_ref[:, 4 * PAIR_WIDTH : 5 * PAIR_WIDTH] = low(spare)
    lane = iota((slots, HEAD_DIM), 1)
    send_ref[:, 5 * PAIR_WIDTH :] = low(
        jnp.where(lane == 0, place_main, jnp.where(lane == 1, place_spare, 0.0))
    )


def home_kernel(dest_ref, home_ref):
    dest_col, same, down, across = ranks_of(dest_ref[...])
    rank_col = jnp.sum(jnp.where(same & (across < down), 1.0, 0.0), axis=1, keepdims=True)
    main_col, spare_col = places_of(dest_col, rank_col)
    lane = iota(home_ref.shape, 1)
    home_ref[...] = jnp.where(lane == 0, main_col, spare_col)


def home_maps(home_ref, slots):
    rows = home_ref.shape[0]
    slot_across = iota((rows, slots), 1)
    spare_col = home_ref[:, 1:2]
    return one_hot(slot_across == home_ref[:, :1]), [
        one_hot(slot_across == spare_col + SPARE * g) for g in range(KV_HEADS)
    ]


def landing_of(tile):
    slots = tile.shape[0]
    tile = tile.astype(jnp.float32)
    lane = iota((slots, HEAD_DIM), 1)
    main_col = jnp.sum(jnp.where(lane == 0, tile, 0.0), axis=1, keepdims=True)
    spare_col = jnp.sum(jnp.where(lane == 1, tile, 0.0), axis=1, keepdims=True)
    return main_col, spare_col


def landing_rows(main_col, spare_col):
    slots = main_col.shape[0]
    diagonal = iota((slots, slots), 0) == iota((slots, slots), 1)
    return (
        jnp.sum(jnp.where(diagonal, main_col, 0.0), axis=0, keepdims=True).astype(jnp.int32),
        jnp.sum(jnp.where(diagonal, spare_col, 0.0), axis=0, keepdims=True).astype(jnp.int32),
    )


def across_maps(rows, main_row, spare_row):
    slots = main_row.shape[1]
    place_down = iota((rows, slots), 0) + 1
    part_across = (iota((rows, slots), 1) & (MAIN - 1)) >> 1
    return one_hot(place_down == main_row), [
        one_hot((place_down == spare_row) & (part_across == g)) for g in range(KV_HEADS)
    ]


def down_maps(rows, main_col, spare_col):
    slots = main_col.shape[0]
    main_col = main_col.astype(jnp.int32)
    spare_col = spare_col.astype(jnp.int32)
    place_across = iota((slots, rows), 1) + 1
    part_down = (iota((slots, rows), 0) & (MAIN - 1)) >> 1
    return one_hot(place_across == main_col), [
        one_hot((place_across == spare_col) & (part_down == g)) for g in range(KV_HEADS)
    ]


def receive_kernel(recv_ref, kv_ref):
    r1t, r2t = across_maps(kv_ref.shape[0], *landing_rows(*landing_of(recv_ref[:, 5 * PAIR_WIDTH :])))
    spare = recv_ref[:, 4 * PAIR_WIDTH : 5 * PAIR_WIDTH]
    for g in range(KV_HEADS):
        columns = slice(g * PAIR_WIDTH, (g + 1) * PAIR_WIDTH)
        kv_ref[:, columns] = low(dot(r1t, recv_ref[:, columns]) + dot(r2t[g], spare))


def pack_queries_kernel(query_ref, grad_ref, m1_ref, m2_ref, send_ref):
    m1 = m1_ref[...]
    spare = jnp.zeros((send_ref.shape[0], BOTH_WIDTH), jnp.float32)
    for g in range(KV_HEADS):
        columns = slice(g * GROUP_WIDTH, (g + 1) * GROUP_WIDTH)
        part = jnp.concatenate([query_ref[:, columns], grad_ref[:, columns]], axis=1)
        send_ref[:, g * BOTH_WIDTH : (g + 1) * BOTH_WIDTH] = low(dot(m1, part))
        spare += dot(m2_ref[g], part)
    send_ref[:, KV_HEADS * BOTH_WIDTH :] = low(spare)


def pack_kernel(source_ref, landing_ref, send_ref):
    width = source_ref.shape[1] // KV_HEADS
    m1, m2 = down_maps(source_ref.shape[0], *landing_of(landing_ref[...]))
    spare = jnp.zeros((send_ref.shape[0], width), jnp.float32)
    for g in range(KV_HEADS):
        columns = slice(g * width, (g + 1) * width)
        part = low(source_ref[:, columns])
        send_ref[:, columns] = low(dot(m1, part))
        spare += dot(m2[g], part)
    send_ref[:, KV_HEADS * width :] = low(spare)


def unpack_queries_kernel(recv_ref, home_ref, attended_ref, grad_ref):
    m1, m2 = home_maps(home_ref, recv_ref.shape[0])
    spare = recv_ref[:, KV_HEADS * BOTH_WIDTH :]
    for g in range(KV_HEADS):
        part = recv_ref[:, g * BOTH_WIDTH : (g + 1) * BOTH_WIDTH]
        both = low(dot(m1, part) + dot(m2[g], spare))
        columns = slice(g * GROUP_WIDTH, (g + 1) * GROUP_WIDTH)
        attended_ref[:, columns] = both[:, :GROUP_WIDTH]
        grad_ref[:, columns] = both[:, GROUP_WIDTH:]


def unpack_kv_kernel(recv_ref, home_ref, key_ref, value_ref):
    m1, m2 = home_maps(home_ref, recv_ref.shape[0])
    spare = recv_ref[:, KV_HEADS * PAIR_WIDTH :]
    for g in range(KV_HEADS):
        both = low(
            dot(m1, recv_ref[:, g * PAIR_WIDTH : (g + 1) * PAIR_WIDTH]) + dot(m2[g], spare)
        )
        key_ref[:, g * HEAD_DIM : (g + 1) * HEAD_DIM] = both[:, :HEAD_DIM]
        value_ref[:, g * HEAD_DIM : (g + 1) * HEAD_DIM] = both[:, HEAD_DIM:]


def ends_of(info_ref):
    ends = [info_ref[0]]
    for k in range(1, 6):
        ends.append(ends[-1] + info_ref[k])
    return ends


def stack_heads(x):
    return jnp.concatenate(
        [x[:, h * HEAD_DIM : (h + 1) * HEAD_DIM] for h in range(GROUP)], axis=0
    )


def unstack_heads(x):
    rows = x.shape[0] // GROUP
    return jnp.concatenate([x[h * rows : (h + 1) * rows] for h in range(GROUP)], axis=1)


def attention_kernel(
    info_ref, weight_ref, recv_ref, key_ref, value_ref, landing_ref,
    kv_ref, send_ref, bias, spare_sum, value_ones, raised, dscore, score, dprob,
    held, ready, kv_own, r12, r1t, r2t, arrived, left, kv_left,
):
    step = pl.program_id(0)
    rows, keys = bias.shape
    count = len(score)
    steps = KV_HEADS // count

    main = KV_HEADS * BOTH_WIDTH
    slots = held.shape[0]

    def arrive(part):
        columns = pl.ds(main, BOTH_WIDTH)
        if part < steps:
            columns = pl.ds(part * count * BOTH_WIDTH, count * BOTH_WIDTH)
        return pltpu.make_async_copy(recv_ref.at[:, columns], held.at[:, columns], arrived.at[part])

    def leave(block):
        start = block * BOTH_WIDTH if isinstance(block, int) else pl.multiple_of(block * BOTH_WIDTH, BOTH_WIDTH)
        columns = pl.ds(start, BOTH_WIDTH)
        return pltpu.make_async_copy(ready.at[:, columns], send_ref.at[:, columns], left.at[block])

    def leave_kv(g):
        start = g * PAIR_WIDTH if isinstance(g, int) else pl.multiple_of(g * PAIR_WIDTH, PAIR_WIDTH)
        return pltpu.make_async_copy(
            kv_own.at[g], kv_ref.at[:, pl.ds(start, PAIR_WIDTH)], kv_left.at[g]
        )

    e0, e1, e2, e3, e4, _ = ends_of(info_ref)
    place = info_ref[6] * rows + iota((rows, 1), 0)
    rejected = (place >= e1) & (place < e2)

    @pl.when(step == 0)
    def _():
        for part in (steps, *range(steps)):
            arrive(part).start()
        first = jnp.where(place >= e2, e2, 0)
        hidden_from = jnp.where(place >= e4, e3, jnp.where(rejected, e0, 0))
        hidden_to = jnp.where(place >= e4, e4, jnp.where(rejected, e1, 0))
        other = iota((rows, keys), 1)
        seen = (other >= first) & (other <= place) & ((other < hidden_from) | (other >= hidden_to))
        bias[...] = jnp.where(seen, 0.0, MASKED)
        spare_sum[...] = jnp.zeros_like(spare_sum)
        landing = landing_of(landing_ref[...])
        r1, down = down_maps(rows, *landing)
        r1t[...], across = across_maps(rows, *landing_rows(*landing))
        for g in range(KV_HEADS):
            r12[g, :slots] = r1
            r12[g, slots:] = down[g]
            r2t[g] = across[g]
        for n in range(count):
            value_ones[n][:, HEAD_DIM:] = jnp.ones((keys, HEAD_DIM), jnp.bfloat16)
        arrive(steps).wait()

    for part in range(steps):

        @pl.when(step == part)
        def _():
            arrive(part).wait()

    weight = jnp.where(place >= e2, weight_ref[1], weight_ref[0])
    factor = jnp.where(rejected | (place >= e4), -weight, weight)
    query, cotangent, key, inverse, attended, delta = ([None] * count for _ in range(6))
    for n in range(count):
        columns = slice(n * HEAD_DIM, (n + 1) * HEAD_DIM)
        g = step * count + n
        start = pl.multiple_of(g * BOTH_WIDTH, BOTH_WIDTH)
        both = dot(r1t[...], held[:, pl.ds(start, BOTH_WIDTH)]) + dot(r2t[g], held[:, main:])
        query[n] = stack_heads(low(both[:, :GROUP_WIDTH]))
        cotangent[n] = stack_heads(low(factor * both[:, GROUP_WIDTH:]))
        key[n] = key_ref[:, columns]
        value_ones[n][:, :HEAD_DIM] = value_ref[:, columns]
    for n in range(count):
        score[n][...] = dot(query[n], key[n], ((1,), (1,)))
    for n in range(count):
        for h in range(GROUP):
            part = slice(h * rows, (h + 1) * rows)
            seen = score[n][part, :] + bias[...]
            highest = jnp.max(seen, axis=1, keepdims=True)
            raised[n][part, :] = low(jnp.exp2((seen - highest) * EXPONENT))
    for n in range(count):
        dprob[n][...] = dot(cotangent[n], value_ones[n][:, :HEAD_DIM], ((1,), (1,)))
    for n in range(count):
        summed = dot(raised[n][...], value_ones[n][...])
        inverse[n] = 1.0 / summed[:, HEAD_DIM:]
        attended[n] = low(summed[:, :HEAD_DIM] * inverse[n])
        delta[n] = jnp.sum(
            cotangent[n].astype(jnp.float32) * attended[n].astype(jnp.float32),
            axis=1,
            keepdims=True,
        )
    for n in range(count):
        dscore[n][...] = raised[n][...] * low(dprob[n][...] - delta[n])
    for n in range(count):
        g = step * count + n
        scaled = inverse[n] * SCALING
        query_low = low(query[n].astype(jnp.float32) * scaled)
        cotangent_low = low(cotangent[n].astype(jnp.float32) * inverse[n])
        kv_own[g, :, :HEAD_DIM] = low(dot(query_low.T, dscore[n][...])).T
        kv_own[g, :, HEAD_DIM:] = low(dot(cotangent_low.T, raised[n][...])).T
        leave_kv(g).start()
        query_grad = low(dot(dscore[n][...], key[n]) * scaled)
        both = jnp.concatenate([unstack_heads(attended[n]), unstack_heads(query_grad)], axis=1)
        placed = dot(r12[g], both)
        ready[:, pl.ds(pl.multiple_of(g * BOTH_WIDTH, BOTH_WIDTH), BOTH_WIDTH)] = low(placed[:slots])
        leave(g).start()
        spare_sum[...] += placed[slots:]

    @pl.when(step == steps - 1)
    def _():
        ready[:, main:] = low(spare_sum[...])
        leave(KV_HEADS).start()
        for block in range(KV_HEADS):
            leave(block).wait()
            leave_kv(block).wait()
        leave(KV_HEADS).wait()


def shape(dims, kind=jnp.bfloat16):
    return jax.ShapeDtypeStruct(dims, kind)


def cost(flops, moved, exps=0):
    return pl.CostEstimate(flops=int(flops), bytes_accessed=int(moved), transcendentals=int(exps))


def body(queries, keys, values, out_grad, pair_weight, lengths, route_dest, route_slot):
    rows = queries.shape[0]
    ranks = lax.axis_size("dp")
    packs = lax.axis_size("pack")
    seq = rows * packs
    slots = ranks * MAIN
    wide = (KV_HEADS + 1) * BOTH_WIDTH
    narrow = (KV_HEADS + 1) * PAIR_WIDTH
    fence = lax.optimization_barrier

    def exchange(block):
        moved = lax.all_to_all(
            block.reshape(ranks, MAIN, block.shape[1]), "dp", split_axis=0, concat_axis=0, tiled=True
        )
        return moved.reshape(block.shape)

    down = (shape((slots, rows)), shape((KV_HEADS, slots, rows)))
    dest = route_dest.reshape(1, rows)

    kv_send, p1, p2 = pl.pallas_call(
        send_kernel,
        out_shape=(shape((slots, narrow + HEAD_DIM)), *down),
        compiler_params=compiler_params(),
        cost_estimate=cost(4 * slots * rows * 2 * KV_WIDTH, 6 * slots * 2 * KV_WIDTH),
    )(dest, route_slot.reshape(1, rows), keys, values)

    kv_recv = exchange(kv_send)
    home = pl.pallas_call(
        home_kernel,
        out_shape=shape((rows, HEAD_DIM), jnp.int32),
        compiler_params=compiler_params(),
        cost_estimate=cost(LONG, 6 * slots * rows),
    )(dest)
    query_send = pl.pallas_call(
        pack_queries_kernel,
        out_shape=shape((slots, wide)),
        compiler_params=compiler_params(),
        cost_estimate=cost(LONG, 10 * slots * QUERY_WIDTH),
    )(queries, out_grad, p1, p2)
    info = jnp.concatenate(
        [lengths.reshape(6), lax.axis_index("pack").astype(jnp.int32).reshape(1)]
    )
    kv_recv, query_send, home, info = fence((kv_recv, query_send, home, info))

    kv_own = pl.pallas_call(
        receive_kernel,
        out_shape=shape((rows, 2 * KV_WIDTH)),
        compiler_params=compiler_params(SMALL_VMEM),
        cost_estimate=cost(4 * slots * rows * 2 * KV_WIDTH, 6 * slots * 2 * KV_WIDTH),
    )(kv_recv)
    kv_all = lax.all_gather(kv_own, "pack", axis=0, tiled=True)
    query_send, kv_own = fence((query_send, kv_own))
    query_recv = exchange(query_send)

    smem = pl.BlockSpec(memory_space=pltpu.SMEM)
    anywhere = pl.BlockSpec(memory_space=pl.ANY)
    at_once = 2
    landing_spec = pl.BlockSpec((slots, HEAD_DIM), lambda g: (0, narrow // HEAD_DIM))
    steps = KV_HEADS // at_once
    work = HEADS * rows * seq * HEAD_DIM

    def several(dims, kind=jnp.bfloat16):
        return [pltpu.VMEM(dims, kind)] * at_once

    kv_part, back_send = pl.pallas_call(
        attention_kernel,
        grid=(steps,),
        in_specs=[
            smem,
            smem,
            anywhere,
            pl.BlockSpec((seq, at_once * HEAD_DIM), lambda g: (0, g)),
            pl.BlockSpec((seq, at_once * HEAD_DIM), lambda g: (0, steps + g)),
            landing_spec,
        ],
        out_specs=(
            anywhere,
            anywhere,
        ),
        out_shape=(shape((seq, 2 * KV_WIDTH)), shape((slots, wide))),
        scratch_shapes=[
            pltpu.VMEM((rows, seq), jnp.float32),
            pltpu.VMEM((slots, BOTH_WIDTH), jnp.float32),
            several((seq, PAIR_WIDTH)),
            several((GROUP * rows, seq)),
            several((GROUP * rows, seq)),
            several((GROUP * rows, seq), jnp.float32),
            several((GROUP * rows, seq), jnp.float32),
            pltpu.VMEM((slots, wide), jnp.bfloat16),
            pltpu.VMEM((slots, wide), jnp.bfloat16),
            pltpu.VMEM((KV_HEADS, seq, PAIR_WIDTH), jnp.bfloat16),
            pltpu.VMEM((KV_HEADS, 2 * slots, rows), jnp.bfloat16),
            pltpu.VMEM((rows, slots), jnp.bfloat16),
            pltpu.VMEM((KV_HEADS, rows, slots), jnp.bfloat16),
            pltpu.SemaphoreType.DMA((steps + 1,)),
            pltpu.SemaphoreType.DMA((KV_HEADS + 1,)),
            pltpu.SemaphoreType.DMA((KV_HEADS,)),
        ],
        compiler_params=compiler_params(dimension_semantics=("arbitrary",)),
        cost_estimate=cost(12 * work, 2 * HEADS * rows * seq, HEADS * rows * seq),
    )(
        info, pair_weight.reshape(2), query_recv, kv_all, kv_all, kv_recv,
    )

    back_recv = exchange(back_send)
    kv_grad = lax.psum_scatter(kv_part, "pack", scatter_dimension=0, tiled=True)
    kv_grad_send = pl.pallas_call(
        pack_kernel,
        grid=(1,),
        in_specs=[pl.BlockSpec((rows, 2 * KV_WIDTH), lambda i: (0, 0)), landing_spec],
        out_specs=pl.BlockSpec((slots, narrow), lambda i: (0, 0)),
        out_shape=shape((slots, narrow)),
        compiler_params=compiler_params(),
        cost_estimate=cost(4 * slots * rows * 2 * KV_WIDTH, 10 * slots * KV_WIDTH),
    )(kv_grad, kv_recv)
    back_recv, kv_grad_send = fence((back_recv, kv_grad_send))
    kv_back = exchange(kv_grad_send)
    attended, query_grad = pl.pallas_call(
        unpack_queries_kernel,
        out_shape=(shape((rows, QUERY_WIDTH)), shape((rows, QUERY_WIDTH))),
        compiler_params=compiler_params(SMALL_VMEM),
        cost_estimate=cost(LONG, 10 * slots * QUERY_WIDTH),
    )(back_recv, home)
    key_grad, value_grad = pl.pallas_call(
        unpack_kv_kernel,
        out_shape=(shape((rows, KV_WIDTH)), shape((rows, KV_WIDTH))),
        compiler_params=compiler_params(SMALL_VMEM),
        cost_estimate=cost(4 * slots * rows * 2 * KV_WIDTH, 4 * slots * 2 * KV_WIDTH),
    )(kv_back, home)
    return attended, query_grad, key_grad, value_grad


def solution(mesh):
    rows = P(("dp", "pack"), None)
    flat = P(("dp", "pack"))
    return jax.shard_map(
        body,
        mesh=mesh,
        in_specs=(rows, rows, rows, rows, P("dp", None), P("dp", None, None), flat, flat),
        out_specs=(rows, rows, rows, rows),
        check_vma=False,
    )
```

```python
import functools
import math

import jax
import jax.numpy as jnp
from jax import lax
from jax.experimental import pallas as pl
from jax.experimental.pallas import tpu as pltpu
from jax.sharding import PartitionSpec as P

HEAD_DIM = 128
HEADS = 20
KV_HEADS = 4
GROUP = 5
CAP = 10
MAIN = 8
SPARE = CAP - MAIN

QUERY_WIDTH = HEADS * HEAD_DIM
KV_WIDTH = KV_HEADS * HEAD_DIM
GROUP_WIDTH = GROUP * HEAD_DIM
PAIR_WIDTH = 2 * HEAD_DIM
SCALING = HEAD_DIM ** (-0.5)
EXPONENT = SCALING * math.log2(math.e)
MASKED = -1e30
VMEM_LIMIT = 60 * 1024 * 1024
SMALL_VMEM = 16 * 1024 * 1024
BOTH_WIDTH = 2 * GROUP_WIDTH
LONG = 10**11


def dot(left, right, contract=((1,), (0,))):
    return lax.dot_general(left, right, (contract, ((), ())), preferred_element_type=jnp.float32)


def low(x):
    return x.astype(jnp.bfloat16)


def iota(shape, dim):
    return lax.broadcasted_iota(jnp.int32, shape, dim)


def one_hot(condition):
    return jnp.where(condition, 1.0, 0.0).astype(jnp.bfloat16)


def compiler_params(limit=VMEM_LIMIT, **extra):
    return pltpu.CompilerParams(vmem_limit_bytes=limit, **extra)


def ranks_of(dest_row):
    rows = dest_row.shape[1]
    down = iota((rows, rows), 0)
    across = iota((rows, rows), 1)
    dest_col = jnp.sum(
        jnp.where(down == across, dest_row.astype(jnp.float32), 0.0), axis=1, keepdims=True
    ).astype(jnp.int32)
    return dest_col, dest_col == dest_row, down, across


def places_of(dest, rank):
    rank = rank.astype(jnp.int32)
    first = dest * MAIN + rank
    return jnp.where(rank < MAIN, first, -MAIN), jnp.where(rank < MAIN, -MAIN, first - MAIN)


def send_kernel(dest_ref, slot_ref, keys_ref, values_ref, send_ref, p1_ref, p2_ref):
    rows = keys_ref.shape[0]
    slots = send_ref.shape[0]
    dest_row = dest_ref[...]
    _, same, down, across = ranks_of(dest_row)
    rank_row = jnp.sum(jnp.where(same & (down < across), 1.0, 0.0), axis=0, keepdims=True)
    main_row, spare_row = places_of(dest_row, rank_row)
    slot_down = iota((slots, rows), 0)
    p1 = slot_down == main_row
    p1_low = one_hot(p1)
    p1_ref[...] = p1_low
    place = (slot_ref[...] + 1).astype(jnp.float32)
    place_main = jnp.sum(jnp.where(p1, place, 0.0), axis=1, keepdims=True)
    taken = jnp.zeros((slots, rows), jnp.float32)
    spare = jnp.zeros((slots, PAIR_WIDTH), jnp.float32)
    for g in range(KV_HEADS):
        p2 = slot_down == spare_row + SPARE * g
        p2_low = one_hot(p2)
        p2_ref[g] = p2_low
        taken += jnp.where(p2, place, 0.0)
        source = keys_ref if g < 2 else values_ref
        columns = source[:, (g % 2) * PAIR_WIDTH : (g % 2 + 1) * PAIR_WIDTH]
        send_ref[:, g * PAIR_WIDTH : (g + 1) * PAIR_WIDTH] = low(dot(p1_low, columns))
        spare += dot(p2_low, columns)
    place_spare = jnp.sum(taken, axis=1, keepdims=True)
    send_ref[:, 4 * PAIR_WIDTH : 5 * PAIR_WIDTH] = low(spare)
    lane = iota((slots, HEAD_DIM), 1)
    send_ref[:, 5 * PAIR_WIDTH :] = low(
        jnp.where(lane == 0, place_main, jnp.where(lane == 1, place_spare, 0.0))
    )


def home_kernel(dest_ref, home_ref):
    dest_col, same, down, across = ranks_of(dest_ref[...])
    rank_col = jnp.sum(jnp.where(same & (across < down), 1.0, 0.0), axis=1, keepdims=True)
    main_col, spare_col = places_of(dest_col, rank_col)
    lane = iota(home_ref.shape, 1)
    home_ref[...] = jnp.where(lane == 0, main_col, spare_col)


def home_maps(home_ref, slots):
    rows = home_ref.shape[0]
    slot_across = iota((rows, slots), 1)
    spare_col = home_ref[:, 1:2]
    return one_hot(slot_across == home_ref[:, :1]), [
        one_hot(slot_across == spare_col + SPARE * g) for g in range(KV_HEADS)
    ]


def landing_of(tile):
    slots = tile.shape[0]
    tile = tile.astype(jnp.float32)
    lane = iota((slots, HEAD_DIM), 1)
    main_col = jnp.sum(jnp.where(lane == 0, tile, 0.0), axis=1, keepdims=True)
    spare_col = jnp.sum(jnp.where(lane == 1, tile, 0.0), axis=1, keepdims=True)
    return main_col, spare_col


def landing_rows(main_col, spare_col):
    slots = main_col.shape[0]
    diagonal = iota((slots, slots), 0) == iota((slots, slots), 1)
    return (
        jnp.sum(jnp.where(diagonal, main_col, 0.0), axis=0, keepdims=True).astype(jnp.int32),
        jnp.sum(jnp.where(diagonal, spare_col, 0.0), axis=0, keepdims=True).astype(jnp.int32),
    )


def across_maps(rows, main_row, spare_row):
    slots = main_row.shape[1]
    place_down = iota((rows, slots), 0) + 1
    part_across = (iota((rows, slots), 1) & (MAIN - 1)) >> 1
    return one_hot(place_down == main_row), [
        one_hot((place_down == spare_row) & (part_across == g)) for g in range(KV_HEADS)
    ]


def down_maps(rows, main_col, spare_col):
    slots = main_col.shape[0]
    main_col = main_col.astype(jnp.int32)
    spare_col = spare_col.astype(jnp.int32)
    place_across = iota((slots, rows), 1) + 1
    part_down = (iota((slots, rows), 0) & (MAIN - 1)) >> 1
    return one_hot(place_across == main_col), [
        one_hot((place_across == spare_col) & (part_down == g)) for g in range(KV_HEADS)
    ]


def receive_kernel(recv_ref, kv_ref):
    r1t, r2t = across_maps(kv_ref.shape[0], *landing_rows(*landing_of(recv_ref[:, 5 * PAIR_WIDTH :])))
    spare = recv_ref[:, 4 * PAIR_WIDTH : 5 * PAIR_WIDTH]
    for g in range(KV_HEADS):
        columns = slice(g * PAIR_WIDTH, (g + 1) * PAIR_WIDTH)
        kv_ref[:, columns] = low(dot(r1t, recv_ref[:, columns]) + dot(r2t[g], spare))


def pack_queries_kernel(query_ref, grad_ref, m1_ref, m2_ref, send_ref):
    m1 = m1_ref[...]
    spare = jnp.zeros((send_ref.shape[0], BOTH_WIDTH), jnp.float32)
    for g in range(KV_HEADS):
        columns = slice(g * GROUP_WIDTH, (g + 1) * GROUP_WIDTH)
        part = jnp.concatenate([query_ref[:, columns], grad_ref[:, columns]], axis=1)
        send_ref[:, g * BOTH_WIDTH : (g + 1) * BOTH_WIDTH] = low(dot(m1, part))
        spare += dot(m2_ref[g], part)
    send_ref[:, KV_HEADS * BOTH_WIDTH :] = low(spare)


def pack_kernel(source_ref, landing_ref, send_ref):
    width = source_ref.shape[1] // KV_HEADS
    m1, m2 = down_maps(source_ref.shape[0], *landing_of(landing_ref[...]))
    spare = jnp.zeros((send_ref.shape[0], width), jnp.float32)
    for g in range(KV_HEADS):
        columns = slice(g * width, (g + 1) * width)
        part = low(source_ref[:, columns])
        send_ref[:, columns] = low(dot(m1, part))
        spare += dot(m2[g], part)
    send_ref[:, KV_HEADS * width :] = low(spare)


def unpack_queries_kernel(recv_ref, home_ref, attended_ref, grad_ref):
    m1, m2 = home_maps(home_ref, recv_ref.shape[0])
    spare = recv_ref[:, KV_HEADS * BOTH_WIDTH :]
    for g in range(KV_HEADS):
        part = recv_ref[:, g * BOTH_WIDTH : (g + 1) * BOTH_WIDTH]
        both = low(dot(m1, part) + dot(m2[g], spare))
        columns = slice(g * GROUP_WIDTH, (g + 1) * GROUP_WIDTH)
        attended_ref[:, columns] = both[:, :GROUP_WIDTH]
        grad_ref[:, columns] = both[:, GROUP_WIDTH:]


def unpack_kv_kernel(recv_ref, home_ref, key_ref, value_ref):
    m1, m2 = home_maps(home_ref, recv_ref.shape[0])
    spare = recv_ref[:, KV_HEADS * PAIR_WIDTH :]
    for g in range(KV_HEADS):
        both = low(
            dot(m1, recv_ref[:, g * PAIR_WIDTH : (g + 1) * PAIR_WIDTH]) + dot(m2[g], spare)
        )
        key_ref[:, g * HEAD_DIM : (g + 1) * HEAD_DIM] = both[:, :HEAD_DIM]
        value_ref[:, g * HEAD_DIM : (g + 1) * HEAD_DIM] = both[:, HEAD_DIM:]


def ends_of(info_ref):
    ends = [info_ref[0]]
    for k in range(1, 6):
        ends.append(ends[-1] + info_ref[k])
    return ends


def stack_heads(x):
    return jnp.concatenate(
        [x[:, h * HEAD_DIM : (h + 1) * HEAD_DIM] for h in range(GROUP)], axis=0
    )


def unstack_heads(x):
    rows = x.shape[0] // GROUP
    return jnp.concatenate([x[h * rows : (h + 1) * rows] for h in range(GROUP)], axis=1)


def attention_kernel(
    info_ref, weight_ref, main_ref, spare_ref, key_ref, value_ref, landing_ref,
    kv_ref, send_ref, bias, spare_sum, value_ones, raised, dscore, score, dprob, r12, r1t, r2t,
):
    step = pl.program_id(0)
    rows, keys = bias.shape
    count = len(score)
    slots = main_ref.shape[0]
    e0, e1, e2, e3, e4, _ = ends_of(info_ref)
    place = info_ref[6] * rows + iota((rows, 1), 0)
    rejected = (place >= e1) & (place < e2)

    @pl.when(step == 0)
    def _():
        first = jnp.where(place >= e2, e2, 0)
        hidden_from = jnp.where(place >= e4, e3, jnp.where(rejected, e0, 0))
        hidden_to = jnp.where(place >= e4, e4, jnp.where(rejected, e1, 0))
        other = iota((rows, keys), 1)
        seen = (other >= first) & (other <= place) & ((other < hidden_from) | (other >= hidden_to))
        bias[...] = jnp.where(seen, 0.0, MASKED)
        spare_sum[...] = jnp.zeros_like(spare_sum)
        landing = landing_of(landing_ref[...])
        r1, down = down_maps(rows, *landing)
        r1t[...], across = across_maps(rows, *landing_rows(*landing))
        for g in range(KV_HEADS):
            r12[g, :slots] = r1
            r12[g, slots:] = down[g]
            r2t[g] = across[g]
        for n in range(count):
            value_ones[n][:, HEAD_DIM:] = jnp.ones((keys, HEAD_DIM), jnp.bfloat16)

    weight = jnp.where(place >= e2, weight_ref[1], weight_ref[0])
    factor = jnp.where(rejected | (place >= e4), -weight, weight)
    query, cotangent, key, inverse, attended, delta = ([None] * count for _ in range(6))
    for n in range(count):
        columns = slice(n * HEAD_DIM, (n + 1) * HEAD_DIM)
        both = dot(r1t[...], main_ref[:, n * BOTH_WIDTH : (n + 1) * BOTH_WIDTH]) + dot(
            r2t[step * count + n], spare_ref[...]
        )
        query[n] = stack_heads(low(both[:, :GROUP_WIDTH]))
        cotangent[n] = stack_heads(low(factor * both[:, GROUP_WIDTH:]))
        key[n] = key_ref[:, columns]
        value_ones[n][:, :HEAD_DIM] = value_ref[:, columns]
    for n in range(count):
        score[n][...] = dot(query[n], key[n], ((1,), (1,)))
    for n in range(count):
        for h in range(GROUP):
            part = slice(h * rows, (h + 1) * rows)
            seen = score[n][part, :] + bias[...]
            highest = jnp.max(seen, axis=1, keepdims=True)
            raised[n][part, :] = low(jnp.exp2((seen - highest) * EXPONENT))
    for n in range(count):
        dprob[n][...] = dot(cotangent[n], value_ones[n][:, :HEAD_DIM], ((1,), (1,)))
    for n in range(count):
        summed = dot(raised[n][...], value_ones[n][...])
        inverse[n] = 1.0 / summed[:, HEAD_DIM:]
        attended[n] = low(summed[:, :HEAD_DIM] * inverse[n])
        delta[n] = jnp.sum(
            cotangent[n].astype(jnp.float32) * attended[n].astype(jnp.float32),
            axis=1,
            keepdims=True,
        )
    for n in range(count):
        dscore[n][...] = raised[n][...] * low(dprob[n][...] - delta[n])
    for n in range(count):
        scaled = inverse[n] * SCALING
        query_grad = low(dot(dscore[n][...], key[n]) * scaled)
        query_low = low(query[n].astype(jnp.float32) * scaled)
        cotangent_low = low(cotangent[n].astype(jnp.float32) * inverse[n])
        first = n * PAIR_WIDTH
        kv_ref[:, first : first + HEAD_DIM] = low(dot(query_low.T, dscore[n][...])).T
        kv_ref[:, first + HEAD_DIM : first + PAIR_WIDTH] = low(dot(cotangent_low.T, raised[n][...])).T
        both = jnp.concatenate([unstack_heads(attended[n]), unstack_heads(query_grad)], axis=1)
        start = pl.multiple_of((step * count + n) * BOTH_WIDTH, BOTH_WIDTH)
        placed = dot(r12[step * count + n], both)
        send_ref[:, pl.ds(start, BOTH_WIDTH)] = low(placed[:slots])
        spare_sum[...] += placed[slots:]

    @pl.when(step == KV_HEADS // count - 1)
    def _():
        send_ref[:, KV_HEADS * BOTH_WIDTH :] = low(spare_sum[...])


def shape(dims, kind=jnp.bfloat16):
    return jax.ShapeDtypeStruct(dims, kind)


def cost(flops, moved, exps=0):
    return pl.CostEstimate(flops=int(flops), bytes_accessed=int(moved), transcendentals=int(exps))


def body(queries, keys, values, out_grad, pair_weight, lengths, route_dest, route_slot):
    rows = queries.shape[0]
    ranks = lax.axis_size("dp")
    packs = lax.axis_size("pack")
    seq = rows * packs
    slots = ranks * MAIN
    wide = (KV_HEADS + 1) * BOTH_WIDTH
    narrow = (KV_HEADS + 1) * PAIR_WIDTH
    fence = lax.optimization_barrier

    def exchange(block):
        moved = lax.all_to_all(
            block.reshape(ranks, MAIN, block.shape[1]), "dp", split_axis=0, concat_axis=0, tiled=True
        )
        return moved.reshape(block.shape)

    down = (shape((slots, rows)), shape((KV_HEADS, slots, rows)))
    dest = route_dest.reshape(1, rows)

    kv_send, p1, p2 = pl.pallas_call(
        send_kernel,
        out_shape=(shape((slots, narrow + HEAD_DIM)), *down),
        compiler_params=compiler_params(),
        cost_estimate=cost(4 * slots * rows * 2 * KV_WIDTH, 6 * slots * 2 * KV_WIDTH),
    )(dest, route_slot.reshape(1, rows), keys, values)

    kv_recv = exchange(kv_send)
    home = pl.pallas_call(
        home_kernel,
        out_shape=shape((rows, HEAD_DIM), jnp.int32),
        compiler_params=compiler_params(),
        cost_estimate=cost(LONG, 6 * slots * rows),
    )(dest)
    query_send = pl.pallas_call(
        pack_queries_kernel,
        out_shape=shape((slots, wide)),
        compiler_params=compiler_params(),
        cost_estimate=cost(LONG, 10 * slots * QUERY_WIDTH),
    )(queries, out_grad, p1, p2)
    info = jnp.concatenate(
        [lengths.reshape(6), lax.axis_index("pack").astype(jnp.int32).reshape(1)]
    )
    kv_recv, query_send, home, info = fence((kv_recv, query_send, home, info))

    kv_own = pl.pallas_call(
        receive_kernel,
        out_shape=shape((rows, 2 * KV_WIDTH)),
        compiler_params=compiler_params(SMALL_VMEM),
        cost_estimate=cost(4 * slots * rows * 2 * KV_WIDTH, 6 * slots * 2 * KV_WIDTH),
    )(kv_recv)
    kv_all = lax.all_gather(kv_own, "pack", axis=0, tiled=True)
    query_send, kv_own = fence((query_send, kv_own))
    query_recv = exchange(query_send)

    smem = pl.BlockSpec(memory_space=pltpu.SMEM)
    at_once = 2
    landing_spec = pl.BlockSpec((slots, HEAD_DIM), lambda g: (0, narrow // HEAD_DIM))
    steps = KV_HEADS // at_once
    work = HEADS * rows * seq * HEAD_DIM

    def several(dims, kind=jnp.bfloat16):
        return [pltpu.VMEM(dims, kind)] * at_once

    kv_part, back_send = pl.pallas_call(
        attention_kernel,
        grid=(steps,),
        in_specs=[
            smem,
            smem,
            pl.BlockSpec((slots, at_once * BOTH_WIDTH), lambda g: (0, g)),
            pl.BlockSpec((slots, BOTH_WIDTH), lambda g: (0, KV_HEADS)),
            pl.BlockSpec((seq, at_once * HEAD_DIM), lambda g: (0, g)),
            pl.BlockSpec((seq, at_once * HEAD_DIM), lambda g: (0, steps + g)),
            landing_spec,
        ],
        out_specs=(
            pl.BlockSpec((seq, at_once * PAIR_WIDTH), lambda g: (0, g)),
            pl.BlockSpec((slots, wide), lambda g: (0, 0)),
        ),
        out_shape=(shape((seq, 2 * KV_WIDTH)), shape((slots, wide))),
        scratch_shapes=[
            pltpu.VMEM((rows, seq), jnp.float32),
            pltpu.VMEM((slots, BOTH_WIDTH), jnp.float32),
            several((seq, PAIR_WIDTH)),
            several((GROUP * rows, seq)),
            several((GROUP * rows, seq)),
            several((GROUP * rows, seq), jnp.float32),
            several((GROUP * rows, seq), jnp.float32),
            pltpu.VMEM((KV_HEADS, 2 * slots, rows), jnp.bfloat16),
            pltpu.VMEM((rows, slots), jnp.bfloat16),
            pltpu.VMEM((KV_HEADS, rows, slots), jnp.bfloat16),
        ],
        compiler_params=compiler_params(dimension_semantics=("arbitrary",)),
        cost_estimate=cost(12 * work, 2 * HEADS * rows * seq, HEADS * rows * seq),
    )(
        info, pair_weight.reshape(2), query_recv, query_recv, kv_all, kv_all, kv_recv,
    )

    back_recv = exchange(back_send)
    kv_grad = lax.psum_scatter(kv_part, "pack", scatter_dimension=0, tiled=True)
    kv_grad_send = pl.pallas_call(
        pack_kernel,
        grid=(1,),
        in_specs=[pl.BlockSpec((rows, 2 * KV_WIDTH), lambda i: (0, 0)), landing_spec],
        out_specs=pl.BlockSpec((slots, narrow), lambda i: (0, 0)),
        out_shape=shape((slots, narrow)),
        compiler_params=compiler_params(),
        cost_estimate=cost(4 * slots * rows * 2 * KV_WIDTH, 10 * slots * KV_WIDTH),
    )(kv_grad, kv_recv)
    back_recv, kv_grad_send = fence((back_recv, kv_grad_send))
    kv_back = exchange(kv_grad_send)
    attended, query_grad = pl.pallas_call(
        unpack_queries_kernel,
        out_shape=(shape((rows, QUERY_WIDTH)), shape((rows, QUERY_WIDTH))),
        compiler_params=compiler_params(SMALL_VMEM),
        cost_estimate=cost(LONG, 10 * slots * QUERY_WIDTH),
    )(back_recv, home)
    key_grad, value_grad = pl.pallas_call(
        unpack_kv_kernel,
        out_shape=(shape((rows, KV_WIDTH)), shape((rows, KV_WIDTH))),
        compiler_params=compiler_params(SMALL_VMEM),
        cost_estimate=cost(4 * slots * rows * 2 * KV_WIDTH, 4 * slots * 2 * KV_WIDTH),
    )(kv_back, home)
    return attended, query_grad, key_grad, value_grad


def solution(mesh):
    rows = P(("dp", "pack"), None)
    flat = P(("dp", "pack"))
    return jax.shard_map(
        body,
        mesh=mesh,
        in_specs=(rows, rows, rows, rows, P("dp", None), P("dp", None, None), flat, flat),
        out_specs=(rows, rows, rows, rows),
        check_vma=False,
    )
```

```python
import functools
import math

import jax
import jax.numpy as jnp
from jax import lax
from jax.experimental import pallas as pl
from jax.experimental.pallas import tpu as pltpu
from jax.sharding import PartitionSpec as P

HEAD_DIM = 128
HEADS = 20
KV_HEADS = 4
GROUP = 5
CAP = 10
MAIN = 8
SPARE = CAP - MAIN

QUERY_WIDTH = HEADS * HEAD_DIM
KV_WIDTH = KV_HEADS * HEAD_DIM
GROUP_WIDTH = GROUP * HEAD_DIM
PAIR_WIDTH = 2 * HEAD_DIM
SCALING = HEAD_DIM ** (-0.5)
EXPONENT = SCALING * math.log2(math.e)
MASKED = -1e30
VMEM_LIMIT = 60 * 1024 * 1024
SMALL_VMEM = 16 * 1024 * 1024
BOTH_WIDTH = 2 * GROUP_WIDTH
LONG = 10**11


def dot(left, right, contract=((1,), (0,))):
    return lax.dot_general(left, right, (contract, ((), ())), preferred_element_type=jnp.float32)


def low(x):
    return x.astype(jnp.bfloat16)


def iota(shape, dim):
    return lax.broadcasted_iota(jnp.int32, shape, dim)


def one_hot(condition):
    return jnp.where(condition, 1.0, 0.0).astype(jnp.bfloat16)


def compiler_params(limit=VMEM_LIMIT, **extra):
    return pltpu.CompilerParams(vmem_limit_bytes=limit, **extra)


def ranks_of(dest_row):
    rows = dest_row.shape[1]
    down = iota((rows, rows), 0)
    across = iota((rows, rows), 1)
    dest_col = jnp.sum(
        jnp.where(down == across, dest_row.astype(jnp.float32), 0.0), axis=1, keepdims=True
    ).astype(jnp.int32)
    return dest_col, dest_col == dest_row, down, across


def places_of(dest, rank):
    rank = rank.astype(jnp.int32)
    first = dest * MAIN + rank
    return jnp.where(rank < MAIN, first, -MAIN), jnp.where(rank < MAIN, -MAIN, first - MAIN)


def home_places(dest_ref):
    dest_row = dest_ref[...]
    _, same, down, across = ranks_of(dest_row)
    rank_row = jnp.sum(jnp.where(same & (down < across), 1.0, 0.0), axis=0, keepdims=True)
    return places_of(dest_row, rank_row)


def send_kernel(dest_ref, slot_ref, keys_ref, values_ref, send_ref):
    rows = keys_ref.shape[0]
    slots = send_ref.shape[0]
    main_row, spare_row = home_places(dest_ref)
    slot_down = iota((slots, rows), 0)
    p1 = one_hot(slot_down == main_row)
    taken = jnp.zeros((slots, rows), jnp.bfloat16)
    spare = jnp.zeros((slots, PAIR_WIDTH), jnp.float32)
    for g in range(KV_HEADS):
        p2 = one_hot(slot_down == spare_row + SPARE * g)
        taken += p2
        source = keys_ref if g < 2 else values_ref
        columns = source[:, (g % 2) * PAIR_WIDTH : (g % 2 + 1) * PAIR_WIDTH]
        send_ref[:, g * PAIR_WIDTH : (g + 1) * PAIR_WIDTH] = low(dot(p1, columns))
        spare += dot(p2, columns)
    send_ref[:, 4 * PAIR_WIDTH : 5 * PAIR_WIDTH] = low(spare)
    place = (slot_ref[...] + 1).astype(jnp.float32)
    line = iota((HEAD_DIM, rows), 0)
    in_main = low(jnp.where(line == 0, place, 0.0))
    in_spare = low(jnp.where(line == 1, place, 0.0))
    send_ref[:, 5 * PAIR_WIDTH :] = low(
        dot(p1, in_main, ((1,), (1,))) + dot(taken, in_spare, ((1,), (1,)))
    )


def home_kernel(dest_ref, home_ref):
    dest_col, same, down, across = ranks_of(dest_ref[...])
    rank_col = jnp.sum(jnp.where(same & (across < down), 1.0, 0.0), axis=1, keepdims=True)
    main_col, spare_col = places_of(dest_col, rank_col)
    lane = iota(home_ref.shape, 1)
    home_ref[...] = jnp.where(lane == 0, main_col, spare_col)


def home_maps(home_ref, slots):
    rows = home_ref.shape[0]
    slot_across = iota((rows, slots), 1)
    spare_col = home_ref[:, 1:2]
    return one_hot(slot_across == home_ref[:, :1]), [
        one_hot(slot_across == spare_col + SPARE * g) for g in range(KV_HEADS)
    ]


def landing_of(tile):
    slots = tile.shape[0]
    tile = tile.astype(jnp.float32)
    lane = iota((slots, HEAD_DIM), 1)
    main_col = jnp.sum(jnp.where(lane == 0, tile, 0.0), axis=1, keepdims=True)
    spare_col = jnp.sum(jnp.where(lane == 1, tile, 0.0), axis=1, keepdims=True)
    return main_col, spare_col


def landing_rows(tile):
    pick = one_hot(iota((8, HEAD_DIM), 0) == iota((8, HEAD_DIM), 1))
    both = dot(pick, tile, ((1,), (1,))).astype(jnp.int32)
    return both[:1, :], both[1:2, :]


def across_maps(rows, main_row, spare_row):
    slots = main_row.shape[1]
    place_down = iota((rows, slots), 0) + 1
    part_across = (iota((rows, slots), 1) & (MAIN - 1)) >> 1
    return one_hot(place_down == main_row), [
        one_hot((place_down == spare_row) & (part_across == g)) for g in range(KV_HEADS)
    ]


def down_maps(rows, main_col, spare_col):
    slots = main_col.shape[0]
    main_col = main_col.astype(jnp.int32)
    spare_col = spare_col.astype(jnp.int32)
    place_across = iota((slots, rows), 1) + 1
    part_down = (iota((slots, rows), 0) & (MAIN - 1)) >> 1
    return one_hot(place_across == main_col), [
        one_hot((place_across == spare_col) & (part_down == g)) for g in range(KV_HEADS)
    ]


def receive_kernel(recv_ref, kv_ref):
    r1t, r2t = across_maps(kv_ref.shape[0], *landing_rows(recv_ref[:, 5 * PAIR_WIDTH :]))
    spare = recv_ref[:, 4 * PAIR_WIDTH : 5 * PAIR_WIDTH]
    for g in range(KV_HEADS):
        columns = slice(g * PAIR_WIDTH, (g + 1) * PAIR_WIDTH)
        kv_ref[:, columns] = low(dot(r1t, recv_ref[:, columns]) + dot(r2t[g], spare))


def pack_queries_kernel(dest_ref, query_ref, grad_ref, send_ref):
    slot_down = iota((send_ref.shape[0], query_ref.shape[0]), 0)
    main_row, spare_row = home_places(dest_ref)
    m1 = one_hot(slot_down == main_row)
    spare = jnp.zeros((send_ref.shape[0], BOTH_WIDTH), jnp.float32)
    for g in range(KV_HEADS):
        columns = slice(g * GROUP_WIDTH, (g + 1) * GROUP_WIDTH)
        part = jnp.concatenate([query_ref[:, columns], grad_ref[:, columns]], axis=1)
        send_ref[:, g * BOTH_WIDTH : (g + 1) * BOTH_WIDTH] = low(dot(m1, part))
        spare += dot(one_hot(slot_down == spare_row + SPARE * g), part)
    send_ref[:, KV_HEADS * BOTH_WIDTH :] = low(spare)


def pack_kernel(source_ref, landing_ref, send_ref):
    width = source_ref.shape[1] // KV_HEADS
    m1, m2 = down_maps(source_ref.shape[0], *landing_of(landing_ref[...]))
    spare = jnp.zeros((send_ref.shape[0], width), jnp.float32)
    for g in range(KV_HEADS):
        columns = slice(g * width, (g + 1) * width)
        part = low(source_ref[:, columns])
        send_ref[:, columns] = low(dot(m1, part))
        spare += dot(m2[g], part)
    send_ref[:, KV_HEADS * width :] = low(spare)


def unpack_queries_kernel(recv_ref, home_ref, attended_ref, grad_ref):
    m1, m2 = home_maps(home_ref, recv_ref.shape[0])
    spare = recv_ref[:, KV_HEADS * BOTH_WIDTH :]
    for g in range(KV_HEADS):
        part = recv_ref[:, g * BOTH_WIDTH : (g + 1) * BOTH_WIDTH]
        both = low(dot(m1, part) + dot(m2[g], spare))
        columns = slice(g * GROUP_WIDTH, (g + 1) * GROUP_WIDTH)
        attended_ref[:, columns] = both[:, :GROUP_WIDTH]
        grad_ref[:, columns] = both[:, GROUP_WIDTH:]


def unpack_kv_kernel(recv_ref, home_ref, key_ref, value_ref):
    m1, m2 = home_maps(home_ref, recv_ref.shape[0])
    spare = recv_ref[:, KV_HEADS * PAIR_WIDTH :]
    for g in range(KV_HEADS):
        both = low(
            dot(m1, recv_ref[:, g * PAIR_WIDTH : (g + 1) * PAIR_WIDTH]) + dot(m2[g], spare)
        )
        key_ref[:, g * HEAD_DIM : (g + 1) * HEAD_DIM] = both[:, :HEAD_DIM]
        value_ref[:, g * HEAD_DIM : (g + 1) * HEAD_DIM] = both[:, HEAD_DIM:]


def ends_of(info_ref):
    ends = [info_ref[0]]
    for k in range(1, 6):
        ends.append(ends[-1] + info_ref[k])
    return ends


def stack_heads(x):
    return jnp.concatenate(
        [x[:, h * HEAD_DIM : (h + 1) * HEAD_DIM] for h in range(GROUP)], axis=0
    )


def unstack_heads(x):
    rows = x.shape[0] // GROUP
    return jnp.concatenate([x[h * rows : (h + 1) * rows] for h in range(GROUP)], axis=1)


def attention_kernel(
    info_ref, weight_ref, main_ref, spare_ref, key_ref, value_ref, landing_ref,
    kv_ref, send_ref, bias, spare_sum, value_ones, raised, dscore, score, dprob, r12, r1t, r2t,
):
    step = pl.program_id(0)
    rows, keys = bias.shape
    count = len(score)
    slots = main_ref.shape[0]
    e0, e1, e2, e3, e4, _ = ends_of(info_ref)
    place = info_ref[6] * rows + iota((rows, 1), 0)
    rejected = (place >= e1) & (place < e2)

    @pl.when(step == 0)
    def _():
        first = jnp.where(place >= e2, e2, 0)
        hidden_from = jnp.where(place >= e4, e3, jnp.where(rejected, e0, 0))
        hidden_to = jnp.where(place >= e4, e4, jnp.where(rejected, e1, 0))
        other = iota((rows, keys), 1)
        seen = (other >= first) & (other <= place) & ((other < hidden_from) | (other >= hidden_to))
        bias[...] = jnp.where(seen, 0.0, MASKED)
        spare_sum[...] = jnp.zeros_like(spare_sum)
        landing = landing_ref[...]
        r1, down = down_maps(rows, *landing_of(landing))
        r1t[...], across = across_maps(rows, *landing_rows(landing))
        for g in range(KV_HEADS):
            r12[g, :slots] = r1
            r12[g, slots:] = down[g]
            r2t[g] = across[g]
        for n in range(count):
            value_ones[n][:, HEAD_DIM:] = jnp.ones((keys, HEAD_DIM), jnp.bfloat16)

    weight = jnp.where(place >= e2, weight_ref[1], weight_ref[0])
    factor = jnp.where(rejected | (place >= e4), -weight, weight)
    query, cotangent, key, inverse, attended, delta = ([None] * count for _ in range(6))
    for n in range(count):
        columns = slice(n * HEAD_DIM, (n + 1) * HEAD_DIM)
        both = dot(r1t[...], main_ref[:, n * BOTH_WIDTH : (n + 1) * BOTH_WIDTH]) + dot(
            r2t[step * count + n], spare_ref[...]
        )
        query[n] = stack_heads(low(both[:, :GROUP_WIDTH]))
        cotangent[n] = stack_heads(low(factor * both[:, GROUP_WIDTH:]))
        key[n] = key_ref[:, columns]
        value_ones[n][:, :HEAD_DIM] = value_ref[:, columns]
    for n in range(count):
        score[n][...] = dot(query[n], key[n], ((1,), (1,)))
    for n in range(count):
        for h in range(GROUP):
            part = slice(h * rows, (h + 1) * rows)
            seen = score[n][part, :] + bias[...]
            highest = jnp.max(seen, axis=1, keepdims=True)
            raised[n][part, :] = low(jnp.exp2((seen - highest) * EXPONENT))
    for n in range(count):
        dprob[n][...] = dot(cotangent[n], value_ones[n][:, :HEAD_DIM], ((1,), (1,)))
    for n in range(count):
        summed = dot(raised[n][...], value_ones[n][...])
        inverse[n] = 1.0 / summed[:, HEAD_DIM:]
        attended[n] = low(summed[:, :HEAD_DIM] * inverse[n])
        delta[n] = jnp.sum(
            cotangent[n].astype(jnp.float32) * attended[n].astype(jnp.float32),
            axis=1,
            keepdims=True,
        )
    for n in range(count):
        dscore[n][...] = raised[n][...] * low(dprob[n][...] - delta[n])
    for n in range(count):
        scaled = inverse[n] * SCALING
        query_grad = low(dot(dscore[n][...], key[n]) * scaled)
        query_low = low(query[n].astype(jnp.float32) * scaled)
        cotangent_low = low(cotangent[n].astype(jnp.float32) * inverse[n])
        first = n * PAIR_WIDTH
        kv_ref[:, first : first + HEAD_DIM] = low(dot(query_low.T, dscore[n][...])).T
        kv_ref[:, first + HEAD_DIM : first + PAIR_WIDTH] = low(dot(cotangent_low.T, raised[n][...])).T
        both = jnp.concatenate([unstack_heads(attended[n]), unstack_heads(query_grad)], axis=1)
        start = pl.multiple_of((step * count + n) * BOTH_WIDTH, BOTH_WIDTH)
        placed = dot(r12[step * count + n], both)
        send_ref[:, pl.ds(start, BOTH_WIDTH)] = low(placed[:slots])
        spare_sum[...] += placed[slots:]

    @pl.when(step == KV_HEADS // count - 1)
    def _():
        send_ref[:, KV_HEADS * BOTH_WIDTH :] = low(spare_sum[...])


def shape(dims, kind=jnp.bfloat16):
    return jax.ShapeDtypeStruct(dims, kind)


def cost(flops, moved, exps=0):
    return pl.CostEstimate(flops=int(flops), bytes_accessed=int(moved), transcendentals=int(exps))


def body(queries, keys, values, out_grad, pair_weight, lengths, route_dest, route_slot):
    rows = queries.shape[0]
    ranks = lax.axis_size("dp")
    packs = lax.axis_size("pack")
    seq = rows * packs
    slots = ranks * MAIN
    wide = (KV_HEADS + 1) * BOTH_WIDTH
    narrow = (KV_HEADS + 1) * PAIR_WIDTH
    fence = lax.optimization_barrier

    def exchange(block):
        moved = lax.all_to_all(
            block.reshape(ranks, MAIN, block.shape[1]), "dp", split_axis=0, concat_axis=0, tiled=True
        )
        return moved.reshape(block.shape)

    dest = route_dest.reshape(1, rows)

    kv_send = pl.pallas_call(
        send_kernel,
        out_shape=shape((slots, narrow + HEAD_DIM)),
        compiler_params=compiler_params(),
        cost_estimate=cost(4 * slots * rows * 2 * KV_WIDTH, 6 * slots * 2 * KV_WIDTH),
    )(dest, route_slot.reshape(1, rows), keys, values)

    kv_recv = exchange(kv_send)
    home = pl.pallas_call(
        home_kernel,
        out_shape=shape((rows, HEAD_DIM), jnp.int32),
        compiler_params=compiler_params(),
        cost_estimate=cost(LONG, 6 * slots * rows),
    )(dest)
    query_send = pl.pallas_call(
        pack_queries_kernel,
        out_shape=shape((slots, wide)),
        compiler_params=compiler_params(),
        cost_estimate=cost(LONG, 10 * slots * QUERY_WIDTH),
    )(dest, queries, out_grad)
    info = jnp.concatenate(
        [lengths.reshape(6), lax.axis_index("pack").astype(jnp.int32).reshape(1)]
    )
    kv_recv, query_send, home, info = fence((kv_recv, query_send, home, info))

    kv_own = pl.pallas_call(
        receive_kernel,
        out_shape=shape((rows, 2 * KV_WIDTH)),
        compiler_params=compiler_params(SMALL_VMEM),
        cost_estimate=cost(4 * slots * rows * 2 * KV_WIDTH, 6 * slots * 2 * KV_WIDTH),
    )(kv_recv)
    kv_all = lax.all_gather(kv_own, "pack", axis=0, tiled=True)
    query_send, kv_own = fence((query_send, kv_own))
    query_recv = exchange(query_send)

    smem = pl.BlockSpec(memory_space=pltpu.SMEM)
    at_once = 2
    landing_spec = pl.BlockSpec((slots, HEAD_DIM), lambda g: (0, narrow // HEAD_DIM))
    steps = KV_HEADS // at_once
    work = HEADS * rows * seq * HEAD_DIM

    def several(dims, kind=jnp.bfloat16):
        return [pltpu.VMEM(dims, kind)] * at_once

    kv_part, back_send = pl.pallas_call(
        attention_kernel,
        grid=(steps,),
        in_specs=[
            smem,
            smem,
            pl.BlockSpec((slots, at_once * BOTH_WIDTH), lambda g: (0, g)),
            pl.BlockSpec((slots, BOTH_WIDTH), lambda g: (0, KV_HEADS)),
            pl.BlockSpec((seq, at_once * HEAD_DIM), lambda g: (0, g)),
            pl.BlockSpec((seq, at_once * HEAD_DIM), lambda g: (0, steps + g)),
            landing_spec,
        ],
        out_specs=(
            pl.BlockSpec((seq, at_once * PAIR_WIDTH), lambda g: (0, g)),
            pl.BlockSpec((slots, wide), lambda g: (0, 0)),
        ),
        out_shape=(shape((seq, 2 * KV_WIDTH)), shape((slots, wide))),
        scratch_shapes=[
            pltpu.VMEM((rows, seq), jnp.float32),
            pltpu.VMEM((slots, BOTH_WIDTH), jnp.float32),
            several((seq, PAIR_WIDTH)),
            several((GROUP * rows, seq)),
            several((GROUP * rows, seq)),
            several((GROUP * rows, seq), jnp.float32),
            several((GROUP * rows, seq), jnp.float32),
            pltpu.VMEM((KV_HEADS, 2 * slots, rows), jnp.bfloat16),
            pltpu.VMEM((rows, slots), jnp.bfloat16),
            pltpu.VMEM((KV_HEADS, rows, slots), jnp.bfloat16),
        ],
        compiler_params=compiler_params(dimension_semantics=("arbitrary",)),
        cost_estimate=cost(12 * work, 2 * HEADS * rows * seq, HEADS * rows * seq),
    )(
        info, pair_weight.reshape(2), query_recv, query_recv, kv_all, kv_all, kv_recv,
    )

    back_recv = exchange(back_send)
    kv_grad = lax.psum_scatter(kv_part, "pack", scatter_dimension=0, tiled=True)
    kv_grad_send = pl.pallas_call(
        pack_kernel,
        grid=(1,),
        in_specs=[pl.BlockSpec((rows, 2 * KV_WIDTH), lambda i: (0, 0)), landing_spec],
        out_specs=pl.BlockSpec((slots, narrow), lambda i: (0, 0)),
        out_shape=shape((slots, narrow)),
        compiler_params=compiler_params(),
        cost_estimate=cost(4 * slots * rows * 2 * KV_WIDTH, 10 * slots * KV_WIDTH),
    )(kv_grad, kv_recv)
    back_recv, kv_grad_send = fence((back_recv, kv_grad_send))
    kv_back = exchange(kv_grad_send)
    attended, query_grad = pl.pallas_call(
        unpack_queries_kernel,
        out_shape=(shape((rows, QUERY_WIDTH)), shape((rows, QUERY_WIDTH))),
        compiler_params=compiler_params(SMALL_VMEM),
        cost_estimate=cost(LONG, 10 * slots * QUERY_WIDTH),
    )(back_recv, home)
    key_grad, value_grad = pl.pallas_call(
        unpack_kv_kernel,
        out_shape=(shape((rows, KV_WIDTH)), shape((rows, KV_WIDTH))),
        compiler_params=compiler_params(SMALL_VMEM),
        cost_estimate=cost(4 * slots * rows * 2 * KV_WIDTH, 4 * slots * 2 * KV_WIDTH),
    )(kv_back, home)
    return attended, query_grad, key_grad, value_grad


def solution(mesh):
    rows = P(("dp", "pack"), None)
    flat = P(("dp", "pack"))
    return jax.shard_map(
        body,
        mesh=mesh,
        in_specs=(rows, rows, rows, rows, P("dp", None), P("dp", None, None), flat, flat),
        out_specs=(rows, rows, rows, rows),
        check_vma=False,
    )
```

```python
import functools
import math

import jax
import jax.numpy as jnp
from jax import lax
from jax.experimental import pallas as pl
from jax.experimental.pallas import tpu as pltpu
from jax.sharding import PartitionSpec as P

HEAD_DIM = 128
HEADS = 20
KV_HEADS = 4
GROUP = 5
CAP = 10
MAIN = 8
SPARE = CAP - MAIN

QUERY_WIDTH = HEADS * HEAD_DIM
KV_WIDTH = KV_HEADS * HEAD_DIM
GROUP_WIDTH = GROUP * HEAD_DIM
PAIR_WIDTH = 2 * HEAD_DIM
SCALING = HEAD_DIM ** (-0.5)
EXPONENT = SCALING * math.log2(math.e)
MASKED = -1e30
VMEM_LIMIT = 60 * 1024 * 1024
SMALL_VMEM = 16 * 1024 * 1024
BOTH_WIDTH = 2 * GROUP_WIDTH
LONG = 10**11


def dot(left, right, contract=((1,), (0,))):
    return lax.dot_general(left, right, (contract, ((), ())), preferred_element_type=jnp.float32)


def low(x):
    return x.astype(jnp.bfloat16)


def iota(shape, dim):
    return lax.broadcasted_iota(jnp.int32, shape, dim)


def one_hot(condition):
    return jnp.where(condition, 1.0, 0.0).astype(jnp.bfloat16)


def compiler_params(limit=VMEM_LIMIT, **extra):
    return pltpu.CompilerParams(vmem_limit_bytes=limit, **extra)


def ranks_of(dest_row):
    rows = dest_row.shape[1]
    down = iota((rows, rows), 0)
    across = iota((rows, rows), 1)
    dest_col = jnp.sum(
        jnp.where(down == across, dest_row.astype(jnp.float32), 0.0), axis=1, keepdims=True
    ).astype(jnp.int32)
    return dest_col, dest_col == dest_row, down, across


def places_of(dest, rank):
    rank = rank.astype(jnp.int32)
    first = dest * MAIN + rank
    return jnp.where(rank < MAIN, first, -MAIN), jnp.where(rank < MAIN, -MAIN, first - MAIN)


def send_kernel(dest_ref, slot_ref, keys_ref, values_ref, send_ref, p1_ref, p2_ref):
    rows = keys_ref.shape[0]
    slots = send_ref.shape[0]
    dest_row = dest_ref[...]
    _, same, down, across = ranks_of(dest_row)
    rank_row = jnp.sum(jnp.where(same & (down < across), 1.0, 0.0), axis=0, keepdims=True)
    main_row, spare_row = places_of(dest_row, rank_row)
    slot_down = iota((slots, rows), 0)
    p1 = slot_down == main_row
    p1_low = one_hot(p1)
    p1_ref[...] = p1_low
    place = (slot_ref[...] + 1).astype(jnp.float32)
    place_main = jnp.sum(jnp.where(p1, place, 0.0), axis=1, keepdims=True)
    taken = jnp.zeros((slots, rows), jnp.float32)
    spare = jnp.zeros((slots, PAIR_WIDTH), jnp.float32)
    for g in range(KV_HEADS):
        p2 = slot_down == spare_row + SPARE * g
        p2_low = one_hot(p2)
        p2_ref[g] = p2_low
        taken += jnp.where(p2, place, 0.0)
        source = keys_ref if g < 2 else values_ref
        columns = source[:, (g % 2) * PAIR_WIDTH : (g % 2 + 1) * PAIR_WIDTH]
        send_ref[:, g * PAIR_WIDTH : (g + 1) * PAIR_WIDTH] = low(dot(p1_low, columns))
        spare += dot(p2_low, columns)
    place_spare = jnp.sum(taken, axis=1, keepdims=True)
    send_ref[:, 4 * PAIR_WIDTH : 5 * PAIR_WIDTH] = low(spare)
    lane = iota((slots, HEAD_DIM), 1)
    send_ref[:, 5 * PAIR_WIDTH :] = low(
        jnp.where(lane == 0, place_main, jnp.where(lane == 1, place_spare, 0.0))
    )


def home_kernel(dest_ref, home_ref):
    dest_col, same, down, across = ranks_of(dest_ref[...])
    rank_col = jnp.sum(jnp.where(same & (across < down), 1.0, 0.0), axis=1, keepdims=True)
    main_col, spare_col = places_of(dest_col, rank_col)
    lane = iota(home_ref.shape, 1)
    home_ref[...] = jnp.where(lane == 0, main_col, spare_col)


def home_maps(home_ref, slots):
    rows = home_ref.shape[0]
    slot_across = iota((rows, slots), 1)
    spare_col = home_ref[:, 1:2]
    return one_hot(slot_across == home_ref[:, :1]), [
        one_hot(slot_across == spare_col + SPARE * g) for g in range(KV_HEADS)
    ]


def landing_of(tile):
    slots = tile.shape[0]
    tile = tile.astype(jnp.float32)
    lane = iota((slots, HEAD_DIM), 1)
    main_col = jnp.sum(jnp.where(lane == 0, tile, 0.0), axis=1, keepdims=True)
    spare_col = jnp.sum(jnp.where(lane == 1, tile, 0.0), axis=1, keepdims=True)
    return main_col, spare_col


def landing_rows(main_col, spare_col):
    slots = main_col.shape[0]
    diagonal = iota((slots, slots), 0) == iota((slots, slots), 1)
    return (
        jnp.sum(jnp.where(diagonal, main_col, 0.0), axis=0, keepdims=True).astype(jnp.int32),
        jnp.sum(jnp.where(diagonal, spare_col, 0.0), axis=0, keepdims=True).astype(jnp.int32),
    )


def across_maps(rows, main_row, spare_row):
    slots = main_row.shape[1]
    place_down = iota((rows, slots), 0) + 1
    part_across = (iota((rows, slots), 1) & (MAIN - 1)) >> 1
    return one_hot(place_down == main_row), [
        one_hot((place_down == spare_row) & (part_across == g)) for g in range(KV_HEADS)
    ]


def down_maps(rows, main_col, spare_col):
    slots = main_col.shape[0]
    main_col = main_col.astype(jnp.int32)
    spare_col = spare_col.astype(jnp.int32)
    place_across = iota((slots, rows), 1) + 1
    part_down = (iota((slots, rows), 0) & (MAIN - 1)) >> 1
    return one_hot(place_across == main_col), [
        one_hot((place_across == spare_col) & (part_down == g)) for g in range(KV_HEADS)
    ]


def receive_kernel(recv_ref, kv_ref):
    r1t, r2t = across_maps(kv_ref.shape[0], *landing_rows(*landing_of(recv_ref[:, 5 * PAIR_WIDTH :])))
    spare = recv_ref[:, 4 * PAIR_WIDTH : 5 * PAIR_WIDTH]
    for g in range(KV_HEADS):
        columns = slice(g * PAIR_WIDTH, (g + 1) * PAIR_WIDTH)
        maps = jnp.concatenate([r1t, r2t[g]], axis=1)
        kv_ref[:, columns] = low(dot(maps, jnp.concatenate([recv_ref[:, columns], spare], axis=0)))


def pack_queries_kernel(query_ref, grad_ref, m1_ref, m2_ref, send_ref):
    m1 = m1_ref[...]
    spare = jnp.zeros((send_ref.shape[0], BOTH_WIDTH), jnp.float32)
    for g in range(KV_HEADS):
        columns = slice(g * GROUP_WIDTH, (g + 1) * GROUP_WIDTH)
        part = jnp.concatenate([query_ref[:, columns], grad_ref[:, columns]], axis=1)
        send_ref[:, g * BOTH_WIDTH : (g + 1) * BOTH_WIDTH] = low(dot(m1, part))
        spare += dot(m2_ref[g], part)
    send_ref[:, KV_HEADS * BOTH_WIDTH :] = low(spare)


def pack_kernel(source_ref, landing_ref, send_ref):
    width = source_ref.shape[1] // KV_HEADS
    m1, m2 = down_maps(source_ref.shape[0], *landing_of(landing_ref[...]))
    spare = jnp.zeros((send_ref.shape[0], width), jnp.float32)
    for g in range(KV_HEADS):
        columns = slice(g * width, (g + 1) * width)
        part = low(source_ref[:, columns])
        send_ref[:, columns] = low(dot(m1, part))
        spare += dot(m2[g], part)
    send_ref[:, KV_HEADS * width :] = low(spare)


def unpack_queries_kernel(recv_ref, home_ref, attended_ref, grad_ref):
    m1, m2 = home_maps(home_ref, recv_ref.shape[0])
    spare = recv_ref[:, KV_HEADS * BOTH_WIDTH :]
    for g in range(KV_HEADS):
        part = recv_ref[:, g * BOTH_WIDTH : (g + 1) * BOTH_WIDTH]
        both = low(dot(m1, part) + dot(m2[g], spare))
        columns = slice(g * GROUP_WIDTH, (g + 1) * GROUP_WIDTH)
        attended_ref[:, columns] = both[:, :GROUP_WIDTH]
        grad_ref[:, columns] = both[:, GROUP_WIDTH:]


def unpack_kv_kernel(recv_ref, home_ref, key_ref, value_ref):
    m1, m2 = home_maps(home_ref, recv_ref.shape[0])
    spare = recv_ref[:, KV_HEADS * PAIR_WIDTH :]
    for g in range(KV_HEADS):
        both = low(
            dot(m1, recv_ref[:, g * PAIR_WIDTH : (g + 1) * PAIR_WIDTH]) + dot(m2[g], spare)
        )
        key_ref[:, g * HEAD_DIM : (g + 1) * HEAD_DIM] = both[:, :HEAD_DIM]
        value_ref[:, g * HEAD_DIM : (g + 1) * HEAD_DIM] = both[:, HEAD_DIM:]


def ends_of(info_ref):
    ends = [info_ref[0]]
    for k in range(1, 6):
        ends.append(ends[-1] + info_ref[k])
    return ends


def stack_heads(x):
    return jnp.concatenate(
        [x[:, h * HEAD_DIM : (h + 1) * HEAD_DIM] for h in range(GROUP)], axis=0
    )


def unstack_heads(x):
    rows = x.shape[0] // GROUP
    return jnp.concatenate([x[h * rows : (h + 1) * rows] for h in range(GROUP)], axis=1)


def attention_kernel(
    info_ref, weight_ref, main_ref, spare_ref, key_ref, value_ref, landing_ref,
    kv_ref, send_ref, bias, spare_sum, value_ones, raised, dscore, score, dprob, r12, r1t, r2t,
):
    step = pl.program_id(0)
    rows, keys = bias.shape
    count = len(score)
    slots = main_ref.shape[0]
    e0, e1, e2, e3, e4, _ = ends_of(info_ref)
    place = info_ref[6] * rows + iota((rows, 1), 0)
    rejected = (place >= e1) & (place < e2)

    @pl.when(step == 0)
    def _():
        first = jnp.where(place >= e2, e2, 0)
        hidden_from = jnp.where(place >= e4, e3, jnp.where(rejected, e0, 0))
        hidden_to = jnp.where(place >= e4, e4, jnp.where(rejected, e1, 0))
        other = iota((rows, keys), 1)
        seen = (other >= first) & (other <= place) & ((other < hidden_from) | (other >= hidden_to))
        bias[...] = jnp.where(seen, 0.0, MASKED)
        spare_sum[...] = jnp.zeros_like(spare_sum)
        landing = landing_of(landing_ref[...])
        r1, down = down_maps(rows, *landing)
        r1t[...], across = across_maps(rows, *landing_rows(*landing))
        for g in range(KV_HEADS):
            r12[g, :slots] = r1
            r12[g, slots:] = down[g]
            r2t[g] = across[g]
        for n in range(count):
            value_ones[n][:, HEAD_DIM:] = jnp.ones((keys, HEAD_DIM), jnp.bfloat16)

    weight = jnp.where(place >= e2, weight_ref[1], weight_ref[0])
    factor = jnp.where(rejected | (place >= e4), -weight, weight)
    query, cotangent, key, inverse, attended, delta = ([None] * count for _ in range(6))
    for n in range(count):
        columns = slice(n * HEAD_DIM, (n + 1) * HEAD_DIM)
        both = dot(r1t[...], main_ref[:, n * BOTH_WIDTH : (n + 1) * BOTH_WIDTH]) + dot(
            r2t[step * count + n], spare_ref[...]
        )
        query[n] = stack_heads(low(both[:, :GROUP_WIDTH]))
        cotangent[n] = stack_heads(low(factor * both[:, GROUP_WIDTH:]))
        key[n] = key_ref[:, columns]
        value_ones[n][:, :HEAD_DIM] = value_ref[:, columns]
    for n in range(count):
        score[n][...] = dot(query[n], key[n], ((1,), (1,)))
    for n in range(count):
        for h in range(GROUP):
            part = slice(h * rows, (h + 1) * rows)
            seen = score[n][part, :] + bias[...]
            highest = jnp.max(seen, axis=1, keepdims=True)
            raised[n][part, :] = low(jnp.exp2((seen - highest) * EXPONENT))
    for n in range(count):
        dprob[n][...] = dot(cotangent[n], value_ones[n][:, :HEAD_DIM], ((1,), (1,)))
    for n in range(count):
        summed = dot(raised[n][...], value_ones[n][...])
        inverse[n] = 1.0 / summed[:, HEAD_DIM:]
        attended[n] = low(summed[:, :HEAD_DIM] * inverse[n])
        delta[n] = jnp.sum(
            cotangent[n].astype(jnp.float32) * attended[n].astype(jnp.float32),
            axis=1,
            keepdims=True,
        )
    for n in range(count):
        dscore[n][...] = raised[n][...] * low(dprob[n][...] - delta[n])
    for n in range(count):
        scaled = inverse[n] * SCALING
        query_grad = low(dot(dscore[n][...], key[n]) * scaled)
        query_low = low(query[n].astype(jnp.float32) * scaled)
        cotangent_low = low(cotangent[n].astype(jnp.float32) * inverse[n])
        first = n * PAIR_WIDTH
        kv_ref[:, first : first + HEAD_DIM] = low(dot(query_low.T, dscore[n][...])).T
        kv_ref[:, first + HEAD_DIM : first + PAIR_WIDTH] = low(dot(cotangent_low.T, raised[n][...])).T
        both = jnp.concatenate([unstack_heads(attended[n]), unstack_heads(query_grad)], axis=1)
        start = pl.multiple_of((step * count + n) * BOTH_WIDTH, BOTH_WIDTH)
        placed = dot(r12[step * count + n], both)
        send_ref[:, pl.ds(start, BOTH_WIDTH)] = low(placed[:slots])
        spare_sum[...] += placed[slots:]

    @pl.when(step == KV_HEADS // count - 1)
    def _():
        send_ref[:, KV_HEADS * BOTH_WIDTH :] = low(spare_sum[...])


def shape(dims, kind=jnp.bfloat16):
    return jax.ShapeDtypeStruct(dims, kind)


def cost(flops, moved, exps=0):
    return pl.CostEstimate(flops=int(flops), bytes_accessed=int(moved), transcendentals=int(exps))


def body(queries, keys, values, out_grad, pair_weight, lengths, route_dest, route_slot):
    rows = queries.shape[0]
    ranks = lax.axis_size("dp")
    packs = lax.axis_size("pack")
    seq = rows * packs
    slots = ranks * MAIN
    wide = (KV_HEADS + 1) * BOTH_WIDTH
    narrow = (KV_HEADS + 1) * PAIR_WIDTH
    fence = lax.optimization_barrier

    def exchange(block):
        moved = lax.all_to_all(
            block.reshape(ranks, MAIN, block.shape[1]), "dp", split_axis=0, concat_axis=0, tiled=True
        )
        return moved.reshape(block.shape)

    down = (shape((slots, rows)), shape((KV_HEADS, slots, rows)))
    dest = route_dest.reshape(1, rows)

    kv_send, p1, p2 = pl.pallas_call(
        send_kernel,
        out_shape=(shape((slots, narrow + HEAD_DIM)), *down),
        compiler_params=compiler_params(),
        cost_estimate=cost(4 * slots * rows * 2 * KV_WIDTH, 6 * slots * 2 * KV_WIDTH),
    )(dest, route_slot.reshape(1, rows), keys, values)

    kv_recv = exchange(kv_send)
    home = pl.pallas_call(
        home_kernel,
        out_shape=shape((rows, HEAD_DIM), jnp.int32),
        compiler_params=compiler_params(),
        cost_estimate=cost(LONG, 6 * slots * rows),
    )(dest)
    query_send = pl.pallas_call(
        pack_queries_kernel,
        out_shape=shape((slots, wide)),
        compiler_params=compiler_params(),
        cost_estimate=cost(LONG, 10 * slots * QUERY_WIDTH),
    )(queries, out_grad, p1, p2)
    info = jnp.concatenate(
        [lengths.reshape(6), lax.axis_index("pack").astype(jnp.int32).reshape(1)]
    )
    kv_recv, query_send, home, info = fence((kv_recv, query_send, home, info))

    kv_own = pl.pallas_call(
        receive_kernel,
        out_shape=shape((rows, 2 * KV_WIDTH)),
        compiler_params=compiler_params(SMALL_VMEM),
        cost_estimate=cost(4 * slots * rows * 2 * KV_WIDTH, 6 * slots * 2 * KV_WIDTH),
    )(kv_recv)
    kv_all = lax.all_gather(kv_own, "pack", axis=0, tiled=True)
    query_send, kv_own = fence((query_send, kv_own))
    query_recv = exchange(query_send)

    smem = pl.BlockSpec(memory_space=pltpu.SMEM)
    at_once = 2
    landing_spec = pl.BlockSpec((slots, HEAD_DIM), lambda g: (0, narrow // HEAD_DIM))
    steps = KV_HEADS // at_once
    work = HEADS * rows * seq * HEAD_DIM

    def several(dims, kind=jnp.bfloat16):
        return [pltpu.VMEM(dims, kind)] * at_once

    kv_part, back_send = pl.pallas_call(
        attention_kernel,
        grid=(steps,),
        in_specs=[
            smem,
            smem,
            pl.BlockSpec((slots, at_once * BOTH_WIDTH), lambda g: (0, g)),
            pl.BlockSpec((slots, BOTH_WIDTH), lambda g: (0, KV_HEADS)),
            pl.BlockSpec((seq, at_once * HEAD_DIM), lambda g: (0, g)),
            pl.BlockSpec((seq, at_once * HEAD_DIM), lambda g: (0, steps + g)),
            landing_spec,
        ],
        out_specs=(
            pl.BlockSpec((seq, at_once * PAIR_WIDTH), lambda g: (0, g)),
            pl.BlockSpec((slots, wide), lambda g: (0, 0)),
        ),
        out_shape=(shape((seq, 2 * KV_WIDTH)), shape((slots, wide))),
        scratch_shapes=[
            pltpu.VMEM((rows, seq), jnp.float32),
            pltpu.VMEM((slots, BOTH_WIDTH), jnp.float32),
            several((seq, PAIR_WIDTH)),
            several((GROUP * rows, seq)),
            several((GROUP * rows, seq)),
            several((GROUP * rows, seq), jnp.float32),
            several((GROUP * rows, seq), jnp.float32),
            pltpu.VMEM((KV_HEADS, 2 * slots, rows), jnp.bfloat16),
            pltpu.VMEM((rows, slots), jnp.bfloat16),
            pltpu.VMEM((KV_HEADS, rows, slots), jnp.bfloat16),
        ],
        compiler_params=compiler_params(dimension_semantics=("arbitrary",)),
        cost_estimate=cost(12 * work, 2 * HEADS * rows * seq, HEADS * rows * seq),
    )(
        info, pair_weight.reshape(2), query_recv, query_recv, kv_all, kv_all, kv_recv,
    )

    back_recv = exchange(back_send)
    kv_grad = lax.psum_scatter(kv_part, "pack", scatter_dimension=0, tiled=True)
    kv_grad_send = pl.pallas_call(
        pack_kernel,
        grid=(1,),
        in_specs=[pl.BlockSpec((rows, 2 * KV_WIDTH), lambda i: (0, 0)), landing_spec],
        out_specs=pl.BlockSpec((slots, narrow), lambda i: (0, 0)),
        out_shape=shape((slots, narrow)),
        compiler_params=compiler_params(),
        cost_estimate=cost(4 * slots * rows * 2 * KV_WIDTH, 10 * slots * KV_WIDTH),
    )(kv_grad, kv_recv)
    back_recv, kv_grad_send = fence((back_recv, kv_grad_send))
    kv_back = exchange(kv_grad_send)
    attended, query_grad = pl.pallas_call(
        unpack_queries_kernel,
        out_shape=(shape((rows, QUERY_WIDTH)), shape((rows, QUERY_WIDTH))),
        compiler_params=compiler_params(SMALL_VMEM),
        cost_estimate=cost(LONG, 10 * slots * QUERY_WIDTH),
    )(back_recv, home)
    key_grad, value_grad = pl.pallas_call(
        unpack_kv_kernel,
        out_shape=(shape((rows, KV_WIDTH)), shape((rows, KV_WIDTH))),
        compiler_params=compiler_params(SMALL_VMEM),
        cost_estimate=cost(4 * slots * rows * 2 * KV_WIDTH, 4 * slots * 2 * KV_WIDTH),
    )(kv_back, home)
    return attended, query_grad, key_grad, value_grad


def solution(mesh):
    rows = P(("dp", "pack"), None)
    flat = P(("dp", "pack"))
    return jax.shard_map(
        body,
        mesh=mesh,
        in_specs=(rows, rows, rows, rows, P("dp", None), P("dp", None, None), flat, flat),
        out_specs=(rows, rows, rows, rows),
        check_vma=False,
    )
```
